32 devices in a mesh: row: 8 (over z, x), col: 4 (over y, core).
Axes of the slice: x: 2, y: 2, z: 4, core: 2. Of those that a mesh axis runs over, the one named last changes fastest.
Arguments:
- start_vectors: float32 [64, 16384], P(None, ('row', 'col')), may hold values from -6 to 6
- scaling: float32 [16384], P(('row', 'col')), may hold values from 0.25 to 1.75
- block_values: bfloat16 [8, 4, 128, 128, 128], P('row', 'col'), may hold values from -0.046875 to 0.046875
- block_places: int32 [8, 4, 2, 128], P('row', 'col'), may hold values from 0 to 31, as said below
- block_counts: int32 [8, 4], P('row', 'col'), may hold values from 16 to 128, as said below
Outputs:
- filtered: float32 [64, 16384], P(None, ('row', 'col'))
The draws below stay inside these ranges and needn't reach their ends.
Inputs may be any that keep to these rules, and one draw needn't show every extreme that they name: `block_places`: within each device's 128 slots the positions (block row, block column) are distinct; entry 0 is the local block row (below 16), entry 1 the local block column (below 32). Slots at or after the device's count are not part of the matrix. `block_counts`: some device has all 128 slots live.
All inputs are finite; a program needn't handle non-finite values.
Results may differ from the reference program's by a relative error of at most 0.0038.
Values may be sent and summed in bfloat16 or wider, within the bound.
No kernel may reach another device: no remote copies, remote signals or barrier semaphores. Data moves between devices by JAX's collectives and lax.ppermute only.
A program may use at most 128 MiB of HBM per device.

```python
import jax
import jax.numpy as jnp
from jax import lax

BLOCK = 128
VEC = 64
CAP = 128
STEPS = 3
GRID_R = 8
GRID_C = 4
TB = 16
TBC = 32
ORDER = 16384


def draw_block_places(key, part):
    device_keys = jax.random.split(jax.random.fold_in(key, 11), GRID_R * GRID_C)

    def one_device(device_key):
        slot_order = jax.random.permutation(device_key, TB * TBC)[:CAP].astype(jnp.int32)
        return jnp.stack([slot_order // TBC, slot_order % TBC])
    return jax.vmap(one_device)(device_keys).reshape(GRID_R, GRID_C, 2, CAP).astype(jnp.int32)


def draw_block_counts(key, part):
    base_key = jax.random.fold_in(key, 23)
    key_base, key_heavy, key_forced = jax.random.split(base_key, 3)
    devices_n = GRID_R * GRID_C
    base_counts = jax.random.randint(key_base, (devices_n,), CAP // 8, CAP // 2 + 1)
    heavy_mask = jax.random.randint(key_heavy, (devices_n,), 0, 8) == 0
    forced = jax.random.randint(key_forced, (), 0, devices_n)
    is_full = heavy_mask | (jnp.arange(devices_n) == forced)
    counts = jnp.where(is_full, CAP, base_counts)
    return counts.reshape(GRID_R, GRID_C).astype(jnp.int32)


def block_levels(stream_key, dims, pieces, least, largest):
    gain = 1.0
    for axis_at, shards_of in pieces:
        heights = jax.random.uniform(jax.random.fold_in(jax.random.fold_in(stream_key, 6), axis_at), (shards_of,), jnp.float32, least / len(pieces), largest / len(pieces))
        gain = gain * jnp.repeat(jnp.exp(heights), dims[axis_at] // shards_of).reshape((-1,) + (1,) * (len(dims) - 1 - axis_at))
    return gain


def scatter_about(rng, extent, spread, limit, cuts=(), held_as=jnp.bfloat16):
    gain = block_levels(rng, extent, cuts, -0.22, 0.18) if cuts else 1.0
    drawn = jax.random.normal(rng, extent, jnp.float32) * spread * gain
    return jnp.minimum(jnp.maximum(drawn, -limit), limit).astype(held_as)


def setup_inputs(seed: int = 0) -> dict:
    arg_keys = jax.random.split(jax.random.key(seed), 6)
    start_vectors = scatter_about(arg_keys[0], (VEC, ORDER), 1.0, 6.0, ((1, 32),), jnp.float32)
    scaling = jnp.clip(1.0 + 0.15 * jax.random.normal(arg_keys[1], (ORDER,), jnp.float32), 0.25, 1.75)
    block_values = scatter_about(arg_keys[2], (GRID_R, GRID_C, CAP, BLOCK, BLOCK), (CAP * BLOCK) ** -0.5, 0.046875, ((0, 8), (1, 4)))
    block_places = draw_block_places(jax.random.fold_in(arg_keys[5], 71), 0)
    block_counts = draw_block_counts(jax.random.fold_in(arg_keys[5], 71), 0)
    return {"start_vectors": start_vectors, "scaling": scaling, "block_values": block_values, "block_places": block_places, "block_counts": block_counts}


center_shift = 0.5
half_width = 3.0


def apply_matrix(scaled, block_values, block_places, block_counts):
    block_total = ORDER // BLOCK
    blocked = scaled.astype(jnp.float32).reshape(VEC, block_total, BLOCK)

    def one_device(totals, device_flat):
        grid_row = device_flat // GRID_C
        grid_col = device_flat % GRID_C
        slabs = block_values[grid_row, grid_col].astype(jnp.float32)
        places = block_places[grid_row, grid_col]
        glob_rows = (grid_row * TB + places[0]).astype(jnp.int32)
        glob_cols = (grid_col * TBC + places[1]).astype(jnp.int32)
        live_mask = (jnp.arange(CAP) < block_counts[grid_row, grid_col]).astype(jnp.float32)
        col_vecs = blocked[:, glob_cols, :]
        row_vecs = blocked[:, glob_rows, :]
        direct = jnp.einsum('gik,ngk->ngi', slabs, col_vecs) * live_mask[None, :, None]
        transposed = jnp.einsum('gik,ngi->ngk', slabs, row_vecs) * live_mask[None, :, None]
        totals = totals.at[:, glob_rows, :].add(direct)
        totals = totals.at[:, glob_cols, :].add(transposed)
        return totals, None

    zeros = jnp.zeros((VEC, block_total, BLOCK), jnp.float32)
    totals, _ = lax.scan(one_device, zeros, jnp.arange(GRID_R * GRID_C).astype(jnp.int32))
    return totals.reshape(VEC, ORDER)


def reference(start_vectors, scaling, block_values, block_places, block_counts):
    current = start_vectors
    previous = start_vectors
    for iterate in range(STEPS):
        scaled = (scaling[None, :] * current).astype(jnp.bfloat16)
        applied = apply_matrix(scaled, block_values, block_places, block_counts)
        mapped = scaling[None, :] * applied - center_shift * current
        if iterate == 0:
            updated = mapped / half_width
        else:
            updated = (2.0 / half_width) * mapped - previous
        previous = current
        current = updated
    return current
```

```python
import functools

import jax
import jax.numpy as jnp
from jax import lax
from jax.experimental import pallas as pl
from jax.experimental.pallas import tpu as pltpu
from jax.sharding import PartitionSpec as P

STEPS = 3

center_shift = 0.5
half_width = 3.0

UNROLL = 8
VMEM_LIMIT = 24 * 1024 * 1024


def to_blocks(x, block_len):
    return [x[:, b * block_len:(b + 1) * block_len] for b in range(x.shape[1] // block_len)]


def scale_kernel(x_ref, s_ref, out_ref):
    block_len = out_ref.shape[2]
    scaled = (x_ref[...] * s_ref[...]).astype(jnp.bfloat16)
    for b, part in enumerate(to_blocks(scaled, block_len)):
        out_ref[b] = part


def scale_blocks(x, s, block_len):
    n, length = x.shape
    return pl.pallas_call(
        scale_kernel,
        out_shape=jax.ShapeDtypeStruct((length // block_len, n, block_len), jnp.bfloat16),
    )(x, s)


def product_kernel(
    plan_in, plan_out, transpose, cap, meta_ref, slabs_hbm, *refs
):
    n_in = len(plan_in)
    n_out = len(plan_out)
    ins = refs[:n_in]
    outs = refs[n_in:n_in + n_out]
    slabs, vecs, acc, slab_sem, vec_sem = refs[n_in + n_out:]
    per_chunk = ins[0].shape[0]
    out_blocks = acc.shape[0] - 1
    count = meta_ref[2 * cap]
    groups = (count + (UNROLL - 1)) // UNROLL

    def slab_copy(g):
        span = pl.ds(g * UNROLL, UNROLL)
        return pltpu.make_async_copy(slabs_hbm.at[span], slabs.at[span], slab_sem.at[g])

    def vec_copy(k):
        place = plan_in[k](meta_ref)
        return pltpu.make_async_copy(
            ins[k], vecs.at[pl.ds(place * per_chunk, per_chunk)], vec_sem.at[k]
        )

    for k in range(n_in):
        vec_copy(k).start()

    def start_slab(g, carry):
        slab_copy(g).start()
        return carry

    lax.fori_loop(0, groups, start_slab, 0)
    acc[...] = jnp.zeros_like(acc)
    for k in range(n_in):
        vec_copy(k).wait()

    def body(g, carry):
        slab_copy(g).wait()
        products = []
        for u in range(UNROLL):
            s = g * UNROLL + u
            row = meta_ref[s]
            col = meta_ref[cap + s]
            if transpose:
                source, target = row, col
                dims = (((1,), (0,)), ((), ()))
            else:
                source, target = col, row
                dims = (((1,), (1,)), ((), ()))
            target = jnp.where(s < count, target, out_blocks)
            product = lax.dot_general(
                vecs[source], slabs[s], dims, preferred_element_type=jnp.float32
            )
            products.append((target, product))
        for target, product in products:
            acc[target] += product
        return carry

    lax.fori_loop(0, groups, body, 0)
    for k in range(n_out):
        place = plan_out[k](meta_ref)
        outs[k][...] = acc[pl.ds(place * per_chunk, per_chunk)].astype(outs[k].dtype)


def products(meta, slabs, ins, plan_in, plan_out, transpose):
    cap, block_len, _ = slabs.shape
    per_chunk, vec_count, _ = ins[0].shape
    n_in, n_out = len(ins), len(plan_out)
    out_shape = [
        jax.ShapeDtypeStruct(ins[0].shape, jnp.float32 if k == 0 else jnp.bfloat16)
        for k in range(n_out)
    ]
    return pl.pallas_call(
        functools.partial(product_kernel, plan_in, plan_out, transpose, cap),
        in_specs=[pl.BlockSpec(memory_space=pltpu.SMEM)]
        + [pl.BlockSpec(memory_space=pl.ANY)] * (1 + n_in),
        out_specs=[pl.BlockSpec(memory_space=pltpu.VMEM)] * n_out,
        out_shape=out_shape,
        scratch_shapes=[
            pltpu.VMEM(slabs.shape, jnp.bfloat16),
            pltpu.VMEM((n_in * per_chunk, vec_count, block_len), jnp.bfloat16),
            pltpu.VMEM((n_out * per_chunk + 1, vec_count, block_len), jnp.float32),
            pltpu.SemaphoreType.DMA((cap // UNROLL,)),
            pltpu.SemaphoreType.DMA((n_in,)),
        ],
        compiler_params=pltpu.CompilerParams(vmem_limit_bytes=VMEM_LIMIT),
        cost_estimate=pl.CostEstimate(
            flops=2 * cap * vec_count * block_len * block_len,
            bytes_accessed=2 * cap * block_len * block_len,
            transcendentals=0,
        ),
        name="transposed" if transpose else "direct",
    )(meta, slabs, *ins)


def sum_kernel(*refs):
    ins, out = refs[:-1], refs[-1]
    total = ins[0][...].astype(jnp.float32)
    for ref in ins[1:]:
        total = total + ref[...].astype(jnp.float32)
    out[...] = total.astype(out.dtype)


def sum_parts(parts):
    return pl.pallas_call(
        sum_kernel,
        out_shape=jax.ShapeDtypeStruct(parts[0].shape, jnp.bfloat16),
        name="row_sum",
    )(*parts)


def update_kernel(first, n_parts, last, *refs):
    s_ref, now_ref = refs[:2]
    refs = refs[2:]
    if not first:
        before_ref, refs = refs[0], refs[1:]
    parts, outs = refs[:n_parts], refs[n_parts:]
    per_chunk, _, block_len = parts[0].shape
    for b in range(per_chunk):
        span = slice(b * block_len, (b + 1) * block_len)
        applied = parts[0][b].astype(jnp.float32)
        for ref in parts[1:]:
            applied = applied + ref[b].astype(jnp.float32)
        scale = s_ref[:, span]
        mapped = scale * applied - center_shift * now_ref[:, span]
        if first:
            updated = mapped / half_width
        else:
            updated = 2.0 / half_width * mapped - before_ref[:, span]
        outs[0][:, span] = updated
        if not last:
            outs[1][b] = (scale * updated).astype(jnp.bfloat16)


def update(s, now, before, parts, first, last):
    out_shape = [jax.ShapeDtypeStruct(now.shape, jnp.float32)]
    if not last:
        out_shape.append(jax.ShapeDtypeStruct(parts[0].shape, jnp.bfloat16))
    states = [s, now] if first else [s, now, before]
    return pl.pallas_call(
        functools.partial(update_kernel, first, len(parts), last),
        out_shape=out_shape,
        name="update",
    )(*states, *parts)


def per_device(start_vectors, scaling, block_values, block_places, block_counts):
    rows = lax.axis_size("row")
    cols = lax.axis_size("col")
    fast = 1
    while fast * fast * 4 <= rows:
        fast *= 2
    while rows % fast:
        fast //= 2
    slow = rows // fast
    cap = block_values.shape[2]
    block_len = block_values.shape[-1]
    slabs = block_values.reshape(cap, block_len, block_len)
    row_index = lax.axis_index("row").astype(jnp.int32)
    col_index = lax.axis_index("col").astype(jnp.int32)
    meta = jnp.concatenate([
        block_places.reshape(2 * cap),
        block_counts.reshape(1),
        jnp.stack([row_index // fast, row_index % fast, col_index]),
    ])

    total = rows * cols
    to_home = [(p, (p % rows) * cols + p // rows) for p in range(total)]
    from_home = [(b, a) for a, b in to_home]
    axes = ("row", "col")

    offsets = [(a, b) for a in range(slow) for b in range(fast)]

    def shift_row(x, a, b):
        pairs = [
            (i * fast + j, ((i + a) % slow) * fast + (j + b) % fast)
            for i in range(slow) for j in range(fast)
        ]
        return lax.ppermute(x, "row", pairs)

    def shift_col(x, a):
        return lax.ppermute(x, "col", [(i, (i + a) % cols) for i in range(cols)])

    def row_place(sign, a, b):
        def place(meta_ref):
            i = lax.rem(meta_ref[2 * cap + 1] + (slow + sign * a), slow)
            j = lax.rem(meta_ref[2 * cap + 2] + (fast + sign * b), fast)
            return i * fast + j
        return place

    def col_place(sign, a):
        def place(meta_ref):
            return lax.rem(meta_ref[2 * cap + 3] + (cols + sign * a), cols)
        return place

    column_in = [row_place(-1, a, b) for a, b in offsets]
    column_out = [row_place(1, a, b) for a, b in offsets]
    row_in = [col_place(-1, a) for a in range(cols)]
    row_out = [col_place(1, a) for a in range(cols)]

    scale_row = scaling.reshape(1, -1)
    guest = scale_blocks(start_vectors, scale_row, block_len)
    own = lax.ppermute(guest, axes, to_home)
    now = lax.ppermute(start_vectors, axes, to_home)
    scale = lax.ppermute(scale_row, axes, to_home)
    before = None
    for iterate in range(STEPS):
        first, last = iterate == 0, iterate == STEPS - 1
        if not first:
            guest = lax.ppermute(own, axes, from_home)
        along = [own] + [shift_row(own, a, 0) for a in range(1, slow)]
        column_chunks = []
        for a in range(slow):
            column_chunks.append(along[a])
            for b in range(1, fast):
                column_chunks.append(shift_row(along[a], 0, b))
        row_chunks = [guest] + [shift_col(guest, a) for a in range(1, cols)]
        transposed = products(meta, slabs, row_chunks, row_in, column_out, True)
        parts = [transposed[0]] + [
            shift_row(x, a, b) for x, (a, b) in zip(transposed[1:], offsets[1:])
        ]
        direct = products(meta, slabs, column_chunks, column_in, row_out, False)
        direct_sum = sum_parts(
            [direct[0]] + [shift_col(direct[a], a) for a in range(1, cols)]
        )
        parts.append(lax.ppermute(direct_sum, axes, to_home))
        results = update(scale, now, before, parts, first, last)
        before = now
        now = results[0]
        if not last:
            own = results[1]
    return lax.ppermute(now, axes, from_home)


def solution(mesh):
    in_specs = (
        P(None, ("row", "col")),
        P(("row", "col")),
        P("row", "col", None, None, None),
        P("row", "col", None, None),
        P("row", "col"),
    )
    out_specs = P(None, ("row", "col"))
    return jax.shard_map(
        per_device, mesh=mesh, in_specs=in_specs, out_specs=out_specs, check_vma=False
    )
```

```python
import functools

import jax
import jax.numpy as jnp
from jax import lax
from jax.experimental import pallas as pl
from jax.experimental.pallas import tpu as pltpu
from jax.sharding import PartitionSpec as P

STEPS = 3

center_shift = 0.5
half_width = 3.0

UNROLL = 16
VMEM_LIMIT = 24 * 1024 * 1024


def to_blocks(x, block_len):
    return [x[:, b * block_len:(b + 1) * block_len] for b in range(x.shape[1] // block_len)]


def scale_kernel(x_ref, s_ref, out_ref):
    block_len = out_ref.shape[2]
    scaled = (x_ref[...] * s_ref[...]).astype(jnp.bfloat16)
    for b, part in enumerate(to_blocks(scaled, block_len)):
        out_ref[b] = part


def scale_blocks(x, s, block_len):
    n, length = x.shape
    return pl.pallas_call(
        scale_kernel,
        out_shape=jax.ShapeDtypeStruct((length // block_len, n, block_len), jnp.bfloat16),
    )(x, s)


def product_kernel(transpose, cap, meta_ref, slabs_hbm, vecs_ref, out, slabs, vecs, acc, slab_sem, vec_sem):
    out_blocks = acc.shape[0] - 1
    count = meta_ref[2 * cap]
    groups = (count + (UNROLL - 1)) // UNROLL

    def slab_copy(g):
        span = pl.ds(g * UNROLL, UNROLL)
        return pltpu.make_async_copy(slabs_hbm.at[span], slabs.at[span], slab_sem.at[g])

    vec_copy = pltpu.make_async_copy(vecs_ref, vecs, vec_sem)
    vec_copy.start()

    def start_slab(g, carry):
        slab_copy(g).start()
        return carry

    lax.fori_loop(0, groups, start_slab, 0)
    acc[...] = jnp.zeros_like(acc)
    vec_copy.wait()

    def body(g, carry):
        slab_copy(g).wait()
        products = []
        for u in range(UNROLL):
            s = g * UNROLL + u
            row = meta_ref[s]
            col = meta_ref[cap + s]
            if transpose:
                source, target = row, col
                dims = (((1,), (0,)), ((), ()))
            else:
                source, target = col, row
                dims = (((1,), (1,)), ((), ()))
            target = jnp.where(s < count, target, out_blocks)
            product = lax.dot_general(
                vecs[source], slabs[s], dims, preferred_element_type=jnp.float32
            )
            products.append((target, product))
        for target, product in products:
            acc[target] += product
        return carry

    lax.fori_loop(0, groups, body, 0)
    out[...] = acc[:out_blocks].astype(out.dtype)


def products(meta, slabs, vecs, out_blocks, transpose):
    cap, block_len, _ = slabs.shape
    _, vec_count, _ = vecs.shape
    return pl.pallas_call(
        functools.partial(product_kernel, transpose, cap),
        in_specs=[
            pl.BlockSpec(memory_space=pltpu.SMEM),
            pl.BlockSpec(memory_space=pltpu.HBM),
            pl.BlockSpec(memory_space=pl.ANY),
        ],
        out_specs=pl.BlockSpec(memory_space=pltpu.VMEM),
        out_shape=jax.ShapeDtypeStruct((out_blocks, vec_count, block_len), jnp.bfloat16),
        scratch_shapes=[
            pltpu.VMEM(slabs.shape, jnp.bfloat16),
            pltpu.VMEM(vecs.shape, jnp.bfloat16),
            pltpu.VMEM((out_blocks + 1, vec_count, block_len), jnp.float32),
            pltpu.SemaphoreType.DMA((cap // UNROLL,)),
            pltpu.SemaphoreType.DMA,
        ],
        compiler_params=pltpu.CompilerParams(vmem_limit_bytes=VMEM_LIMIT),
        cost_estimate=pl.CostEstimate(
            flops=2 * cap * vec_count * block_len * block_len,
            bytes_accessed=2 * cap * block_len * block_len,
            transcendentals=0,
        ),
        name="transposed" if transpose else "direct",
    )(meta, slabs, vecs)


def sum_kernel(parts_ref, out):
    total = parts_ref[0].astype(jnp.float32)
    for k in range(1, parts_ref.shape[0]):
        total = total + parts_ref[k].astype(jnp.float32)
    out[...] = total.astype(out.dtype)


def sum_parts(parts):
    return pl.pallas_call(
        sum_kernel,
        out_shape=jax.ShapeDtypeStruct(parts.shape[1:], jnp.bfloat16),
        name="row_sum",
    )(parts)


def update_kernel(first, last, *refs):
    s_ref, now_ref = refs[:2]
    refs = refs[2:]
    if not first:
        before_ref, refs = refs[0], refs[1:]
    col_parts, row_part = refs[:2]
    outs = refs[2:]
    per_chunk, _, block_len = row_part.shape
    for b in range(per_chunk):
        span = slice(b * block_len, (b + 1) * block_len)
        applied = row_part[b].astype(jnp.float32)
        for k in range(col_parts.shape[0]):
            applied = applied + col_parts[k, b].astype(jnp.float32)
        scale = s_ref[:, span]
        mapped = scale * applied - center_shift * now_ref[:, span]
        if first:
            updated = mapped / half_width
        else:
            updated = 2.0 / half_width * mapped - before_ref[:, span]
        outs[0][:, span] = updated
        if not last:
            outs[1][b] = (scale * updated).astype(jnp.bfloat16)


def update(s, now, before, col_parts, row_part, first, last):
    out_shape = [jax.ShapeDtypeStruct(now.shape, jnp.float32)]
    if not last:
        out_shape.append(jax.ShapeDtypeStruct(row_part.shape, jnp.bfloat16))
    states = [s, now] if first else [s, now, before]
    return pl.pallas_call(
        functools.partial(update_kernel, first, last),
        out_shape=out_shape,
        name="update",
    )(*states, col_parts, row_part)


def per_device(start_vectors, scaling, block_values, block_places, block_counts):
    rows = lax.axis_size("row")
    cols = lax.axis_size("col")
    cap = block_values.shape[2]
    block_len = block_values.shape[-1]
    per_chunk = start_vectors.shape[1] // block_len
    vec_count = start_vectors.shape[0]
    slabs = block_values.reshape(cap, block_len, block_len)
    meta = jnp.concatenate([block_places.reshape(2 * cap), block_counts.reshape(1)])

    total = rows * cols
    to_home = [(p, (p % rows) * cols + p // rows) for p in range(total)]
    from_home = [(b, a) for a, b in to_home]
    axes = ("row", "col")

    scale_row = scaling.reshape(1, -1)
    guest = scale_blocks(start_vectors, scale_row, block_len)
    own = lax.ppermute(guest, axes, to_home)
    now = lax.ppermute(start_vectors, axes, to_home)
    scale = lax.ppermute(scale_row, axes, to_home)
    before = None
    for iterate in range(STEPS):
        first, last = iterate == 0, iterate == STEPS - 1
        if not first:
            guest = lax.ppermute(own, axes, from_home)
        row_tile = lax.all_gather(guest, "col", axis=0, tiled=True)
        column_tile = lax.all_gather(own, "row", axis=0, tiled=True)
        transposed = products(meta, slabs, row_tile, rows * per_chunk, True)
        direct = products(meta, slabs, column_tile, cols * per_chunk, False)
        col_parts = lax.all_to_all(
            transposed.reshape(rows, per_chunk, vec_count, block_len), "row", 0, 0
        )
        row_parts = lax.all_to_all(
            direct.reshape(cols, per_chunk, vec_count, block_len), "col", 0, 0
        )
        row_part = lax.ppermute(sum_parts(row_parts), axes, to_home)
        results = update(scale, now, before, col_parts, row_part, first, last)
        before = now
        now = results[0]
        if not last:
            own = results[1]
    return lax.ppermute(now, axes, from_home)


def solution(mesh):
    in_specs = (
        P(None, ("row", "col")),
        P(("row", "col")),
        P("row", "col", None, None, None),
        P("row", "col", None, None),
        P("row", "col"),
    )
    out_specs = P(None, ("row", "col"))
    return jax.shard_map(
        per_device, mesh=mesh, in_specs=in_specs, out_specs=out_specs, check_vma=False
    )
```

```python
import functools

import jax
import jax.numpy as jnp
from jax import lax
from jax.experimental import pallas as pl
from jax.experimental.pallas import tpu as pltpu
from jax.sharding import PartitionSpec as P

STEPS = 3

center_shift = 0.5
half_width = 3.0

UNROLL = 32
VMEM_LIMIT = 24 * 1024 * 1024
AXES = ("row", "col")
PAD = 8


class Layout:
    def __init__(self, rows, cols):
        self.rows, self.cols = rows, cols
        self.chips = cols // 2
        self.fast = 2
        self.slow = rows // 2
        self.group = self.slow // self.chips
        assert self.group * self.chips * self.fast == rows

    def device(self, slow, fast, chip, core):
        return (slow * self.fast + fast) * self.cols + chip * 2 + core

    def home(self, chunk):
        chip, k = chunk // self.rows, chunk % self.rows
        e, f, t = k % self.chips, (k // self.chips) % self.fast, k // (self.chips * self.fast)
        return (chip ^ e) * self.group + t, f, chip

    def moves_home(self, swap):
        pairs = []
        for chunk in range(self.rows * self.chips):
            row, chip = chunk // self.chips, chunk % self.chips
            for core in range(2):
                source = row * self.cols + chip * 2 + core
                pairs.append((source, self.device(*self.home(chunk), core ^ swap)))
        return pairs

    def moves_slow(self, d):
        return [
            (self.device(s, f, c, q), self.device(s ^ d, f, c, q))
            for s in range(self.slow) for f in range(self.fast)
            for c in range(self.chips) for q in range(2)
        ]

    def moves_fast(self):
        return [
            (self.device(s, f, c, q), self.device(s, f ^ 1, c, q))
            for s in range(self.slow) for f in range(self.fast)
            for c in range(self.chips) for q in range(2)
        ]

    def moves_root(self, d):
        return [
            (self.device(s, f, s // self.group, q), self.device(s, f, (s // self.group) ^ d, q))
            for s in range(self.slow) for f in range(self.fast) for q in range(2)
        ]

    def moves_core(self):
        return [(i, i ^ 1) for i in range(self.rows * self.cols)]


def turned(pairs):
    return [(b, a) for a, b in pairs]


def pack_kernel(core_ref, x_ref, s_ref, same_ref, other_ref):
    core = core_ref[0]
    blocks, _, block_len = same_ref.shape
    half = x_ref.shape[0] // 2
    for b in range(blocks):
        span = slice(b * block_len, (b + 1) * block_len)
        scale = jnp.broadcast_to(s_ref[:, span], (PAD, block_len))
        for out, which in ((same_ref, core), (other_ref, 1 - core)):
            start = pl.multiple_of(which * half, half)
            out[b, :half] = x_ref[pl.ds(start, half), span]
            out[b, half:] = scale


def unpack_kernel(core_ref, same_ref, other_ref, out_ref):
    core = core_ref[0]
    blocks, half, block_len = same_ref.shape
    for b in range(blocks):
        span = slice(b * block_len, (b + 1) * block_len)
        for part, which in ((same_ref, core), (other_ref, 1 - core)):
            start = pl.multiple_of(which * half, half)
            out_ref[pl.ds(start, half), span] = part[b]


def product_kernel(transpose, cap, n_in, n_out, after, meta_ref, *refs):
    slab_refs, refs = refs[:2], refs[2:]
    ins, refs = refs[:n_in], refs[n_in + after:]
    outs, refs = refs[:n_out], refs[n_out:]
    slabs, vecs, acc, slab_sem, vec_sem = refs
    per_in = ins[0].shape[0]
    base = 0 if transpose else 4 * cap
    first_groups = (meta_ref[8 * cap] + (UNROLL - 1)) // UNROLL
    other_groups = (meta_ref[8 * cap + 1] + (UNROLL - 1)) // UNROLL

    def slab_copy(which, g):
        span = pl.ds(g * UNROLL, UNROLL)
        to = pl.ds(which * cap + g * UNROLL, UNROLL)
        sem = slab_sem.at[which * (cap // UNROLL) + g]
        return pltpu.make_async_copy(slab_refs[which].at[span], slabs.at[to], sem)

    if transpose:
        chosen = meta_ref[8 * cap + 2]

        def vec_copies(k):
            return pltpu.make_async_copy(ins[k], vecs, vec_sem.at[0])

        for k in range(n_in):
            @pl.when(chosen == k)
            def _():
                vec_copies(k).start()
    else:
        def vec_copies(k):
            return pltpu.make_async_copy(
                ins[k], vecs.at[pl.ds(k * per_in, per_in)], vec_sem.at[k]
            )

        for k in range(n_in):
            vec_copies(k).start()

    def start_slab(which, g, carry):
        slab_copy(which, g).start()
        return carry

    lax.fori_loop(0, first_groups, functools.partial(start_slab, 0), 0)
    lax.fori_loop(0, other_groups, functools.partial(start_slab, 1), 0)
    acc[...] = jnp.zeros_like(acc)
    if transpose:
        vec_copies(0).wait()
    else:
        for k in range(n_in):
            vec_copies(k).wait()

    def body(which, g, carry):
        slab_copy(which, g).wait()
        start = which * cap + g * UNROLL
        products = []
        for u in range(UNROLL):
            source = meta_ref[base + start + u]
            dims = (((1,), (0 if transpose else 1,)), ((), ()))
            products.append(lax.dot_general(
                vecs[source], slabs[start + u], dims, preferred_element_type=jnp.float32
            ))
        for u, product in enumerate(products):
            acc[meta_ref[base + 2 * cap + start + u]] += product
        return carry

    lax.fori_loop(0, first_groups, functools.partial(body, 0), 0)
    lax.fori_loop(0, other_groups, functools.partial(body, 1), 0)
    size = outs[0].shape[0]
    for k, out in enumerate(outs):
        out[...] = acc[k * size:(k + 1) * size].astype(out.dtype)


def products(meta, slabs, ins, out_dtypes, out_blocks, transpose, after=()):
    cap, block_len, _ = slabs[0].shape
    per_in, vec_count, _ = ins[0].shape
    in_blocks = per_in if transpose else per_in * len(ins)
    total_out = out_blocks * len(out_dtypes)
    return pl.pallas_call(
        functools.partial(
            product_kernel, transpose, cap, len(ins), len(out_dtypes), len(after)
        ),
        in_specs=[pl.BlockSpec(memory_space=pltpu.SMEM)]
        + [pl.BlockSpec(memory_space=pl.ANY)] * (2 + len(ins) + len(after)),
        out_specs=[pl.BlockSpec(memory_space=pltpu.VMEM)] * len(out_dtypes),
        out_shape=[
            jax.ShapeDtypeStruct((out_blocks, vec_count, block_len), dtype)
            for dtype in out_dtypes
        ],
        scratch_shapes=[
            pltpu.VMEM((2 * cap, block_len, block_len), jnp.bfloat16),
            pltpu.VMEM((in_blocks, vec_count, block_len), jnp.bfloat16),
            pltpu.VMEM((total_out + 1, vec_count, block_len), jnp.float32),
            pltpu.SemaphoreType.DMA((2 * cap // UNROLL,)),
            pltpu.SemaphoreType.DMA((len(ins),)),
        ],
        compiler_params=pltpu.CompilerParams(vmem_limit_bytes=VMEM_LIMIT),
        cost_estimate=pl.CostEstimate(
            flops=4 * cap * vec_count * block_len * block_len,
            bytes_accessed=4 * cap * block_len * block_len,
            transcendentals=0,
        ),
        name="transposed" if transpose else "direct",
    )(meta, *slabs, *ins, *after)


def per_device(start_vectors, scaling, block_values, block_places, block_counts):
    at = Layout(lax.axis_size("row"), lax.axis_size("col"))
    cap = block_values.shape[2]
    block_len = block_values.shape[-1]
    half = start_vectors.shape[0] // 2
    part = start_vectors.shape[1] // block_len
    per_chunk = 2 * part
    row_index = lax.axis_index("row").astype(jnp.int32)
    col_index = lax.axis_index("col").astype(jnp.int32)
    slow, fast = row_index // at.fast, row_index % at.fast
    chip, core = col_index // 2, col_index % 2
    root = slow // at.group
    is_root = chip == root
    core_arg = core.reshape(1)
    smem = pl.BlockSpec(memory_space=pltpu.SMEM)
    vmem = pl.BlockSpec(memory_space=pltpu.VMEM)

    def send(x, pairs):
        return lax.ppermute(x, AXES, pairs)

    slabs = block_values.reshape(cap, block_len, block_len)
    slots = jnp.concatenate([block_places.reshape(2 * cap), block_counts.reshape(1)])
    other_slabs = send(slabs, at.moves_core())
    other_slots = send(slots, at.moves_core())

    packed = pl.pallas_call(
        pack_kernel,
        in_specs=[smem, vmem, vmem],
        out_specs=[vmem, vmem],
        out_shape=[jax.ShapeDtypeStruct((part, half + PAD, block_len), jnp.float32)] * 2,
        name="pack",
    )(core_arg, start_vectors, scaling.reshape(1, -1))
    there = [at.moves_home(swap) for swap in range(2)]
    arrived = jnp.concatenate([send(x, pairs) for x, pairs in zip(packed, there)], axis=0)
    now = arrived[:, :half]
    scale = arrived[:, half:half + 1]
    own = (scale * now).astype(jnp.bfloat16)

    n_col = at.rows * per_chunk
    n_row = at.chips * per_chunk
    lists = []
    for which, held in enumerate((slots, other_slots)):
        row_block, col_block = held[:cap], held[cap:2 * cap]
        live = jnp.arange(cap, dtype=jnp.int32) < held[2 * cap]

        def inside(block):
            return ((block // part) ^ core) * part + block % part

        e = row_block // per_chunk
        row_at = e * per_chunk + inside(row_block % per_chunk)
        block = (core ^ which) * (n_col // 2) + col_block
        k = block // per_chunk
        e, f, t = k % at.chips, (k // at.chips) % at.fast, k // (at.chips * at.fast)
        d = slow ^ ((chip ^ e) * at.group + t)
        col_at = ((fast ^ f) * at.slow + d) * per_chunk + inside(block % per_chunk)
        lists.append((
            row_at, jnp.where(live, col_at, n_col), col_at, jnp.where(live, row_at, n_row)
        ))
    meta = jnp.concatenate(
        [jnp.concatenate([mine, theirs]) for mine, theirs in zip(*lists)]
        + [slots[2 * cap:], other_slots[2 * cap:], (chip ^ root).reshape(1)]
    )
    both = (slabs, other_slabs)

    before = None
    for iterate in range(STEPS):
        along = [own] + [send(own, at.moves_slow(d)) for d in range(1, at.slow)]
        row_own = jnp.concatenate([along[e * at.group] for e in range(at.chips)], axis=0)
        row_tiles = [row_own] + [send(row_own, at.moves_root(d)) for d in range(1, at.chips)]
        near = jnp.concatenate(along, axis=0)
        far = send(near, at.moves_fast())
        near_sum, far_sum = products(
            meta, both, row_tiles, (jnp.float32, jnp.bfloat16), n_col // 2, True
        )
        from_fast = send(far_sum, at.moves_fast())
        (row_sum,) = products(
            meta, both, (near, far), (jnp.bfloat16,), n_row, False, after=(far_sum,)
        )
        row_parts = [jnp.where(is_root, row_sum, jnp.zeros_like(row_sum))] + [
            send(row_sum, turned(at.moves_root(d))) for d in range(1, at.chips)
        ]
        sums = []
        for d in range(at.slow):
            span = slice(d * per_chunk, (d + 1) * per_chunk)
            total = near_sum[span] + from_fast[span].astype(jnp.float32)
            if d % at.group == 0:
                e = d // at.group
                for x in row_parts:
                    total = total + x[e * per_chunk:(e + 1) * per_chunk].astype(jnp.float32)
            sums.append(total)
        applied = sums[0]
        for d in range(1, at.slow):
            applied = applied + send(
                sums[d].astype(jnp.bfloat16), at.moves_slow(d)
            ).astype(jnp.float32)
        mapped = scale * applied - center_shift * now
        if iterate == 0:
            updated = mapped / half_width
        else:
            updated = 2.0 / half_width * mapped - before
        before = now
        now = updated
        own = (scale * now).astype(jnp.bfloat16)
    back = [
        send(x, turned(pairs)) for x, pairs in zip((now[:part], now[part:]), there)
    ]
    return pl.pallas_call(
        unpack_kernel,
        in_specs=[smem, vmem, vmem],
        out_specs=vmem,
        out_shape=jax.ShapeDtypeStruct(start_vectors.shape, jnp.float32),
        name="unpack",
    )(core_arg, *back)


def solution(mesh):
    in_specs = (
        P(None, ("row", "col")),
        P(("row", "col")),
        P("row", "col", None, None, None),
        P("row", "col", None, None),
        P("row", "col"),
    )
    out_specs = P(None, ("row", "col"))
    return jax.shard_map(
        per_device, mesh=mesh, in_specs=in_specs, out_specs=out_specs, check_vma=False
    )
```

```python
import functools

import jax
import jax.numpy as jnp
from jax import lax
from jax.experimental import pallas as pl
from jax.experimental.pallas import tpu as pltpu
from jax.sharding import PartitionSpec as P

STEPS = 3

center_shift = 0.5
half_width = 3.0

UNROLL = 32
VMEM_LIMIT = 24 * 1024 * 1024
AXES = ("row", "col")
PAD = 8


class Layout:
    def __init__(self, rows, cols):
        self.rows, self.cols = rows, cols
        self.chips = cols // 2
        self.fast = 2
        self.slow = rows // 2
        self.group = self.slow // self.chips
        assert self.group * self.chips * self.fast == rows

    def device(self, slow, fast, chip, core):
        return (slow * self.fast + fast) * self.cols + chip * 2 + core

    def home(self, chunk):
        chip, k = chunk // self.rows, chunk % self.rows
        e, f, t = k % self.chips, (k // self.chips) % self.fast, k // (self.chips * self.fast)
        return (chip ^ e) * self.group + t, f, chip

    def moves_home(self, swap):
        pairs = []
        for chunk in range(self.rows * self.chips):
            row, chip = chunk // self.chips, chunk % self.chips
            for core in range(2):
                source = row * self.cols + chip * 2 + core
                pairs.append((source, self.device(*self.home(chunk), core ^ swap)))
        return pairs

    def moves_slow(self, d):
        return [
            (self.device(s, f, c, q), self.device(s ^ d, f, c, q))
            for s in range(self.slow) for f in range(self.fast)
            for c in range(self.chips) for q in range(2)
        ]

    def moves_fast(self):
        return [
            (self.device(s, f, c, q), self.device(s, f ^ 1, c, q))
            for s in range(self.slow) for f in range(self.fast)
            for c in range(self.chips) for q in range(2)
        ]

    def moves_root(self, d):
        return [
            (self.device(s, f, s // self.group, q), self.device(s, f, (s // self.group) ^ d, q))
            for s in range(self.slow) for f in range(self.fast) for q in range(2)
        ]

    def moves_core(self):
        return [(i, i ^ 1) for i in range(self.rows * self.cols)]


def turned(pairs):
    return [(b, a) for a, b in pairs]


def pack_kernel(core_ref, x_ref, s_ref, same_ref, other_ref):
    core = core_ref[0]
    blocks, _, block_len = same_ref.shape
    half = x_ref.shape[0] // 2
    for b in range(blocks):
        span = slice(b * block_len, (b + 1) * block_len)
        scale = jnp.broadcast_to(s_ref[:, span], (PAD, block_len))
        for out, which in ((same_ref, core), (other_ref, 1 - core)):
            start = pl.multiple_of(which * half, half)
            out[b, :half] = x_ref[pl.ds(start, half), span]
            out[b, half:] = scale


def unpack_kernel(core_ref, same_ref, other_ref, out_ref):
    core = core_ref[0]
    blocks, half, block_len = same_ref.shape
    for b in range(blocks):
        span = slice(b * block_len, (b + 1) * block_len)
        for part, which in ((same_ref, core), (other_ref, 1 - core)):
            start = pl.multiple_of(which * half, half)
            out_ref[pl.ds(start, half), span] = part[b]


def product_kernel(transpose, cap, meta_ref, mine_ref, other_ref, vecs_ref, *refs):
    outs, acc = refs[:-1], refs[-1]
    base = 0 if transpose else 4 * cap
    acc[...] = jnp.zeros_like(acc)

    def body(which, slab_ref, g, carry):
        start = base + which * cap + g * UNROLL
        products = []
        for u in range(UNROLL):
            source = meta_ref[start + u]
            dims = (((1,), (0 if transpose else 1,)), ((), ()))
            products.append(lax.dot_general(
                vecs_ref[source], slab_ref[g * UNROLL + u], dims,
                preferred_element_type=jnp.float32,
            ))
        for u, product in enumerate(products):
            acc[meta_ref[start + 2 * cap + u]] += product
        return carry

    for which, slab_ref in enumerate((mine_ref, other_ref)):
        groups = (meta_ref[8 * cap + which] + (UNROLL - 1)) // UNROLL
        lax.fori_loop(0, groups, functools.partial(body, which, slab_ref), 0)
    size = outs[0].shape[0]
    for k, out in enumerate(outs):
        out[...] = acc[k * size:(k + 1) * size].astype(out.dtype)


def products(meta, slabs, vecs, out_dtypes, out_blocks, transpose):
    cap, block_len, _ = slabs[0].shape
    vec_count = vecs.shape[1]
    total_out = out_blocks * len(out_dtypes)
    vmem = pl.BlockSpec(memory_space=pltpu.VMEM)
    return pl.pallas_call(
        functools.partial(product_kernel, transpose, cap),
        in_specs=[pl.BlockSpec(memory_space=pltpu.SMEM), vmem, vmem, vmem],
        out_specs=[vmem] * len(out_dtypes),
        out_shape=[
            jax.ShapeDtypeStruct((out_blocks, vec_count, block_len), dtype)
            for dtype in out_dtypes
        ],
        scratch_shapes=[pltpu.VMEM((total_out + 1, vec_count, block_len), jnp.float32)],
        compiler_params=pltpu.CompilerParams(vmem_limit_bytes=VMEM_LIMIT),
        cost_estimate=pl.CostEstimate(
            flops=4 * cap * vec_count * block_len * block_len,
            bytes_accessed=4 * cap * block_len * block_len,
            transcendentals=0,
        ),
        name="transposed" if transpose else "direct",
    )(meta, *slabs, vecs)


def per_device(start_vectors, scaling, block_values, block_places, block_counts):
    at = Layout(lax.axis_size("row"), lax.axis_size("col"))
    cap = block_values.shape[2]
    block_len = block_values.shape[-1]
    half = start_vectors.shape[0] // 2
    part = start_vectors.shape[1] // block_len
    per_chunk = 2 * part
    row_index = lax.axis_index("row").astype(jnp.int32)
    col_index = lax.axis_index("col").astype(jnp.int32)
    slow, fast = row_index // at.fast, row_index % at.fast
    chip, core = col_index // 2, col_index % 2
    root = slow // at.group
    is_root = chip == root
    core_arg = core.reshape(1)
    smem = pl.BlockSpec(memory_space=pltpu.SMEM)
    vmem = pl.BlockSpec(memory_space=pltpu.VMEM)

    def send(x, pairs):
        return lax.ppermute(x, AXES, pairs)

    slabs = block_values.reshape(cap, block_len, block_len)
    slots = jnp.concatenate([block_places.reshape(2 * cap), block_counts.reshape(1)])
    other_slabs = send(slabs, at.moves_core())
    other_slots = send(slots, at.moves_core())

    packed = pl.pallas_call(
        pack_kernel,
        in_specs=[smem, vmem, vmem],
        out_specs=[vmem, vmem],
        out_shape=[jax.ShapeDtypeStruct((part, half + PAD, block_len), jnp.float32)] * 2,
        name="pack",
    )(core_arg, start_vectors, scaling.reshape(1, -1))
    there = [at.moves_home(swap) for swap in range(2)]
    arrived = jnp.concatenate([send(x, pairs) for x, pairs in zip(packed, there)], axis=0)
    now = arrived[:, :half]
    scale = arrived[:, half:half + 1]
    own = (scale * now).astype(jnp.bfloat16)

    n_col = at.rows * per_chunk
    n_row = at.chips * per_chunk
    lists = []
    for which, held in enumerate((slots, other_slots)):
        row_block, col_block = held[:cap], held[cap:2 * cap]
        live = jnp.arange(cap, dtype=jnp.int32) < held[2 * cap]

        def inside(block):
            return ((block // part) ^ core) * part + block % part

        e = row_block // per_chunk
        row_at = e * per_chunk + inside(row_block % per_chunk)
        block = (core ^ which) * (n_col // 2) + col_block
        k = block // per_chunk
        e, f, t = k % at.chips, (k // at.chips) % at.fast, k // (at.chips * at.fast)
        d = slow ^ ((chip ^ e) * at.group + t)
        col_at = ((fast ^ f) * at.slow + d) * per_chunk + inside(block % per_chunk)
        lists.append((
            row_at, jnp.where(live, col_at, n_col), col_at, jnp.where(live, row_at, n_row)
        ))
    meta = jnp.concatenate(
        [jnp.concatenate([mine, theirs]) for mine, theirs in zip(*lists)]
        + [slots[2 * cap:], other_slots[2 * cap:]]
    )
    live = jnp.arange(cap, dtype=jnp.int32) < block_counts.reshape(())
    both = (jnp.where(live[:, None, None], slabs, jnp.zeros_like(slabs)), other_slabs)

    before = None
    for iterate in range(STEPS):
        along = [own] + [send(own, at.moves_slow(d)) for d in range(1, at.slow)]
        row_tile = row_own = jnp.concatenate(
            [along[e * at.group] for e in range(at.chips)], axis=0
        )
        for d in range(1, at.chips):
            got = send(row_own, at.moves_root(d))
            row_tile = jnp.where((chip ^ root) == d, got, row_tile)
        along, row_tile = lax.optimization_barrier((along, row_tile))
        near = jnp.concatenate(along, axis=0)
        far = send(near, at.moves_fast())
        near_sum, far_sum = products(
            meta, both, row_tile, (jnp.float32, jnp.bfloat16), n_col // 2, True
        )
        from_fast = send(far_sum, at.moves_fast())
        near, far, near_sum = lax.optimization_barrier((near, far, near_sum))
        (row_sum,) = products(
            meta, both, jnp.concatenate([near, far], axis=0), (jnp.bfloat16,), n_row, False
        )
        from_fast, row_sum = lax.optimization_barrier((from_fast, row_sum))
        row_parts = [jnp.where(is_root, row_sum, jnp.zeros_like(row_sum))] + [
            send(row_sum, turned(at.moves_root(d))) for d in range(1, at.chips)
        ]

        def sum_of(d, near_sum, from_fast):
            span = slice(d * per_chunk, (d + 1) * per_chunk)
            return near_sum[span] + from_fast[span].astype(jnp.float32)

        def to_slow(d, total):
            return send(total.astype(jnp.bfloat16), at.moves_slow(d)).astype(jnp.float32)

        arrived = [
            to_slow(d, sum_of(d, near_sum, from_fast))
            for d in range(at.slow) if d % at.group
        ]
        near_sum, from_fast, row_parts = lax.optimization_barrier(
            (near_sum, from_fast, row_parts)
        )
        sums = []
        for e in range(at.chips):
            total = sum_of(e * at.group, near_sum, from_fast)
            for x in row_parts:
                total = total + x[e * per_chunk:(e + 1) * per_chunk].astype(jnp.float32)
            sums.append(total)
        applied = sums[0]
        for e in range(1, at.chips):
            arrived.append(to_slow(e * at.group, sums[e]))
        for x in arrived:
            applied = applied + x
        mapped = scale * applied - center_shift * now
        if iterate == 0:
            updated = mapped / half_width
        else:
            updated = 2.0 / half_width * mapped - before
        before = now
        now = updated
        own = (scale * now).astype(jnp.bfloat16)
    back = [
        send(x, turned(pairs)) for x, pairs in zip((now[:part], now[part:]), there)
    ]
    return pl.pallas_call(
        unpack_kernel,
        in_specs=[smem, vmem, vmem],
        out_specs=vmem,
        out_shape=jax.ShapeDtypeStruct(start_vectors.shape, jnp.float32),
        name="unpack",
    )(core_arg, *back)


def solution(mesh):
    in_specs = (
        P(None, ("row", "col")),
        P(("row", "col")),
        P("row", "col", None, None, None),
        P("row", "col", None, None),
        P("row", "col"),
    )
    out_specs = P(None, ("row", "col"))
    return jax.shard_map(
        per_device, mesh=mesh, in_specs=in_specs, out_specs=out_specs, check_vma=False
    )
```

```python
import functools

import jax
import jax.numpy as jnp
from jax import lax
from jax.experimental import pallas as pl
from jax.experimental.pallas import tpu as pltpu
from jax.sharding import PartitionSpec as P

STEPS = 3

center_shift = 0.5
half_width = 3.0

UNROLL = 32
VMEM_LIMIT = 24 * 1024 * 1024
AXES = ("row", "col")
PAD = 8


class Layout:
    def __init__(self, rows, cols):
        self.rows, self.cols = rows, cols
        self.chips = cols // 2
        self.fast = 2
        self.slow = rows // 2
        self.group = self.slow // self.chips
        assert self.group * self.chips * self.fast == rows

    def device(self, slow, fast, chip, core):
        return (slow * self.fast + fast) * self.cols + chip * 2 + core

    def home(self, chunk):
        chip, k = chunk // self.rows, chunk % self.rows
        e, f, t = k % self.chips, (k // self.chips) % self.fast, k // (self.chips * self.fast)
        return (chip ^ e) * self.group + t, f, chip

    def moves_home(self, swap):
        pairs = []
        for chunk in range(self.rows * self.chips):
            row, chip = chunk // self.chips, chunk % self.chips
            for core in range(2):
                source = row * self.cols + chip * 2 + core
                pairs.append((source, self.device(*self.home(chunk), core ^ swap)))
        return pairs

    def moves_slow(self, d):
        return [
            (self.device(s, f, c, q), self.device(s ^ d, f, c, q))
            for s in range(self.slow) for f in range(self.fast)
            for c in range(self.chips) for q in range(2)
        ]

    def moves_fast(self):
        return [
            (self.device(s, f, c, q), self.device(s, f ^ 1, c, q))
            for s in range(self.slow) for f in range(self.fast)
            for c in range(self.chips) for q in range(2)
        ]

    def moves_row(self, e, d):
        return [
            (
                self.device(s ^ (e * self.group), f, s // self.group, q),
                self.device(s, f, (s // self.group) ^ d, q),
            )
            for s in range(self.slow) for f in range(self.fast) for q in range(2)
        ]

    def moves_core(self):
        return [(i, i ^ 1) for i in range(self.rows * self.cols)]


def turned(pairs):
    return [(b, a) for a, b in pairs]


def pack_kernel(core_ref, x_ref, s_ref, same_ref, other_ref):
    core = core_ref[0]
    blocks, _, block_len = same_ref.shape
    half = x_ref.shape[0] // 2
    for b in range(blocks):
        span = slice(b * block_len, (b + 1) * block_len)
        scale = jnp.broadcast_to(s_ref[:, span], (PAD, block_len))
        for out, which in ((same_ref, core), (other_ref, 1 - core)):
            start = pl.multiple_of(which * half, half)
            out[b, :half] = x_ref[pl.ds(start, half), span]
            out[b, half:] = scale


def unpack_kernel(core_ref, same_ref, other_ref, out_ref):
    core = core_ref[0]
    blocks, half, block_len = same_ref.shape
    for b in range(blocks):
        span = slice(b * block_len, (b + 1) * block_len)
        for part, which in ((same_ref, core), (other_ref, 1 - core)):
            start = pl.multiple_of(which * half, half)
            out_ref[pl.ds(start, half), span] = part[b]


def product_kernel(transpose, cap, n_in, n_out, after, meta_ref, *refs):
    slab_refs, refs = refs[:2], refs[2:]
    ins, refs = refs[:n_in], refs[n_in + after:]
    outs, refs = refs[:n_out], refs[n_out:]
    slabs, vecs, acc, slab_sem, vec_sem = refs
    per_in = ins[0].shape[0]
    base = 0 if transpose else 4 * cap
    first_groups = (meta_ref[8 * cap] + (UNROLL - 1)) // UNROLL
    other_groups = (meta_ref[8 * cap + 1] + (UNROLL - 1)) // UNROLL

    def slab_copy(which, g):
        span = pl.ds(g * UNROLL, UNROLL)
        to = pl.ds(which * cap + g * UNROLL, UNROLL)
        sem = slab_sem.at[which * (cap // UNROLL) + g]
        return pltpu.make_async_copy(slab_refs[which].at[span], slabs.at[to], sem)

    def vec_copy(k):
        return pltpu.make_async_copy(
            ins[k], vecs.at[pl.ds(k * per_in, per_in)], vec_sem.at[k]
        )

    for k in range(n_in):
        vec_copy(k).start()

    def start_slab(which, g, carry):
        slab_copy(which, g).start()
        return carry

    lax.fori_loop(0, first_groups, functools.partial(start_slab, 0), 0)
    lax.fori_loop(0, other_groups, functools.partial(start_slab, 1), 0)
    acc[...] = jnp.zeros_like(acc)
    for k in range(n_in):
        vec_copy(k).wait()

    def body(which, g, carry):
        slab_copy(which, g).wait()
        start = which * cap + g * UNROLL
        products = []
        for u in range(UNROLL):
            source = meta_ref[base + start + u]
            dims = (((1,), (0 if transpose else 1,)), ((), ()))
            products.append(lax.dot_general(
                vecs[source], slabs[start + u], dims, preferred_element_type=jnp.float32
            ))
        for u, product in enumerate(products):
            acc[meta_ref[base + 2 * cap + start + u]] += product
        return carry

    lax.fori_loop(0, first_groups, functools.partial(body, 0), 0)
    lax.fori_loop(0, other_groups, functools.partial(body, 1), 0)
    size = outs[0].shape[0]
    for k, out in enumerate(outs):
        out[...] = acc[k * size:(k + 1) * size].astype(out.dtype)


def products(meta, slabs, ins, out_dtypes, out_blocks, transpose, after=()):
    cap, block_len, _ = slabs[0].shape
    per_in, vec_count, _ = ins[0].shape
    in_blocks = per_in * len(ins)
    total_out = out_blocks * len(out_dtypes)
    return pl.pallas_call(
        functools.partial(
            product_kernel, transpose, cap, len(ins), len(out_dtypes), len(after)
        ),
        in_specs=[pl.BlockSpec(memory_space=pltpu.SMEM)]
        + [pl.BlockSpec(memory_space=pl.ANY)] * (2 + len(ins) + len(after)),
        out_specs=[pl.BlockSpec(memory_space=pltpu.VMEM)] * len(out_dtypes),
        out_shape=[
            jax.ShapeDtypeStruct((out_blocks, vec_count, block_len), dtype)
            for dtype in out_dtypes
        ],
        scratch_shapes=[
            pltpu.VMEM((2 * cap, block_len, block_len), jnp.bfloat16),
            pltpu.VMEM((in_blocks, vec_count, block_len), jnp.bfloat16),
            pltpu.VMEM((total_out + 1, vec_count, block_len), jnp.float32),
            pltpu.SemaphoreType.DMA((2 * cap // UNROLL,)),
            pltpu.SemaphoreType.DMA((len(ins),)),
        ],
        compiler_params=pltpu.CompilerParams(vmem_limit_bytes=VMEM_LIMIT),
        cost_estimate=pl.CostEstimate(
            flops=4 * cap * vec_count * block_len * block_len,
            bytes_accessed=4 * cap * block_len * block_len,
            transcendentals=0,
        ),
        name="transposed" if transpose else "direct",
    )(meta, *slabs, *ins, *after)


def per_device(start_vectors, scaling, block_values, block_places, block_counts):
    at = Layout(lax.axis_size("row"), lax.axis_size("col"))
    cap = block_values.shape[2]
    block_len = block_values.shape[-1]
    half = start_vectors.shape[0] // 2
    part = start_vectors.shape[1] // block_len
    per_chunk = 2 * part
    row_index = lax.axis_index("row").astype(jnp.int32)
    col_index = lax.axis_index("col").astype(jnp.int32)
    slow, fast = row_index // at.fast, row_index % at.fast
    chip, core = col_index // 2, col_index % 2
    root = slow // at.group
    is_root = chip == root
    core_arg = core.reshape(1)
    smem = pl.BlockSpec(memory_space=pltpu.SMEM)
    vmem = pl.BlockSpec(memory_space=pltpu.VMEM)

    def send(x, pairs):
        return lax.ppermute(x, AXES, pairs)

    slabs = block_values.reshape(cap, block_len, block_len)
    slots = jnp.concatenate([block_places.reshape(2 * cap), block_counts.reshape(1)])
    other_slabs = send(slabs, at.moves_core())
    own_slabs = send(slabs, [(i, i) for i in range(at.rows * at.cols)])
    other_slots = send(slots, at.moves_core())

    packed = pl.pallas_call(
        pack_kernel,
        in_specs=[smem, vmem, vmem],
        out_specs=[vmem, vmem],
        out_shape=[jax.ShapeDtypeStruct((part, half + PAD, block_len), jnp.float32)] * 2,
        name="pack",
    )(core_arg, start_vectors, scaling.reshape(1, -1))
    there = [at.moves_home(swap) for swap in range(2)]
    arrived = jnp.concatenate([send(x, pairs) for x, pairs in zip(packed, there)], axis=0)
    arrived, own_slabs, other_slabs = lax.optimization_barrier(
        (arrived, own_slabs, other_slabs)
    )
    now = arrived[:, :half]
    scale = arrived[:, half:half + 1]
    own = (scale * now).astype(jnp.bfloat16)

    n_col = at.rows * per_chunk
    n_row = at.chips * per_chunk
    lists = []
    for which, held in enumerate((slots, other_slots)):
        row_block, col_block = held[:cap], held[cap:2 * cap]
        live = jnp.arange(cap, dtype=jnp.int32) < held[2 * cap]

        def inside(block):
            return ((block // part) ^ core) * part + block % part

        e = row_block // per_chunk
        row_at = e * per_chunk + inside(row_block % per_chunk)
        block = (core ^ which) * (n_col // 2) + col_block
        k = block // per_chunk
        e, f, t = k % at.chips, (k // at.chips) % at.fast, k // (at.chips * at.fast)
        d = slow ^ ((chip ^ e) * at.group + t)
        col_at = ((fast ^ f) * at.slow + d) * per_chunk + inside(block % per_chunk)
        lists.append((
            row_at, jnp.where(live, col_at, n_col), col_at, jnp.where(live, row_at, n_row)
        ))
    meta = jnp.concatenate(
        [jnp.concatenate([mine, theirs]) for mine, theirs in zip(*lists)]
        + [slots[2 * cap:], other_slots[2 * cap:]]
    )
    both = (own_slabs, other_slabs)

    before = None
    for iterate in range(STEPS):
        row_tile = []
        got = [
            [send(own, at.moves_row(e, d)) for d in range(1, at.chips)]
            for e in range(at.chips)
        ]
        along = [own] + [send(own, at.moves_slow(d)) for d in range(1, at.slow)]
        near = jnp.concatenate(along, axis=0)
        far = send(near, at.moves_fast())
        for e in range(at.chips):
            chunk = along[e * at.group]
            for d in range(1, at.chips):
                chunk = jnp.where((chip ^ root) == d, got[e][d - 1], chunk)
            row_tile.append(chunk)
        near_sum, far_sum = products(
            meta, both, [jnp.concatenate(row_tile, axis=0)],
            (jnp.float32, jnp.bfloat16), n_col // 2, True,
        )
        from_fast = send(far_sum, at.moves_fast())
        row_sums = products(
            meta, both, (near, far), (jnp.bfloat16,) * at.chips, per_chunk, False,
            after=(far_sum,),
        )
        parts = [
            send(row_sums[e], turned(at.moves_row(e, d)))
            for e in range(at.chips) for d in range(1, at.chips)
        ]
        sums = []
        for d in range(at.slow):
            span = slice(d * per_chunk, (d + 1) * per_chunk)
            total = near_sum[span] + from_fast[span].astype(jnp.float32)
            if d % at.group == 0:
                mine = row_sums[d // at.group].astype(jnp.float32)
                total = total + jnp.where(is_root, mine, jnp.zeros_like(mine))
            sums.append(total)
        applied = sums[0]
        for d in range(1, at.slow):
            parts.append(send(sums[d].astype(jnp.bfloat16), at.moves_slow(d)))
        for x in parts:
            applied = applied + x.astype(jnp.float32)
        mapped = scale * applied - center_shift * now
        if iterate == 0:
            updated = mapped / half_width
        else:
            updated = 2.0 / half_width * mapped - before
        before = now
        now = updated
        own = (scale * now).astype(jnp.bfloat16)
    back = [
        send(x, turned(pairs)) for x, pairs in zip((now[:part], now[part:]), there)
    ]
    return pl.pallas_call(
        unpack_kernel,
        in_specs=[smem, vmem, vmem],
        out_specs=vmem,
        out_shape=jax.ShapeDtypeStruct(start_vectors.shape, jnp.float32),
        name="unpack",
    )(core_arg, *back)


def solution(mesh):
    in_specs = (
        P(None, ("row", "col")),
        P(("row", "col")),
        P("row", "col", None, None, None),
        P("row", "col", None, None),
        P("row", "col"),
    )
    out_specs = P(None, ("row", "col"))
    return jax.shard_map(
        per_device, mesh=mesh, in_specs=in_specs, out_specs=out_specs, check_vma=False
    )
```

```python
import functools

import jax
import jax.numpy as jnp
from jax import lax
from jax.experimental import pallas as pl
from jax.experimental.pallas import tpu as pltpu
from jax.sharding import PartitionSpec as P

STEPS = 3

center_shift = 0.5
half_width = 3.0

UNROLL = 32
VMEM_LIMIT = 24 * 1024 * 1024
AXES = ("row", "col")
PAD = 8


class Layout:
    def __init__(self, rows, cols):
        self.rows, self.cols = rows, cols
        self.chips = cols // 2
        self.fast = 2
        self.slow = rows // 2
        self.group = self.slow // self.chips
        assert self.group * self.chips * self.fast == rows

    def device(self, slow, fast, chip, core):
        return (slow * self.fast + fast) * self.cols + chip * 2 + core

    def home(self, chunk):
        chip, k = chunk // self.rows, chunk % self.rows
        e, f, t = k % self.chips, (k // self.chips) % self.fast, k // (self.chips * self.fast)
        return (chip ^ e) * self.group + t, f, chip

    def moves_home(self, swap, e):
        pairs = []
        for chunk in range(self.rows * self.chips):
            row, chip = chunk // self.chips, chunk % self.chips
            for core in range(2):
                source = row * self.cols + chip * 2 + core
                slow, fast, home_chip = self.home(chunk)
                keeper = slow ^ (e * self.group)
                pairs.append((source, self.device(keeper, fast, home_chip, core ^ swap)))
        return pairs

    def moves_slow(self, d):
        return [
            (self.device(s, f, c, q), self.device(s ^ d, f, c, q))
            for s in range(self.slow) for f in range(self.fast)
            for c in range(self.chips) for q in range(2)
        ]

    def moves_fast(self):
        return [
            (self.device(s, f, c, q), self.device(s, f ^ 1, c, q))
            for s in range(self.slow) for f in range(self.fast)
            for c in range(self.chips) for q in range(2)
        ]

    def moves_root(self, d):
        return [
            (
                self.device(s, f, s // self.group, q),
                self.device(s, f, (s // self.group) ^ d, q),
            )
            for s in range(self.slow) for f in range(self.fast) for q in range(2)
        ]

    def moves_core(self):
        return [(i, i ^ 1) for i in range(self.rows * self.cols)]


def turned(pairs):
    return [(b, a) for a, b in pairs]


def pack_kernel(core_ref, x_ref, s_ref, same_ref, other_ref):
    core = core_ref[0]
    blocks, _, block_len = same_ref.shape
    half = x_ref.shape[0] // 2
    for b in range(blocks):
        span = slice(b * block_len, (b + 1) * block_len)
        scale = jnp.broadcast_to(s_ref[:, span], (PAD, block_len))
        for out, which in ((same_ref, core), (other_ref, 1 - core)):
            start = pl.multiple_of(which * half, half)
            out[b, :half] = x_ref[pl.ds(start, half), span]
            out[b, half:] = scale


def unpack_kernel(core_ref, same_ref, other_ref, out_ref):
    core = core_ref[0]
    blocks, half, block_len = same_ref.shape
    for b in range(blocks):
        span = slice(b * block_len, (b + 1) * block_len)
        for part, which in ((same_ref, core), (other_ref, 1 - core)):
            start = pl.multiple_of(which * half, half)
            out_ref[pl.ds(start, half), span] = part[b]


def product_kernel(transpose, cap, n_in, n_out, after, meta_ref, *refs):
    slab_refs, refs = refs[:2], refs[2:]
    ins, refs = refs[:n_in], refs[n_in + after:]
    outs, refs = refs[:n_out], refs[n_out:]
    slabs, vecs, acc, slab_sem, vec_sem = refs
    per_in = ins[0].shape[0]
    base = 0 if transpose else 4 * cap
    first_groups = (meta_ref[8 * cap] + (UNROLL - 1)) // UNROLL
    other_groups = (meta_ref[8 * cap + 1] + (UNROLL - 1)) // UNROLL

    def slab_copy(which, g):
        span = pl.ds(g * UNROLL, UNROLL)
        to = pl.ds(which * cap + g * UNROLL, UNROLL)
        sem = slab_sem.at[which * (cap // UNROLL) + g]
        return pltpu.make_async_copy(slab_refs[which].at[span], slabs.at[to], sem)

    def vec_copy(k):
        return pltpu.make_async_copy(
            ins[k], vecs.at[pl.ds(k * per_in, per_in)], vec_sem.at[k]
        )

    for k in range(n_in):
        vec_copy(k).start()

    def start_slab(which, g, carry):
        slab_copy(which, g).start()
        return carry

    lax.fori_loop(0, first_groups, functools.partial(start_slab, 0), 0)
    lax.fori_loop(0, other_groups, functools.partial(start_slab, 1), 0)
    acc[...] = jnp.zeros_like(acc)
    for k in range(n_in):
        vec_copy(k).wait()

    def body(which, g, carry):
        slab_copy(which, g).wait()
        start = which * cap + g * UNROLL
        products = []
        for u in range(UNROLL):
            source = meta_ref[base + start + u]
            dims = (((1,), (0 if transpose else 1,)), ((), ()))
            products.append(lax.dot_general(
                vecs[source], slabs[start + u], dims, preferred_element_type=jnp.float32
            ))
        for u, product in enumerate(products):
            acc[meta_ref[base + 2 * cap + start + u]] += product
        return carry

    lax.fori_loop(0, first_groups, functools.partial(body, 0), 0)
    lax.fori_loop(0, other_groups, functools.partial(body, 1), 0)
    size = outs[0].shape[0]
    for k, out in enumerate(outs):
        out[...] = acc[k * size:(k + 1) * size].astype(out.dtype)


def products(meta, slabs, ins, out_dtypes, out_blocks, transpose, after=()):
    cap, block_len, _ = slabs[0].shape
    per_in, vec_count, _ = ins[0].shape
    in_blocks = per_in * len(ins)
    total_out = out_blocks * len(out_dtypes)
    return pl.pallas_call(
        functools.partial(
            product_kernel, transpose, cap, len(ins), len(out_dtypes), len(after)
        ),
        in_specs=[pl.BlockSpec(memory_space=pltpu.SMEM)]
        + [pl.BlockSpec(memory_space=pl.ANY)] * (2 + len(ins) + len(after)),
        out_specs=[pl.BlockSpec(memory_space=pltpu.VMEM)] * len(out_dtypes),
        out_shape=[
            jax.ShapeDtypeStruct((out_blocks, vec_count, block_len), dtype)
            for dtype in out_dtypes
        ],
        scratch_shapes=[
            pltpu.VMEM((2 * cap, block_len, block_len), jnp.bfloat16),
            pltpu.VMEM((in_blocks, vec_count, block_len), jnp.bfloat16),
            pltpu.VMEM((total_out + 1, vec_count, block_len), jnp.float32),
            pltpu.SemaphoreType.DMA((2 * cap // UNROLL,)),
            pltpu.SemaphoreType.DMA((len(ins),)),
        ],
        compiler_params=pltpu.CompilerParams(vmem_limit_bytes=VMEM_LIMIT),
        cost_estimate=pl.CostEstimate(
            flops=4 * cap * vec_count * block_len * block_len,
            bytes_accessed=4 * cap * block_len * block_len,
            transcendentals=0,
        ),
        name="transposed" if transpose else "direct",
    )(meta, *slabs, *ins, *after)


def per_device(start_vectors, scaling, block_values, block_places, block_counts):
    at = Layout(lax.axis_size("row"), lax.axis_size("col"))
    cap = block_values.shape[2]
    block_len = block_values.shape[-1]
    half = start_vectors.shape[0] // 2
    part = start_vectors.shape[1] // block_len
    per_chunk = 2 * part
    row_index = lax.axis_index("row").astype(jnp.int32)
    col_index = lax.axis_index("col").astype(jnp.int32)
    slow, fast = row_index // at.fast, row_index % at.fast
    chip, core = col_index // 2, col_index % 2
    root = slow // at.group
    is_root = chip == root
    core_arg = core.reshape(1)
    smem = pl.BlockSpec(memory_space=pltpu.SMEM)
    vmem = pl.BlockSpec(memory_space=pltpu.VMEM)

    def send(x, pairs):
        return lax.ppermute(x, AXES, pairs)

    slabs = block_values.reshape(cap, block_len, block_len)
    slots = jnp.concatenate([block_places.reshape(2 * cap), block_counts.reshape(1)])
    other_slabs = send(slabs, at.moves_core())
    other_slots = send(slots, at.moves_core())

    packed = pl.pallas_call(
        pack_kernel,
        in_specs=[smem, vmem, vmem],
        out_specs=[vmem, vmem],
        out_shape=[jax.ShapeDtypeStruct((part, half + PAD, block_len), jnp.float32)] * 2,
        name="pack",
    )(core_arg, start_vectors, scaling.reshape(1, -1))
    kept = jnp.concatenate(
        [
            send(x, at.moves_home(swap, e))
            for e in range(at.chips) for swap, x in enumerate(packed)
        ],
        axis=0,
    )
    now = kept[:, :half]
    scale = kept[:, half:half + 1]
    own = (scale * now).astype(jnp.bfloat16)
    n_kept = at.chips * per_chunk

    n_col = at.rows * per_chunk
    n_row = at.chips * per_chunk
    lists = []
    for which, held in enumerate((slots, other_slots)):
        row_block, col_block = held[:cap], held[cap:2 * cap]
        live = jnp.arange(cap, dtype=jnp.int32) < held[2 * cap]

        def inside(block):
            return ((block // part) ^ core) * part + block % part

        e = row_block // per_chunk
        row_at = e * per_chunk + inside(row_block % per_chunk)
        block = (core ^ which) * (n_col // 2) + col_block
        k = block // per_chunk
        e, f, t = k % at.chips, (k // at.chips) % at.fast, k // (at.chips * at.fast)
        d = slow ^ ((chip ^ e) * at.group + t)
        place = (d % at.group) * at.chips + d // at.group
        col_at = ((fast ^ f) * at.slow + place) * per_chunk + inside(block % per_chunk)
        lists.append((
            row_at, jnp.where(live, col_at, n_col), col_at, jnp.where(live, row_at, n_row)
        ))
    meta = jnp.concatenate(
        [jnp.concatenate([mine, theirs]) for mine, theirs in zip(*lists)]
        + [slots[2 * cap:], other_slots[2 * cap:]]
    )
    both = (slabs, other_slabs)

    before = None
    for iterate in range(STEPS):
        row_tile = own
        for d in range(1, at.chips):
            got = send(own, at.moves_root(d))
            row_tile = jnp.where((chip ^ root) == d, got, row_tile)
        near = jnp.concatenate(
            [own] + [send(own, at.moves_slow(g)) for g in range(1, at.group)], axis=0
        )
        far = send(near, at.moves_fast())
        near_sum, far_sum = products(
            meta, both, (row_tile,), (jnp.float32, jnp.bfloat16), n_col // 2, True
        )
        from_fast = send(far_sum, at.moves_fast())
        (row_sum,) = products(
            meta, both, (near, far), (jnp.bfloat16,), n_row, False, after=(far_sum,)
        )
        from_row = [send(row_sum, turned(at.moves_root(d))) for d in range(1, at.chips)]

        def sum_of(g):
            span = slice(g * n_kept, (g + 1) * n_kept)
            return near_sum[span] + from_fast[span].astype(jnp.float32)

        total = sum_of(0)
        for g in range(1, at.group):
            total = total + send(
                sum_of(g).astype(jnp.bfloat16), at.moves_slow(g)
            ).astype(jnp.float32)
        total = total + jnp.where(is_root, row_sum, jnp.zeros_like(row_sum)).astype(jnp.float32)
        for x in from_row:
            total = total + x.astype(jnp.float32)
        message = total.astype(jnp.bfloat16)
        applied = total
        for e in range(1, at.chips):
            got = send(message, at.moves_slow(e * at.group))
            got = [got[k * per_chunk:(k + 1) * per_chunk] for k in range(at.chips)]
            got = jnp.concatenate([got[k ^ e] for k in range(at.chips)], axis=0)
            applied = applied + got.astype(jnp.float32)
        mapped = scale * applied - center_shift * now
        if iterate == 0:
            updated = mapped / half_width
        else:
            updated = 2.0 / half_width * mapped - before
        before = now
        now = updated
        own = (scale * now).astype(jnp.bfloat16)
    back = [
        send(now[swap * part:(swap + 1) * part], turned(at.moves_home(swap, 0)))
        for swap in range(2)
    ]
    return pl.pallas_call(
        unpack_kernel,
        in_specs=[smem, vmem, vmem],
        out_specs=vmem,
        out_shape=jax.ShapeDtypeStruct(start_vectors.shape, jnp.float32),
        name="unpack",
    )(core_arg, *back)


def solution(mesh):
    in_specs = (
        P(None, ("row", "col")),
        P(("row", "col")),
        P("row", "col", None, None, None),
        P("row", "col", None, None),
        P("row", "col"),
    )
    out_specs = P(None, ("row", "col"))
    return jax.shard_map(
        per_device, mesh=mesh, in_specs=in_specs, out_specs=out_specs, check_vma=False
    )
```

```python
import functools

import jax
import jax.numpy as jnp
from jax import lax
from jax.experimental import pallas as pl
from jax.experimental.pallas import tpu as pltpu
from jax.sharding import PartitionSpec as P

STEPS = 3

center_shift = 0.5
half_width = 3.0

UNROLL = 32
PACK = 4
VMEM_LIMIT = 24 * 1024 * 1024
AXES = ("row", "col")
PAD = 8


class Layout:
    def __init__(self, rows, cols):
        self.rows, self.cols = rows, cols
        self.chips = cols // 2
        self.fast = 2
        self.slow = rows // 2
        self.group = self.slow // self.chips
        assert self.group * self.chips * self.fast == rows

    def device(self, slow, fast, chip, core):
        return (slow * self.fast + fast) * self.cols + chip * 2 + core

    def home(self, chunk):
        chip, k = chunk // self.rows, chunk % self.rows
        e, f, t = k % self.chips, (k // self.chips) % self.fast, k // (self.chips * self.fast)
        return (chip ^ e) * self.group + t, f, chip

    def moves_home(self, swap, e):
        pairs = []
        for chunk in range(self.rows * self.chips):
            row, chip = chunk // self.chips, chunk % self.chips
            for core in range(2):
                source = row * self.cols + chip * 2 + core
                slow, fast, home_chip = self.home(chunk)
                keeper = slow ^ (e * self.group)
                pairs.append((source, self.device(keeper, fast, home_chip, core ^ swap)))
        return pairs

    def moves_slow(self, d):
        return [
            (self.device(s, f, c, q), self.device(s ^ d, f, c, q))
            for s in range(self.slow) for f in range(self.fast)
            for c in range(self.chips) for q in range(2)
        ]

    def moves_fast(self):
        return [
            (self.device(s, f, c, q), self.device(s, f ^ 1, c, q))
            for s in range(self.slow) for f in range(self.fast)
            for c in range(self.chips) for q in range(2)
        ]

    def moves_root(self, d):
        return [
            (
                self.device(s, f, s // self.group, q),
                self.device(s, f, (s // self.group) ^ d, q),
            )
            for s in range(self.slow) for f in range(self.fast) for q in range(2)
        ]

    def moves_core(self):
        return [(i, i ^ 1) for i in range(self.rows * self.cols)]


def turned(pairs):
    return [(b, a) for a, b in pairs]


def pack_kernel(core_ref, x_ref, s_ref, same_ref, other_ref):
    core = core_ref[0]
    blocks, _, block_len = same_ref.shape
    half = x_ref.shape[0] // 2
    for b in range(blocks):
        span = slice(b * block_len, (b + 1) * block_len)
        scale = jnp.broadcast_to(s_ref[:, span], (PAD, block_len))
        for out, which in ((same_ref, core), (other_ref, 1 - core)):
            start = pl.multiple_of(which * half, half)
            out[b, :half] = x_ref[pl.ds(start, half), span]
            out[b, half:] = scale


def unpack_kernel(core_ref, same_ref, other_ref, out_ref):
    core = core_ref[0]
    blocks, half, block_len = same_ref.shape
    for b in range(blocks):
        span = slice(b * block_len, (b + 1) * block_len)
        for part, which in ((same_ref, core), (other_ref, 1 - core)):
            start = pl.multiple_of(which * half, half)
            out_ref[pl.ds(start, half), span] = part[b]


def product_kernel(transpose, cap, n_out, after, meta_ref, vecs_ref, *refs):
    slab_refs, refs = refs[:2], refs[2 + after:]
    outs, refs = refs[:n_out], refs[n_out:]
    slabs, acc, slab_sem = refs
    base = 0 if transpose else 4 * cap
    groups = [
        (meta_ref[8 * cap + which] + (UNROLL - 1)) // UNROLL for which in range(2)
    ]

    def slab_copy(which, g):
        span = pl.ds(g * UNROLL, UNROLL)
        to = pl.ds(which * cap + g * UNROLL, UNROLL)
        sem = slab_sem.at[which * (cap // UNROLL) + g]
        return pltpu.make_async_copy(slab_refs[which].at[span], slabs.at[to], sem)

    def start_slab(which, g, carry):
        slab_copy(which, g).start()
        return carry

    for which in range(2):
        lax.fori_loop(0, groups[which], functools.partial(start_slab, which), 0)
    acc[...] = jnp.zeros_like(acc)
    vec_count, block_len = vecs_ref.shape[1:]
    zero = jnp.zeros((vec_count, block_len), jnp.bfloat16)

    def body(which, g, carry):
        slab_copy(which, g).wait()
        start = which * cap + g * UNROLL
        products = []
        for u in range(0, UNROLL, PACK):
            v = [vecs_ref[meta_ref[base + start + u + k]] for k in range(PACK)]
            m = [slabs[start + u + k] for k in range(PACK)]
            left = jnp.concatenate([
                jnp.concatenate([v[0], zero, v[2], zero], axis=0),
                jnp.concatenate([zero, v[1], zero, v[3]], axis=0),
            ], axis=1)
            if transpose:
                halves = [jnp.concatenate(m[:2], axis=0), jnp.concatenate(m[2:], axis=0)]
                right, dims = jnp.concatenate(halves, axis=1), (((1,), (0,)), ((), ()))
            else:
                halves = [jnp.concatenate(m[:2], axis=1), jnp.concatenate(m[2:], axis=1)]
                right, dims = jnp.concatenate(halves, axis=0), (((1,), (1,)), ((), ()))
            products.append(
                lax.dot_general(left, right, dims, preferred_element_type=jnp.float32)
            )
        for u in range(UNROLL):
            k = u % PACK
            rows = slice(k * vec_count, (k + 1) * vec_count)
            lanes = slice((k // 2) * block_len, (k // 2 + 1) * block_len)
            acc[meta_ref[base + 2 * cap + start + u]] += products[u // PACK][rows, lanes]
        return carry

    for which in range(2):
        lax.fori_loop(0, groups[which], functools.partial(body, which), 0)
    size = outs[0].shape[0]
    for k, out in enumerate(outs):
        out[...] = acc[k * size:(k + 1) * size].astype(out.dtype)


def products(meta, slabs, vecs, out_dtypes, out_blocks, transpose, after=()):
    cap, block_len, _ = slabs[0].shape
    vec_count = vecs.shape[1]
    total_out = out_blocks * len(out_dtypes)
    anywhere = pl.BlockSpec(memory_space=pl.ANY)
    vmem = pl.BlockSpec(memory_space=pltpu.VMEM)
    return pl.pallas_call(
        functools.partial(product_kernel, transpose, cap, len(out_dtypes), len(after)),
        in_specs=[pl.BlockSpec(memory_space=pltpu.SMEM), vmem]
        + [anywhere] * (2 + len(after)),
        out_specs=[vmem] * len(out_dtypes),
        out_shape=[
            jax.ShapeDtypeStruct((out_blocks, vec_count, block_len), dtype)
            for dtype in out_dtypes
        ],
        scratch_shapes=[
            pltpu.VMEM((2 * cap, block_len, block_len), jnp.bfloat16),
            pltpu.VMEM((total_out + 1, vec_count, block_len), jnp.float32),
            pltpu.SemaphoreType.DMA((2 * cap // UNROLL,)),
        ],
        compiler_params=pltpu.CompilerParams(vmem_limit_bytes=VMEM_LIMIT),
        cost_estimate=pl.CostEstimate(
            flops=4 * cap * vec_count * block_len * block_len,
            bytes_accessed=4 * cap * block_len * block_len,
            transcendentals=0,
        ),
        name="transposed" if transpose else "direct",
    )(meta, vecs, *slabs, *after)


def per_device(start_vectors, scaling, block_values, block_places, block_counts):
    at = Layout(lax.axis_size("row"), lax.axis_size("col"))
    cap = block_values.shape[2]
    block_len = block_values.shape[-1]
    half = start_vectors.shape[0] // 2
    part = start_vectors.shape[1] // block_len
    per_chunk = 2 * part
    row_index = lax.axis_index("row").astype(jnp.int32)
    col_index = lax.axis_index("col").astype(jnp.int32)
    slow, fast = row_index // at.fast, row_index % at.fast
    chip, core = col_index // 2, col_index % 2
    root = slow // at.group
    is_root = chip == root
    core_arg = core.reshape(1)
    smem = pl.BlockSpec(memory_space=pltpu.SMEM)
    vmem = pl.BlockSpec(memory_space=pltpu.VMEM)

    def send(x, pairs):
        return lax.ppermute(x, AXES, pairs)

    slabs = block_values.reshape(cap, block_len, block_len)
    slots = jnp.concatenate([block_places.reshape(2 * cap), block_counts.reshape(1)])
    other_slabs = send(slabs, at.moves_core())
    other_slots = send(slots, at.moves_core())

    packed = pl.pallas_call(
        pack_kernel,
        in_specs=[smem, vmem, vmem],
        out_specs=[vmem, vmem],
        out_shape=[jax.ShapeDtypeStruct((part, half + PAD, block_len), jnp.float32)] * 2,
        name="pack",
    )(core_arg, start_vectors, scaling.reshape(1, -1))
    kept = jnp.concatenate(
        [
            send(x, at.moves_home(swap, e))
            for e in range(at.chips) for swap, x in enumerate(packed)
        ],
        axis=0,
    )
    n_col = at.rows * per_chunk
    n_row = at.chips * per_chunk
    lists = []
    for which, held in enumerate((slots, other_slots)):
        row_block, col_block = held[:cap], held[cap:2 * cap]
        live = jnp.arange(cap, dtype=jnp.int32) < held[2 * cap]

        def inside(block):
            return ((block // part) ^ core) * part + block % part

        e = row_block // per_chunk
        row_at = e * per_chunk + inside(row_block % per_chunk)
        block = (core ^ which) * (n_col // 2) + col_block
        k = block // per_chunk
        e, f, t = k % at.chips, (k // at.chips) % at.fast, k // (at.chips * at.fast)
        d = slow ^ ((chip ^ e) * at.group + t)
        place = (d % at.group) * at.chips + d // at.group
        col_at = ((fast ^ f) * at.slow + place) * per_chunk + inside(block % per_chunk)
        lists.append((
            row_at, jnp.where(live, col_at, n_col), col_at, jnp.where(live, row_at, n_row)
        ))
    meta = jnp.concatenate(
        [jnp.concatenate([mine, theirs]) for mine, theirs in zip(*lists)]
        + [slots[2 * cap:], other_slots[2 * cap:]]
    )
    kept, meta, other_slabs = lax.optimization_barrier((kept, meta, other_slabs))
    both = (send(other_slabs, at.moves_core()), other_slabs)
    now = kept[:, :half]
    scale = kept[:, half:half + 1]
    own = (scale * now).astype(jnp.bfloat16)
    n_kept = at.chips * per_chunk

    before = None
    for iterate in range(STEPS):
        row_tile = own
        for d in range(1, at.chips):
            got = send(own, at.moves_root(d))
            row_tile = jnp.where((chip ^ root) == d, got, row_tile)
        near = [own] + [send(own, at.moves_slow(g)) for g in range(1, at.group)]
        far = [send(x, at.moves_fast()) for x in near]
        sums = products(
            meta, both, row_tile, (jnp.float32,) * at.group + (jnp.bfloat16,) * at.group,
            n_kept, True,
        )
        near_sums, far_sums = sums[:at.group], sums[at.group:]
        from_fast = [send(x, at.moves_fast()) for x in far_sums[::-1]][::-1]
        (row_sum,) = products(
            meta, both, jnp.concatenate(near + far, axis=0), (jnp.bfloat16,), n_row, False,
            after=far_sums,
        )
        from_row = [send(row_sum, turned(at.moves_root(d))) for d in range(1, at.chips)]
        sums = [x + y.astype(jnp.float32) for x, y in zip(near_sums, from_fast)]
        total = sums[0]
        for g in range(1, at.group):
            total = total + send(
                sums[g].astype(jnp.bfloat16), at.moves_slow(g)
            ).astype(jnp.float32)
        total = total + jnp.where(is_root, row_sum, jnp.zeros_like(row_sum)).astype(jnp.float32)
        for x in from_row:
            total = total + x.astype(jnp.float32)
        message = total.astype(jnp.bfloat16)

        def chunk_of(x, e):
            return x[e * per_chunk:(e + 1) * per_chunk]

        last = iterate == STEPS - 1
        if last:
            total, now, scale = chunk_of(total, 0), chunk_of(now, 0), chunk_of(scale, 0)
            before = chunk_of(before, 0)
        applied = total
        for e in range(1, at.chips):
            if last:
                got = send(chunk_of(message, e), at.moves_slow(e * at.group))
            else:
                got = send(message, at.moves_slow(e * at.group))
                got = jnp.concatenate([chunk_of(got, k ^ e) for k in range(at.chips)], axis=0)
            applied = applied + got.astype(jnp.float32)
        mapped = scale * applied - center_shift * now
        if iterate == 0:
            updated = mapped / half_width
        else:
            updated = 2.0 / half_width * mapped - before
        before = now
        now = updated
        if not last:
            own = (scale * now).astype(jnp.bfloat16)
    back = [
        send(now[swap * part:(swap + 1) * part], turned(at.moves_home(swap, 0)))
        for swap in range(2)
    ]
    return pl.pallas_call(
        unpack_kernel,
        in_specs=[smem, vmem, vmem],
        out_specs=vmem,
        out_shape=jax.ShapeDtypeStruct(start_vectors.shape, jnp.float32),
        name="unpack",
    )(core_arg, *back)


def solution(mesh):
    in_specs = (
        P(None, ("row", "col")),
        P(("row", "col")),
        P("row", "col", None, None, None),
        P("row", "col", None, None),
        P("row", "col"),
    )
    out_specs = P(None, ("row", "col"))
    return jax.shard_map(
        per_device, mesh=mesh, in_specs=in_specs, out_specs=out_specs, check_vma=False
    )
```

```python
import functools

import jax
import jax.numpy as jnp
from jax import lax
from jax.experimental import pallas as pl
from jax.experimental.pallas import tpu as pltpu
from jax.sharding import PartitionSpec as P

STEPS = 3

center_shift = 0.5
half_width = 3.0

UNROLL = 32
PACK = 4
VMEM_LIMIT = 24 * 1024 * 1024
AXES = ("row", "col")
PAD = 8


class Layout:
    def __init__(self, rows, cols):
        self.rows, self.cols = rows, cols
        self.chips = cols // 2
        self.fast = 2
        self.slow = rows // 2
        self.group = self.slow // self.chips
        assert self.group * self.chips * self.fast == rows

    def device(self, slow, fast, chip, core):
        return (slow * self.fast + fast) * self.cols + chip * 2 + core

    def home(self, chunk):
        chip, k = chunk // self.rows, chunk % self.rows
        e, f, t = k % self.chips, (k // self.chips) % self.fast, k // (self.chips * self.fast)
        return (chip ^ e) * self.group + t, f, chip

    def moves_home(self, swap):
        pairs = []
        for chunk in range(self.rows * self.chips):
            row, chip = chunk // self.chips, chunk % self.chips
            for core in range(2):
                source = row * self.cols + chip * 2 + core
                pairs.append((source, self.device(*self.home(chunk), core ^ swap)))
        return pairs

    def moves_slow(self, d):
        return [
            (self.device(s, f, c, q), self.device(s ^ d, f, c, q))
            for s in range(self.slow) for f in range(self.fast)
            for c in range(self.chips) for q in range(2)
        ]

    def moves_fast(self):
        return [
            (self.device(s, f, c, q), self.device(s, f ^ 1, c, q))
            for s in range(self.slow) for f in range(self.fast)
            for c in range(self.chips) for q in range(2)
        ]

    def moves_chip(self, d, swap=0):
        return [
            (self.device(s, f, c, q), self.device(s, f, c ^ d, q ^ swap))
            for s in range(self.slow) for f in range(self.fast)
            for c in range(self.chips) for q in range(2)
        ]

    def moves_core(self):
        return [(i, i ^ 1) for i in range(self.rows * self.cols)]


def turned(pairs):
    return [(b, a) for a, b in pairs]


def product_kernel(transpose, cap, n_out, after, meta_in, vecs_in, *refs):
    slab_refs, refs = refs[:2], refs[2 + after:]
    outs, refs = refs[:n_out], refs[n_out:]
    meta_ref, vecs_ref, slabs, acc, slab_sem, in_sem = refs
    base = 0 if transpose else 4 * cap

    def slab_copy(which, g):
        span = pl.ds(g * UNROLL, UNROLL)
        to = pl.ds(which * cap + g * UNROLL, UNROLL)
        sem = slab_sem.at[which * (cap // UNROLL) + g]
        return pltpu.make_async_copy(slab_refs[which].at[span], slabs.at[to], sem)

    def start_slab(which, g, carry):
        slab_copy(which, g).start()
        return carry

    meta_copy = pltpu.make_async_copy(meta_in, meta_ref, in_sem.at[0])
    vecs_copy = pltpu.make_async_copy(vecs_in, vecs_ref, in_sem.at[1])
    meta_copy.start()
    slab_copy(0, 0).start()
    vecs_copy.start()
    slab_copy(1, 0).start()
    acc[...] = jnp.zeros_like(acc)
    meta_copy.wait()
    groups = [
        jnp.maximum((meta_ref[8 * cap + which] + (UNROLL - 1)) // UNROLL, 1)
        for which in range(2)
    ]
    for which in range(2):
        lax.fori_loop(1, groups[which], functools.partial(start_slab, which), 0)
    vecs_copy.wait()
    vec_count, block_len = vecs_ref.shape[1:]
    zero = jnp.zeros((vec_count, block_len), jnp.bfloat16)

    def body(which, g, carry):
        slab_copy(which, g).wait()
        start = which * cap + g * UNROLL
        products = []
        for u in range(0, UNROLL, PACK):
            v = [vecs_ref[meta_ref[base + start + u + k]] for k in range(PACK)]
            m = [slabs[start + u + k] for k in range(PACK)]
            left = jnp.concatenate([
                jnp.concatenate([v[0], zero, v[2], zero], axis=0),
                jnp.concatenate([zero, v[1], zero, v[3]], axis=0),
            ], axis=1)
            if transpose:
                halves = [jnp.concatenate(m[:2], axis=0), jnp.concatenate(m[2:], axis=0)]
                right, dims = jnp.concatenate(halves, axis=1), (((1,), (0,)), ((), ()))
            else:
                halves = [jnp.concatenate(m[:2], axis=1), jnp.concatenate(m[2:], axis=1)]
                right, dims = jnp.concatenate(halves, axis=0), (((1,), (1,)), ((), ()))
            products.append(
                lax.dot_general(left, right, dims, preferred_element_type=jnp.float32)
            )
        for u in range(UNROLL):
            k = u % PACK
            rows = slice(k * vec_count, (k + 1) * vec_count)
            lanes = slice((k // 2) * block_len, (k // 2 + 1) * block_len)
            acc[meta_ref[base + 2 * cap + start + u]] += products[u // PACK][rows, lanes]
        return carry

    for which in range(2):
        lax.fori_loop(0, groups[which], functools.partial(body, which), 0)
    size = outs[0].shape[0]
    for k, out in enumerate(outs):
        out[...] = acc[k * size:(k + 1) * size].astype(out.dtype)


def products(meta, slabs, vecs, out_dtypes, out_blocks, transpose, after=()):
    cap, block_len, _ = slabs[0].shape
    vec_count = vecs.shape[1]
    total_out = out_blocks * len(out_dtypes)
    anywhere = pl.BlockSpec(memory_space=pl.ANY)
    vmem = pl.BlockSpec(memory_space=pltpu.VMEM)
    return pl.pallas_call(
        functools.partial(product_kernel, transpose, cap, len(out_dtypes), len(after)),
        in_specs=[anywhere] * (4 + len(after)),
        out_specs=[vmem] * len(out_dtypes),
        out_shape=[
            jax.ShapeDtypeStruct((out_blocks, vec_count, block_len), dtype)
            for dtype in out_dtypes
        ],
        scratch_shapes=[
            pltpu.SMEM(meta.shape, jnp.int32),
            pltpu.VMEM(vecs.shape, jnp.bfloat16),
            pltpu.VMEM((2 * cap, block_len, block_len), jnp.bfloat16),
            pltpu.VMEM((total_out + 1, vec_count, block_len), jnp.float32),
            pltpu.SemaphoreType.DMA((2 * cap // UNROLL,)),
            pltpu.SemaphoreType.DMA((2,)),
        ],
        compiler_params=pltpu.CompilerParams(vmem_limit_bytes=VMEM_LIMIT),
        cost_estimate=pl.CostEstimate(
            flops=4 * cap * vec_count * block_len * block_len,
            bytes_accessed=2 * vec_count * block_len * (vecs.shape[0] + total_out),
            transcendentals=0,
        ),
        name="transposed" if transpose else "direct",
    )(meta, vecs, *slabs, *after)


def per_device(start_vectors, scaling, block_values, block_places, block_counts):
    at = Layout(lax.axis_size("row"), lax.axis_size("col"))
    cap = block_values.shape[2]
    block_len = block_values.shape[-1]
    half = start_vectors.shape[0] // 2
    part = start_vectors.shape[1] // block_len
    per_chunk = 2 * part
    row_index = lax.axis_index("row").astype(jnp.int32)
    col_index = lax.axis_index("col").astype(jnp.int32)
    slow, fast = row_index // at.fast, row_index % at.fast
    chip, core = col_index // 2, col_index % 2
    root = slow // at.group
    is_root = chip == root
    def send(x, pairs):
        return lax.ppermute(x, AXES, pairs)

    slabs = block_values.reshape(cap, block_len, block_len)
    slots = jnp.concatenate([block_places.reshape(2 * cap), block_counts.reshape(1)])
    other_slabs = send(slabs, at.moves_core())
    other_slots = send(slots, at.moves_core())

    halves = start_vectors.reshape(2, half, part, block_len).transpose(0, 2, 1, 3)
    scale_rows = jnp.broadcast_to(
        scaling.reshape(1, part, 1, block_len), (2, part, PAD, block_len)
    )
    halves = jnp.concatenate([halves, scale_rows], axis=2)
    packed = [
        jnp.where(core == swap, halves[0], halves[1]) for swap in range(2)
    ]
    pieces = [
        jnp.concatenate([
            packed[swap] if (d, swap) == (0, 0) else send(packed[swap], at.moves_chip(d, swap))
            for swap in range(2)
        ], axis=0)
        for d in range(at.chips)
    ]
    n_kept = at.chips * per_chunk

    def chunk_of(x, e):
        return x[e * per_chunk:(e + 1) * per_chunk]

    def pick(index, choices):
        x = choices[0]
        for d in range(1, len(choices)):
            x = jnp.where(index == d, choices[d], x)
        return x

    row_state = jnp.concatenate([pick(chip ^ e, pieces) for e in range(at.chips)], axis=0)

    n_col = at.rows * per_chunk
    n_row = at.chips * per_chunk
    lists = []
    for which, held in enumerate((slots, other_slots)):
        row_block, col_block = held[:cap], held[cap:2 * cap]
        live = jnp.arange(cap, dtype=jnp.int32) < held[2 * cap]

        def inside(block):
            return ((block // part) ^ core) * part + block % part

        e = row_block // per_chunk
        row_at = e * per_chunk + inside(row_block % per_chunk)
        block = (core ^ which) * (n_col // 2) + col_block
        k = block // per_chunk
        e, f, t = k % at.chips, (k // at.chips) % at.fast, k // (at.chips * at.fast)
        d = slow ^ ((chip ^ e) * at.group + t)
        place = (d % at.group) * at.chips + d // at.group
        col_at = ((fast ^ f) * at.slow + place) * per_chunk + inside(block % per_chunk)
        lists.append((
            row_at, jnp.where(live, col_at, n_col), col_at, jnp.where(live, row_at, n_row)
        ))
    meta = jnp.concatenate(
        [jnp.concatenate([mine, theirs]) for mine, theirs in zip(*lists)]
        + [slots[2 * cap:], other_slots[2 * cap:], jnp.zeros(126, jnp.int32)]
    )
    row_state, meta, other_slabs = lax.optimization_barrier((row_state, meta, other_slabs))
    both = (send(other_slabs, at.moves_core()), other_slabs)

    def across(x):
        return [send(x, at.moves_slow(d * at.group)) for d in range(1, at.chips)]

    def kept_of(x, got):
        got = [
            jnp.concatenate([chunk_of(y, k ^ d) for k in range(at.chips)], axis=0)
            for d, y in enumerate(got, 1)
        ]
        return pick(chip ^ root, [x] + got)

    row_now, row_scale = row_state[:, :half], row_state[:, half:half + 1]
    row_tile = (row_scale * row_now).astype(jnp.bfloat16)
    sent_across = across(row_now), across(row_scale)
    before = None
    for iterate in range(STEPS):
        near, far = [], []

        def gather():
            near.extend([own] + [send(own, at.moves_slow(g)) for g in range(1, at.group)])
            far.extend([send(x, at.moves_fast()) for x in near])

        if iterate > 0:
            row_tile = pick(
                chip ^ root,
                [own] + [send(own, at.moves_chip(d)) for d in range(1, at.chips)],
            )
            gather()
        sums = products(
            meta, both, row_tile, (jnp.float32,) * at.group + (jnp.bfloat16,) * at.group,
            n_kept, True,
        )
        if iterate == 0:
            sums, sent_across = lax.optimization_barrier((sums, sent_across))
            now, scale = (kept_of(x, y) for x, y in zip((row_now, row_scale), sent_across))
            own = (scale * now).astype(jnp.bfloat16)
            gather()
        near_sums, far_sums = sums[:at.group], sums[at.group:]
        from_fast = [send(x, at.moves_fast()) for x in far_sums[::-1]][::-1]
        (row_sum,) = products(
            meta, both, jnp.concatenate(near + far, axis=0), (jnp.bfloat16,), n_row, False,
            after=far_sums,
        )
        from_row = [row_sum] + [
            send(row_sum, at.moves_chip(d)) for d in range(1, at.chips)
        ]
        sums = [x + y.astype(jnp.float32) for x, y in zip(near_sums, from_fast)]
        total = sums[0]
        for g in range(1, at.group):
            total = total + send(
                sums[g].astype(jnp.bfloat16), at.moves_slow(g)
            ).astype(jnp.float32)
        for x in from_row:
            total = total + jnp.where(is_root, x, jnp.zeros_like(x)).astype(jnp.float32)
        message = total.astype(jnp.bfloat16)
        last = iterate == STEPS - 1
        if last:
            total, now, scale = chunk_of(total, 0), chunk_of(now, 0), chunk_of(scale, 0)
            before = chunk_of(before, 0)
        applied = total
        for e in range(1, at.chips):
            if last:
                got = send(chunk_of(message, e), at.moves_slow(e * at.group))
            else:
                got = send(message, at.moves_slow(e * at.group))
                got = jnp.concatenate([chunk_of(got, k ^ e) for k in range(at.chips)], axis=0)
            applied = applied + got.astype(jnp.float32)
        mapped = scale * applied - center_shift * now
        if iterate == 0:
            updated = mapped / half_width
        else:
            updated = 2.0 / half_width * mapped - before
        before = now
        now = updated
        if not last:
            own = (scale * now).astype(jnp.bfloat16)
    back = [
        send(now[swap * part:(swap + 1) * part], turned(at.moves_home(swap)))
        for swap in range(2)
    ]
    result = jnp.stack([jnp.where(core == k, back[0], back[1]) for k in range(2)])
    return result.transpose(0, 2, 1, 3).reshape(start_vectors.shape)


def solution(mesh):
    in_specs = (
        P(None, ("row", "col")),
        P(("row", "col")),
        P("row", "col", None, None, None),
        P("row", "col", None, None),
        P("row", "col"),
    )
    out_specs = P(None, ("row", "col"))
    return jax.shard_map(
        per_device, mesh=mesh, in_specs=in_specs, out_specs=out_specs, check_vma=False
    )
```

```python
import functools

import jax
import jax.numpy as jnp
from jax import lax
from jax.experimental import pallas as pl
from jax.experimental.pallas import tpu as pltpu
from jax.sharding import PartitionSpec as P

STEPS = 3

center_shift = 0.5
half_width = 3.0

UNROLL = 32
PACK = 4
VMEM_LIMIT = 24 * 1024 * 1024
AXES = ("row", "col")
PAD = 8


class Layout:
    def __init__(self, rows, cols):
        self.rows, self.cols = rows, cols
        self.chips = cols // 2
        self.fast = 2
        self.slow = rows // 2
        self.group = self.slow // self.chips
        assert self.group * self.chips * self.fast == rows

    def device(self, slow, fast, chip, core):
        return (slow * self.fast + fast) * self.cols + chip * 2 + core

    def home(self, chunk):
        chip, k = chunk // self.rows, chunk % self.rows
        e, f, t = k % self.chips, (k // self.chips) % self.fast, k // (self.chips * self.fast)
        return (chip ^ e) * self.group + t, f, chip

    def moves_home(self, swap):
        pairs = []
        for chunk in range(self.rows * self.chips):
            row, chip = chunk // self.chips, chunk % self.chips
            for core in range(2):
                source = row * self.cols + chip * 2 + core
                pairs.append((source, self.device(*self.home(chunk), core ^ swap)))
        return pairs

    def moves_slow(self, d, side=0):
        return [
            (self.device(s, f, c, q), self.device(s ^ d, f ^ side, c, q))
            for s in range(self.slow) for f in range(self.fast)
            for c in range(self.chips) for q in range(2)
        ]

    def moves_chip(self, d, swap=0):
        return [
            (self.device(s, f, c, q), self.device(s, f, c ^ d, q ^ swap))
            for s in range(self.slow) for f in range(self.fast)
            for c in range(self.chips) for q in range(2)
        ]

    def moves_core(self):
        return [(i, i ^ 1) for i in range(self.rows * self.cols)]


def turned(pairs):
    return [(b, a) for a, b in pairs]


def product_kernel(transpose, cap, n_out, after, meta_in, vecs_in, *refs):
    slab_refs, refs = refs[:2], refs[2 + after:]
    outs, refs = refs[:n_out], refs[n_out:]
    meta_ref, vecs_ref, slabs, acc, slab_sem, in_sem = refs
    base = 0 if transpose else 4 * cap

    def slab_copy(which, g):
        span = pl.ds(g * UNROLL, UNROLL)
        to = pl.ds(which * cap + g * UNROLL, UNROLL)
        sem = slab_sem.at[which * (cap // UNROLL) + g]
        return pltpu.make_async_copy(slab_refs[which].at[span], slabs.at[to], sem)

    def start_slab(which, g, carry):
        slab_copy(which, g).start()
        return carry

    meta_copy = pltpu.make_async_copy(meta_in, meta_ref, in_sem.at[0])
    vecs_copy = pltpu.make_async_copy(vecs_in, vecs_ref, in_sem.at[1])
    meta_copy.start()
    slab_copy(0, 0).start()
    vecs_copy.start()
    slab_copy(1, 0).start()
    acc[...] = jnp.zeros_like(acc)
    meta_copy.wait()
    groups = [
        jnp.maximum((meta_ref[8 * cap + which] + (UNROLL - 1)) // UNROLL, 1)
        for which in range(2)
    ]
    for which in range(2):
        lax.fori_loop(1, groups[which], functools.partial(start_slab, which), 0)
    vecs_copy.wait()
    vec_count, block_len = vecs_ref.shape[1:]
    zero = jnp.zeros((vec_count, block_len), jnp.bfloat16)

    def body(which, g, carry):
        slab_copy(which, g).wait()
        start = which * cap + g * UNROLL
        products = []
        for u in range(0, UNROLL, PACK):
            v = [vecs_ref[meta_ref[base + start + u + k]] for k in range(PACK)]
            m = [slabs[start + u + k] for k in range(PACK)]
            left = jnp.concatenate([
                jnp.concatenate([v[0], zero, v[2], zero], axis=0),
                jnp.concatenate([zero, v[1], zero, v[3]], axis=0),
            ], axis=1)
            if transpose:
                halves = [jnp.concatenate(m[:2], axis=0), jnp.concatenate(m[2:], axis=0)]
                right, dims = jnp.concatenate(halves, axis=1), (((1,), (0,)), ((), ()))
            else:
                halves = [jnp.concatenate(m[:2], axis=1), jnp.concatenate(m[2:], axis=1)]
                right, dims = jnp.concatenate(halves, axis=0), (((1,), (1,)), ((), ()))
            products.append(
                lax.dot_general(left, right, dims, preferred_element_type=jnp.float32)
            )
        for u in range(UNROLL):
            k = u % PACK
            rows = slice(k * vec_count, (k + 1) * vec_count)
            lanes = slice((k // 2) * block_len, (k // 2 + 1) * block_len)
            acc[meta_ref[base + 2 * cap + start + u]] += products[u // PACK][rows, lanes]
        return carry

    for which in range(2):
        lax.fori_loop(0, groups[which], functools.partial(body, which), 0)
    size = outs[0].shape[0]
    for k, out in enumerate(outs):
        out[...] = acc[k * size:(k + 1) * size].astype(out.dtype)


def products(meta, slabs, vecs, out_dtypes, out_blocks, transpose, after=()):
    cap, block_len, _ = slabs[0].shape
    vec_count = vecs.shape[1]
    total_out = out_blocks * len(out_dtypes)
    anywhere = pl.BlockSpec(memory_space=pl.ANY)
    vmem = pl.BlockSpec(memory_space=pltpu.VMEM)
    return pl.pallas_call(
        functools.partial(product_kernel, transpose, cap, len(out_dtypes), len(after)),
        in_specs=[anywhere] * (4 + len(after)),
        out_specs=[vmem] * len(out_dtypes),
        out_shape=[
            jax.ShapeDtypeStruct((out_blocks, vec_count, block_len), dtype)
            for dtype in out_dtypes
        ],
        scratch_shapes=[
            pltpu.SMEM(meta.shape, jnp.int32),
            pltpu.VMEM(vecs.shape, jnp.bfloat16),
            pltpu.VMEM((2 * cap, block_len, block_len), jnp.bfloat16),
            pltpu.VMEM((total_out + 1, vec_count, block_len), jnp.float32),
            pltpu.SemaphoreType.DMA((2 * cap // UNROLL,)),
            pltpu.SemaphoreType.DMA((2,)),
        ],
        compiler_params=pltpu.CompilerParams(vmem_limit_bytes=VMEM_LIMIT),
        cost_estimate=pl.CostEstimate(
            flops=4 * cap * vec_count * block_len * block_len,
            bytes_accessed=2 * vec_count * block_len * (vecs.shape[0] + total_out),
            transcendentals=0,
        ),
        name="transposed" if transpose else "direct",
    )(meta, vecs, *slabs, *after)


def per_device(start_vectors, scaling, block_values, block_places, block_counts):
    at = Layout(lax.axis_size("row"), lax.axis_size("col"))
    cap = block_values.shape[2]
    block_len = block_values.shape[-1]
    half = start_vectors.shape[0] // 2
    part = start_vectors.shape[1] // block_len
    per_chunk = 2 * part
    row_index = lax.axis_index("row").astype(jnp.int32)
    col_index = lax.axis_index("col").astype(jnp.int32)
    slow, fast = row_index // at.fast, row_index % at.fast
    chip, core = col_index // 2, col_index % 2
    root = slow // at.group
    is_root = chip == root
    def send(x, pairs):
        return lax.ppermute(x, AXES, pairs)

    slabs = block_values.reshape(cap, block_len, block_len)
    slots = jnp.concatenate([block_places.reshape(2 * cap), block_counts.reshape(1)])
    other_slabs = send(slabs, at.moves_core())

    halves = start_vectors.reshape(2, half, part, block_len).transpose(0, 2, 1, 3)
    scale_rows = jnp.broadcast_to(
        scaling.reshape(1, part, 1, block_len), (2, part, PAD, block_len)
    )
    halves = jnp.concatenate([halves, scale_rows], axis=2)
    packed = [
        jnp.where(core == swap, halves[0], halves[1]) for swap in range(2)
    ]
    pieces = [
        jnp.concatenate([
            packed[swap] if (d, swap) == (0, 0) else send(packed[swap], at.moves_chip(d, swap))
            for swap in range(2)
        ], axis=0)
        for d in range(at.chips)
    ]
    n_kept = at.chips * per_chunk

    def chunk_of(x, e):
        return x[e * per_chunk:(e + 1) * per_chunk]

    def pick(index, choices):
        x = choices[0]
        for d in range(1, len(choices)):
            x = jnp.where(index == d, choices[d], x)
        return x

    row_state = jnp.concatenate([pick(chip ^ e, pieces) for e in range(at.chips)], axis=0)

    row_state, other_slabs = lax.optimization_barrier((row_state, other_slabs))
    both = (send(other_slabs, at.moves_core()), other_slabs)

    def across(x):
        return [send(x, at.moves_slow(d * at.group)) for d in range(1, at.chips)]

    def kept_of(x, got):
        got = [
            jnp.concatenate([chunk_of(y, k ^ d) for k in range(at.chips)], axis=0)
            for d, y in enumerate(got, 1)
        ]
        return pick(chip ^ root, [x] + got)

    row_now, row_scale = row_state[:, :half], row_state[:, half:half + 1]
    row_tile = (row_scale * row_now).astype(jnp.bfloat16)
    row_rest = (row_now - row_tile.astype(jnp.float32) / row_scale).astype(jnp.bfloat16)
    slots, row_tile = lax.optimization_barrier((slots, row_tile))
    tiles_across = across(row_tile)
    own = kept_of(row_tile, tiles_across)
    other_slots = send(slots, at.moves_core())
    n_col = at.rows * per_chunk
    n_row = at.chips * per_chunk
    lists = []
    for which, held in enumerate((slots, other_slots)):
        row_block, col_block = held[:cap], held[cap:2 * cap]
        live = jnp.arange(cap, dtype=jnp.int32) < held[2 * cap]

        def inside(block):
            return ((block // part) ^ core) * part + block % part

        e = row_block // per_chunk
        row_at = e * per_chunk + inside(row_block % per_chunk)
        block = (core ^ which) * (n_col // 2) + col_block
        k = block // per_chunk
        e, f, t = k % at.chips, (k // at.chips) % at.fast, k // (at.chips * at.fast)
        d = slow ^ ((chip ^ e) * at.group + t)
        place = (d % at.group) * at.chips + d // at.group
        col_at = ((fast ^ f) * at.slow + place) * per_chunk + inside(block % per_chunk)
        lists.append((
            row_at, jnp.where(live, col_at, n_col), col_at, jnp.where(live, row_at, n_row)
        ))
    meta = jnp.concatenate(
        [jnp.concatenate([mine, theirs]) for mine, theirs in zip(*lists)]
        + [slots[2 * cap:], other_slots[2 * cap:], jnp.zeros(126, jnp.int32)]
    )

    before = None
    for iterate in range(STEPS):
        if iterate > 0:
            row_tile = pick(
                chip ^ root,
                [own] + [send(own, at.moves_chip(d)) for d in range(1, at.chips)],
            )
        near = [own] + [send(own, at.moves_slow(g)) for g in range(1, at.group)]
        far = [send(own, at.moves_slow(g, 1)) for g in range(at.group)]
        sums = products(
            meta, both, row_tile, (jnp.float32,) + (jnp.bfloat16,) * (2 * at.group - 1),
            n_kept, True,
        )
        if iterate == 0:
            row_rest, far, sums = lax.optimization_barrier((row_rest, far, sums))
            scales_across = across(row_scale)
            scale = kept_of(row_scale, scales_across)
            now = kept_of(row_now, [
                tile.astype(jnp.float32) / factor + rest.astype(jnp.float32)
                for tile, factor, rest in zip(tiles_across, scales_across, across(row_rest))
            ])
        arrived = [
            send(x, at.moves_slow(k % at.group, k // at.group))
            for k, x in enumerate(sums) if k > 0
        ]
        (row_sum,) = products(
            meta, both, jnp.concatenate(near + far, axis=0), (jnp.bfloat16,), n_row, False,
            after=sums[1:],
        )
        from_row = [row_sum] + [
            send(row_sum, at.moves_chip(d)) for d in range(1, at.chips)
        ]
        total = sums[0]
        for x in arrived:
            total = total + x.astype(jnp.float32)
        total, from_row = lax.optimization_barrier((total, from_row))
        for x in from_row:
            total = total + jnp.where(is_root, x, jnp.zeros_like(x)).astype(jnp.float32)
        message = total.astype(jnp.bfloat16)
        last = iterate == STEPS - 1
        if last:
            total, now, scale = chunk_of(total, 0), chunk_of(now, 0), chunk_of(scale, 0)
            before = chunk_of(before, 0)
        applied = total
        for e in range(1, at.chips):
            if last:
                got = send(chunk_of(message, e), at.moves_slow(e * at.group))
            else:
                got = send(message, at.moves_slow(e * at.group))
                got = jnp.concatenate([chunk_of(got, k ^ e) for k in range(at.chips)], axis=0)
            applied = applied + got.astype(jnp.float32)
        mapped = scale * applied - center_shift * now
        if iterate == 0:
            updated = mapped / half_width
        else:
            updated = 2.0 / half_width * mapped - before
        before = now
        now = updated
        if not last:
            own = (scale * now).astype(jnp.bfloat16)
    back = [
        send(now[swap * part:(swap + 1) * part], turned(at.moves_home(swap)))
        for swap in range(2)
    ]
    result = jnp.stack([jnp.where(core == k, back[0], back[1]) for k in range(2)])
    return result.transpose(0, 2, 1, 3).reshape(start_vectors.shape)


def solution(mesh):
    in_specs = (
        P(None, ("row", "col")),
        P(("row", "col")),
        P("row", "col", None, None, None),
        P("row", "col", None, None),
        P("row", "col"),
    )
    out_specs = P(None, ("row", "col"))
    return jax.shard_map(
        per_device, mesh=mesh, in_specs=in_specs, out_specs=out_specs, check_vma=False
    )
```

```python
import functools

import jax
import jax.numpy as jnp
from jax import lax
from jax.experimental import pallas as pl
from jax.experimental.pallas import tpu as pltpu
from jax.sharding import PartitionSpec as P

STEPS = 3

center_shift = 0.5
half_width = 3.0

UNROLL = 32
PACK = 4
VMEM_LIMIT = 24 * 1024 * 1024
AXES = ("row", "col")
PAD = 8


class Layout:
    def __init__(self, rows, cols):
        self.rows, self.cols = rows, cols
        self.chips = cols // 2
        self.fast = 2
        self.slow = rows // 2
        self.group = self.slow // self.chips
        assert self.group * self.chips * self.fast == rows

    def device(self, slow, fast, chip, core):
        return (slow * self.fast + fast) * self.cols + chip * 2 + core

    def home(self, chunk):
        chip, k = chunk // self.rows, chunk % self.rows
        e, f, t = k % self.chips, (k // self.chips) % self.fast, k // (self.chips * self.fast)
        return (chip ^ e) * self.group + t, f, chip

    def moves_home(self, swap, e):
        pairs = []
        for chunk in range(self.rows * self.chips):
            row, chip = chunk // self.chips, chunk % self.chips
            for core in range(2):
                source = row * self.cols + chip * 2 + core
                slow, fast, home_chip = self.home(chunk)
                keeper = slow ^ (e * self.group)
                pairs.append((source, self.device(keeper, fast, home_chip, core ^ swap)))
        return pairs

    def moves_slow(self, d, side=0):
        return [
            (self.device(s, f, c, q), self.device(s ^ d, f ^ side, c, q))
            for s in range(self.slow) for f in range(self.fast)
            for c in range(self.chips) for q in range(2)
        ]

    def moves_chip(self, d, swap=0):
        return [
            (self.device(s, f, c, q), self.device(s, f, c ^ d, q ^ swap))
            for s in range(self.slow) for f in range(self.fast)
            for c in range(self.chips) for q in range(2)
        ]

    def moves_core(self):
        return [(i, i ^ 1) for i in range(self.rows * self.cols)]


def turned(pairs):
    return [(b, a) for a, b in pairs]


def product_kernel(cap, n_out, meta_in, row_in, col_in, *refs):
    slab_refs, refs = refs[:2], refs[2:]
    outs, refs = refs[:n_out], refs[n_out:]
    row_out, outs = outs[0], outs[1:]
    meta_ref, row_vecs, col_vecs, slabs, row_acc, col_acc, slab_sem, in_sem = refs
    vec_count, block_len = row_vecs.shape[1:]

    def slab_copy(which, g):
        span = pl.ds(g * UNROLL, UNROLL)
        to = pl.ds(which * cap + g * UNROLL, UNROLL)
        sem = slab_sem.at[which * (cap // UNROLL) + g]
        return pltpu.make_async_copy(slab_refs[which].at[span], slabs.at[to], sem)

    def start_slab(which, g, carry):
        slab_copy(which, g).start()
        return carry

    meta_copy = pltpu.make_async_copy(meta_in, meta_ref, in_sem.at[0])
    vec_copies = [
        pltpu.make_async_copy(row_in, row_vecs, in_sem.at[1]),
        pltpu.make_async_copy(col_in, col_vecs, in_sem.at[2]),
    ]
    meta_copy.start()
    slab_copy(0, 0).start()
    for copy in vec_copies:
        copy.start()
    slab_copy(1, 0).start()
    row_acc[...] = jnp.zeros_like(row_acc)
    col_acc[...] = jnp.zeros_like(col_acc)
    meta_copy.wait()
    groups = [
        jnp.maximum((meta_ref[8 * cap + which] + (UNROLL - 1)) // UNROLL, 1)
        for which in range(2)
    ]
    for which in range(2):
        lax.fori_loop(1, groups[which], functools.partial(start_slab, which), 0)
    for copy in vec_copies:
        copy.wait()
    zero = jnp.zeros((vec_count, block_len), jnp.bfloat16)

    def spread(v):
        return jnp.concatenate([
            jnp.concatenate([v[0], zero, v[2], zero], axis=0),
            jnp.concatenate([zero, v[1], zero, v[3]], axis=0),
        ], axis=1)

    def body(which, g, carry):
        slab_copy(which, g).wait()
        start = which * cap + g * UNROLL
        products = []
        for u in range(0, UNROLL, PACK):
            at = [start + u + k for k in range(PACK)]
            m = [slabs[s] for s in at]
            tall = [jnp.concatenate(m[:2], axis=0), jnp.concatenate(m[2:], axis=0)]
            wide = [jnp.concatenate(m[:2], axis=1), jnp.concatenate(m[2:], axis=1)]
            transposed = lax.dot_general(
                spread([row_vecs[meta_ref[s]] for s in at]),
                jnp.concatenate(tall, axis=1),
                (((1,), (0,)), ((), ())), preferred_element_type=jnp.float32,
            )
            direct = lax.dot_general(
                spread([col_vecs[meta_ref[4 * cap + s]] for s in at]),
                jnp.concatenate(wide, axis=0),
                (((1,), (1,)), ((), ())), preferred_element_type=jnp.float32,
            )
            products.append((transposed, direct))
        for u in range(UNROLL):
            k = u % PACK
            rows = slice(k * vec_count, (k + 1) * vec_count)
            lanes = slice((k // 2) * block_len, (k // 2 + 1) * block_len)
            transposed, direct = products[u // PACK]
            col_acc[meta_ref[2 * cap + start + u]] += transposed[rows, lanes]
            row_acc[meta_ref[6 * cap + start + u]] += direct[rows, lanes]
        return carry

    for which in range(2):
        lax.fori_loop(0, groups[which], functools.partial(body, which), 0)
    size = row_out.shape[0]
    row_out[...] = row_acc[:size].astype(row_out.dtype)
    for k, out in enumerate(outs):
        out[...] = col_acc[k * size:(k + 1) * size].astype(out.dtype)


def products(meta, slabs, row_vecs, col_vecs):
    cap, block_len, _ = slabs[0].shape
    shape = n_kept, vec_count, _ = row_vecs.shape
    sets = col_vecs.shape[0] // n_kept
    n_out = 1 + sets
    return pl.pallas_call(
        functools.partial(product_kernel, cap, n_out),
        in_specs=[pl.BlockSpec(memory_space=pl.ANY)] * 5,
        out_specs=[pl.BlockSpec(memory_space=pltpu.VMEM)] * n_out,
        out_shape=[
            jax.ShapeDtypeStruct(shape, jnp.float32 if k == 1 else jnp.bfloat16)
            for k in range(n_out)
        ],
        scratch_shapes=[
            pltpu.SMEM(meta.shape, jnp.int32),
            pltpu.VMEM(shape, jnp.bfloat16),
            pltpu.VMEM(col_vecs.shape, jnp.bfloat16),
            pltpu.VMEM((2 * cap, block_len, block_len), jnp.bfloat16),
            pltpu.VMEM((n_kept + 1, vec_count, block_len), jnp.float32),
            pltpu.VMEM((sets * n_kept + 1, vec_count, block_len), jnp.float32),
            pltpu.SemaphoreType.DMA((2 * cap // UNROLL,)),
            pltpu.SemaphoreType.DMA((3,)),
        ],
        compiler_params=pltpu.CompilerParams(vmem_limit_bytes=VMEM_LIMIT),
        cost_estimate=pl.CostEstimate(
            flops=8 * cap * vec_count * block_len * block_len,
            bytes_accessed=4 * vec_count * block_len * n_kept * (1 + sets),
            transcendentals=0,
        ),
        name="both_products",
    )(meta, row_vecs, col_vecs, *slabs)


def per_device(start_vectors, scaling, block_values, block_places, block_counts):
    at = Layout(lax.axis_size("row"), lax.axis_size("col"))
    cap = block_values.shape[2]
    block_len = block_values.shape[-1]
    half = start_vectors.shape[0] // 2
    part = start_vectors.shape[1] // block_len
    per_chunk = 2 * part
    row_index = lax.axis_index("row").astype(jnp.int32)
    col_index = lax.axis_index("col").astype(jnp.int32)
    slow, fast = row_index // at.fast, row_index % at.fast
    chip, core = col_index // 2, col_index % 2
    root = slow // at.group
    is_root = chip == root
    def send(x, pairs):
        return lax.ppermute(x, AXES, pairs)

    slabs = block_values.reshape(cap, block_len, block_len)
    slots = jnp.concatenate([block_places.reshape(2 * cap), block_counts.reshape(1)])
    other_slabs = send(slabs, at.moves_core())

    halves = start_vectors.reshape(2, half, part, block_len).transpose(0, 2, 1, 3)
    scale_rows = jnp.broadcast_to(
        scaling.reshape(1, part, 1, block_len), (2, part, PAD, block_len)
    )
    halves = jnp.concatenate([halves, scale_rows], axis=2)
    packed = [
        jnp.where(core == swap, halves[0], halves[1]) for swap in range(2)
    ]
    pieces = [
        jnp.concatenate([
            packed[swap] if (d, swap) == (0, 0) else send(packed[swap], at.moves_chip(d, swap))
            for swap in range(2)
        ], axis=0)
        for d in range(at.chips)
    ]
    n_kept = at.chips * per_chunk

    def chunk_of(x, e):
        return x[e * per_chunk:(e + 1) * per_chunk]

    def pick(index, choices):
        x = choices[0]
        for d in range(1, len(choices)):
            x = jnp.where(index == d, choices[d], x)
        return x

    row_state = jnp.concatenate([pick(chip ^ e, pieces) for e in range(at.chips)], axis=0)

    row_state, other_slabs = lax.optimization_barrier((row_state, other_slabs))
    both = (send(other_slabs, at.moves_core()), other_slabs)

    def across(x):
        return [send(x, at.moves_slow(d * at.group)) for d in range(1, at.chips)]

    def kept_of(x, got):
        got = [
            jnp.concatenate([chunk_of(y, k ^ d) for k in range(at.chips)], axis=0)
            for d, y in enumerate(got, 1)
        ]
        return pick(chip ^ root, [x] + got)

    row_now, row_scale = row_state[:, :half], row_state[:, half:half + 1]
    row_tile = (row_scale * row_now).astype(jnp.bfloat16)
    tiles_across = across(row_tile)
    row_tile, row_state, slots, *tiles_across = lax.optimization_barrier(
        (row_tile, row_state, slots, *tiles_across)
    )
    own = kept_of(row_tile, tiles_across)
    row_now, row_scale = row_state[:, :half], row_state[:, half:half + 1]
    row_rest = (row_now - row_tile.astype(jnp.float32) / row_scale).astype(jnp.bfloat16)
    scales_across, rests_across = across(row_scale), across(row_rest)

    other_slots = send(slots, at.moves_core())
    n_col = at.rows * per_chunk
    n_row = at.chips * per_chunk
    lists = []
    for which, held in enumerate((slots, other_slots)):
        row_block, col_block = held[:cap], held[cap:2 * cap]
        live = jnp.arange(cap, dtype=jnp.int32) < held[2 * cap]

        def inside(block):
            return ((block // part) ^ core) * part + block % part

        e = row_block // per_chunk
        row_at = e * per_chunk + inside(row_block % per_chunk)
        block = (core ^ which) * (n_col // 2) + col_block
        k = block // per_chunk
        e, f, t = k % at.chips, (k // at.chips) % at.fast, k // (at.chips * at.fast)
        d = slow ^ ((chip ^ e) * at.group + t)
        place = (d % at.group) * at.chips + d // at.group
        col_at = ((fast ^ f) * at.slow + place) * per_chunk + inside(block % per_chunk)
        lists.append((
            row_at, jnp.where(live, col_at, n_col), col_at, jnp.where(live, row_at, n_row)
        ))
    meta = jnp.concatenate(
        [jnp.concatenate([mine, theirs]) for mine, theirs in zip(*lists)]
        + [slots[2 * cap:], other_slots[2 * cap:], jnp.zeros(126, jnp.int32)]
    )

    now = scale = before = None
    for iterate in range(STEPS):
        first, last = iterate == 0, iterate == STEPS - 1
        if not first:
            row_tile = pick(
                chip ^ root,
                [own] + [send(own, at.moves_chip(d)) for d in range(1, at.chips)],
            )
        near = [own] + [send(own, at.moves_slow(g)) for g in range(1, at.group)]
        far = [send(own, at.moves_slow(g, 1)) for g in range(at.group)]
        if last:
            base = 2.0 / half_width * -center_shift * now - before
            base = [
                send(base[swap * part:(swap + 1) * part], turned(at.moves_home(swap, 0)))
                for swap in range(2)
            ]
        row_sum, *sums = products(meta, both, row_tile, jnp.concatenate(near + far, axis=0))
        if first:
            row_sum, scales_across, rests_across = lax.optimization_barrier(
                (row_sum, scales_across, rests_across)
            )
            scale = kept_of(row_scale, scales_across)
            now = kept_of(row_now, [
                tile.astype(jnp.float32) / factor + rest.astype(jnp.float32)
                for tile, factor, rest in zip(tiles_across, scales_across, rests_across)
            ])
        if last:
            row_sum, base = lax.optimization_barrier((row_sum, base))
        total = sums[0]
        for x in [row_sum] + [send(row_sum, at.moves_chip(d)) for d in range(1, at.chips)]:
            total = total + jnp.where(is_root, x, jnp.zeros_like(x)).astype(jnp.float32)
        for k in range(1, len(sums)):
            total = total + send(
                sums[k], at.moves_slow(k % at.group, k // at.group)
            ).astype(jnp.float32)
        message = total.astype(jnp.bfloat16)
        if last:
            break
        applied = total
        for e in range(1, at.chips):
            got = send(message, at.moves_slow(e * at.group))
            got = jnp.concatenate([chunk_of(got, k ^ e) for k in range(at.chips)], axis=0)
            applied = applied + got.astype(jnp.float32)
        mapped = scale * applied - center_shift * now
        if first:
            updated = mapped / half_width
        else:
            updated = 2.0 / half_width * mapped - before
        before = now
        now = updated
        own = (scale * now).astype(jnp.bfloat16)

    own_scale = scaling.reshape(part, 1, block_len)
    parts = []
    for swap in range(2):
        applied = jnp.zeros(base[swap].shape, jnp.float32)
        for e in range(at.chips):
            begin = e * per_chunk + swap * part
            applied = applied + send(
                message[begin:begin + part], turned(at.moves_home(swap, e))
            ).astype(jnp.float32)
        parts.append(2.0 / half_width * (own_scale * applied) + base[swap])
    result = jnp.stack([jnp.where(core == k, parts[0], parts[1]) for k in range(2)])
    return result.transpose(0, 2, 1, 3).reshape(start_vectors.shape)


def solution(mesh):
    in_specs = (
        P(None, ("row", "col")),
        P(("row", "col")),
        P("row", "col", None, None, None),
        P("row", "col", None, None),
        P("row", "col"),
    )
    out_specs = P(None, ("row", "col"))
    return jax.shard_map(
        per_device, mesh=mesh, in_specs=in_specs, out_specs=out_specs, check_vma=False
    )
```

```python
import functools

import jax
import jax.numpy as jnp
from jax import lax
from jax.experimental import pallas as pl
from jax.experimental.pallas import tpu as pltpu
from jax.sharding import PartitionSpec as P

STEPS = 3

center_shift = 0.5
half_width = 3.0

UNROLL = 64
PACK = 4
VMEM_LIMIT = 24 * 1024 * 1024
AXES = ("row", "col")
PAD = 8


class Layout:
    def __init__(self, rows, cols):
        self.rows, self.cols = rows, cols
        self.chips = cols // 2
        self.fast = 2
        self.slow = rows // 2
        self.group = self.slow // self.chips
        assert self.group * self.chips * self.fast == rows

    def device(self, slow, fast, chip, core):
        return (slow * self.fast + fast) * self.cols + chip * 2 + core

    def home(self, chunk):
        chip, k = chunk // self.rows, chunk % self.rows
        e, f, t = k % self.chips, (k // self.chips) % self.fast, k // (self.chips * self.fast)
        return (chip ^ e) * self.group + t, f, chip

    def moves_home(self, swap, e):
        pairs = []
        for chunk in range(self.rows * self.chips):
            row, chip = chunk // self.chips, chunk % self.chips
            for core in range(2):
                source = row * self.cols + chip * 2 + core
                slow, fast, home_chip = self.home(chunk)
                keeper = slow ^ (e * self.group)
                pairs.append((source, self.device(keeper, fast, home_chip, core ^ swap)))
        return pairs

    def moves_slow(self, d, side=0):
        return [
            (self.device(s, f, c, q), self.device(s ^ d, f ^ side, c, q))
            for s in range(self.slow) for f in range(self.fast)
            for c in range(self.chips) for q in range(2)
        ]

    def moves_fast(self):
        return self.moves_slow(0, 1)

    def moves_chip(self, d, swap=0):
        return [
            (self.device(s, f, c, q), self.device(s, f, c ^ d, q ^ swap))
            for s in range(self.slow) for f in range(self.fast)
            for c in range(self.chips) for q in range(2)
        ]

    def moves_core(self):
        return [(i, i ^ 1) for i in range(self.rows * self.cols)]


def turned(pairs):
    return [(b, a) for a, b in pairs]


def product_kernel(transpose, cap, n_out, after, meta_in, vecs_in, *refs):
    slab_refs, refs = refs[:2], refs[2 + after:]
    outs, refs = refs[:n_out], refs[n_out:]
    meta_ref, vecs_ref, slabs, acc, slab_sem, in_sem = refs
    base = 0 if transpose else 4 * cap

    def slab_copy(which, g):
        span = pl.ds(g * UNROLL, UNROLL)
        to = pl.ds(which * cap + g * UNROLL, UNROLL)
        sem = slab_sem.at[which * (cap // UNROLL) + g]
        return pltpu.make_async_copy(slab_refs[which].at[span], slabs.at[to], sem)

    def start_slab(which, g, carry):
        slab_copy(which, g).start()
        return carry

    meta_copy = pltpu.make_async_copy(meta_in, meta_ref, in_sem.at[0])
    vecs_copy = pltpu.make_async_copy(vecs_in, vecs_ref, in_sem.at[1])
    meta_copy.start()
    slab_copy(0, 0).start()
    vecs_copy.start()
    slab_copy(1, 0).start()
    acc[...] = jnp.zeros_like(acc)
    meta_copy.wait()
    groups = [
        jnp.maximum((meta_ref[8 * cap + which] + (UNROLL - 1)) // UNROLL, 1)
        for which in range(2)
    ]
    for which in range(2):
        lax.fori_loop(1, groups[which], functools.partial(start_slab, which), 0)
    vecs_copy.wait()
    vec_count, block_len = vecs_ref.shape[1:]
    zero = jnp.zeros((vec_count, block_len), jnp.bfloat16)

    def body(which, g, carry):
        slab_copy(which, g).wait()
        start = which * cap + g * UNROLL
        products = []
        for u in range(0, UNROLL, PACK):
            v = [vecs_ref[meta_ref[base + start + u + k]] for k in range(PACK)]
            m = [slabs[start + u + k] for k in range(PACK)]
            left = jnp.concatenate([
                jnp.concatenate([v[0], zero, v[2], zero], axis=0),
                jnp.concatenate([zero, v[1], zero, v[3]], axis=0),
            ], axis=1)
            if transpose:
                halves = [jnp.concatenate(m[:2], axis=0), jnp.concatenate(m[2:], axis=0)]
                right, dims = jnp.concatenate(halves, axis=1), (((1,), (0,)), ((), ()))
            else:
                halves = [jnp.concatenate(m[:2], axis=1), jnp.concatenate(m[2:], axis=1)]
                right, dims = jnp.concatenate(halves, axis=0), (((1,), (1,)), ((), ()))
            products.append(
                lax.dot_general(left, right, dims, preferred_element_type=jnp.float32)
            )
        for u in range(UNROLL):
            k = u % PACK
            rows = slice(k * vec_count, (k + 1) * vec_count)
            lanes = slice((k // 2) * block_len, (k // 2 + 1) * block_len)
            acc[meta_ref[base + 2 * cap + start + u]] += products[u // PACK][rows, lanes]
        return carry

    for which in range(2):
        lax.fori_loop(0, groups[which], functools.partial(body, which), 0)
    size = outs[0].shape[0]
    for k, out in enumerate(outs):
        out[...] = acc[k * size:(k + 1) * size].astype(out.dtype)


def products(meta, slabs, vecs, out_dtypes, out_blocks, transpose, after=()):
    cap, block_len, _ = slabs[0].shape
    vec_count = vecs.shape[1]
    total_out = out_blocks * len(out_dtypes)
    anywhere = pl.BlockSpec(memory_space=pl.ANY)
    vmem = pl.BlockSpec(memory_space=pltpu.VMEM)
    return pl.pallas_call(
        functools.partial(product_kernel, transpose, cap, len(out_dtypes), len(after)),
        in_specs=[anywhere] * (4 + len(after)),
        out_specs=[vmem] * len(out_dtypes),
        out_shape=[
            jax.ShapeDtypeStruct((out_blocks, vec_count, block_len), dtype)
            for dtype in out_dtypes
        ],
        scratch_shapes=[
            pltpu.SMEM(meta.shape, jnp.int32),
            pltpu.VMEM(vecs.shape, jnp.bfloat16),
            pltpu.VMEM((2 * cap, block_len, block_len), jnp.bfloat16),
            pltpu.VMEM((total_out + 1, vec_count, block_len), jnp.float32),
            pltpu.SemaphoreType.DMA((2 * cap // UNROLL,)),
            pltpu.SemaphoreType.DMA((2,)),
        ],
        compiler_params=pltpu.CompilerParams(vmem_limit_bytes=VMEM_LIMIT),
        cost_estimate=pl.CostEstimate(
            flops=4 * cap * vec_count * block_len * block_len,
            bytes_accessed=2 * vec_count * block_len * (vecs.shape[0] + total_out),
            transcendentals=0,
        ),
        name="transposed" if transpose else "direct",
    )(meta, vecs, *slabs, *after)


def per_device(start_vectors, scaling, block_values, block_places, block_counts):
    at = Layout(lax.axis_size("row"), lax.axis_size("col"))
    cap = block_values.shape[2]
    block_len = block_values.shape[-1]
    half = start_vectors.shape[0] // 2
    part = start_vectors.shape[1] // block_len
    per_chunk = 2 * part
    row_index = lax.axis_index("row").astype(jnp.int32)
    col_index = lax.axis_index("col").astype(jnp.int32)
    slow, fast = row_index // at.fast, row_index % at.fast
    chip, core = col_index // 2, col_index % 2
    root = slow // at.group
    is_root = chip == root
    def send(x, pairs):
        return lax.ppermute(x, AXES, pairs)

    slabs = block_values.reshape(cap, block_len, block_len)
    slots = jnp.concatenate([block_places.reshape(2 * cap), block_counts.reshape(1)])
    other_slabs = send(slabs, at.moves_core())

    halves = start_vectors.reshape(2, half, part, block_len).transpose(0, 2, 1, 3)
    scale_rows = jnp.broadcast_to(
        scaling.reshape(1, part, 1, block_len), (2, part, PAD, block_len)
    )
    halves = jnp.concatenate([halves, scale_rows], axis=2)
    packed = [
        jnp.where(core == swap, halves[0], halves[1]) for swap in range(2)
    ]
    pieces = [
        jnp.concatenate([
            packed[swap] if (d, swap) == (0, 0) else send(packed[swap], at.moves_chip(d, swap))
            for swap in range(2)
        ], axis=0)
        for d in range(at.chips)
    ]
    n_kept = at.chips * per_chunk

    def chunk_of(x, e):
        return x[e * per_chunk:(e + 1) * per_chunk]

    def pick(index, choices):
        x = choices[0]
        for d in range(1, len(choices)):
            x = jnp.where(index == d, choices[d], x)
        return x

    row_state = jnp.concatenate([pick(chip ^ e, pieces) for e in range(at.chips)], axis=0)

    row_state, other_slabs = lax.optimization_barrier((row_state, other_slabs))
    both = (send(other_slabs, at.moves_core()), other_slabs)

    def across(x):
        return [send(x, at.moves_slow(d * at.group)) for d in range(1, at.chips)]

    def kept_of(x, got):
        got = [
            jnp.concatenate([chunk_of(y, k ^ d) for k in range(at.chips)], axis=0)
            for d, y in enumerate(got, 1)
        ]
        return pick(chip ^ root, [x] + got)

    row_now, row_scale = row_state[:, :half], row_state[:, half:half + 1]
    row_tile = (row_scale * row_now).astype(jnp.bfloat16)
    tiles_across = across(row_tile)
    row_tile, row_state, slots, *tiles_across = lax.optimization_barrier(
        (row_tile, row_state, slots, *tiles_across)
    )
    own = kept_of(row_tile, tiles_across)
    row_now, row_scale = row_state[:, :half], row_state[:, half:half + 1]
    row_rest = (row_now - row_tile.astype(jnp.float32) / row_scale).astype(jnp.bfloat16)
    scales_across = across(row_scale)

    other_slots = send(slots, at.moves_core())
    n_col = at.rows * per_chunk
    n_row = at.chips * per_chunk
    lists = []
    for which, held in enumerate((slots, other_slots)):
        row_block, col_block = held[:cap], held[cap:2 * cap]
        live = jnp.arange(cap, dtype=jnp.int32) < held[2 * cap]

        def inside(block):
            return ((block // part) ^ core) * part + block % part

        e = row_block // per_chunk
        row_at = e * per_chunk + inside(row_block % per_chunk)
        block = (core ^ which) * (n_col // 2) + col_block
        k = block // per_chunk
        e, f, t = k % at.chips, (k // at.chips) % at.fast, k // (at.chips * at.fast)
        d = slow ^ ((chip ^ e) * at.group + t)
        place = (d % at.group) * at.chips + d // at.group
        col_at = ((fast ^ f) * at.slow + place) * per_chunk + inside(block % per_chunk)
        lists.append((
            row_at, jnp.where(live, col_at, n_col), col_at, jnp.where(live, row_at, n_row)
        ))
    meta = jnp.concatenate(
        [jnp.concatenate([mine, theirs]) for mine, theirs in zip(*lists)]
        + [slots[2 * cap:], other_slots[2 * cap:], jnp.zeros(126, jnp.int32)]
    )

    now = scale = before = None
    for iterate in range(STEPS):
        first, last = iterate == 0, iterate == STEPS - 1
        if not first:
            row_tile = pick(
                chip ^ root,
                [own] + [send(own, at.moves_chip(d)) for d in range(1, at.chips)],
            )
        near = [own] + [send(own, at.moves_slow(g)) for g in range(1, at.group)]
        far = [send(x, at.moves_fast()) for x in near]
        sums = products(
            meta, both, row_tile,
            (jnp.float32,) * at.group + (jnp.bfloat16,) * at.group, n_kept, True,
        )
        if first:
            row_rest, far, sums = lax.optimization_barrier((row_rest, far, sums))
        near_sums, far_sums = sums[:at.group], sums[at.group:]
        if last:
            base = 2.0 / half_width * -center_shift * now - before
            base = [
                send(base[swap * part:(swap + 1) * part], turned(at.moves_home(swap, 0)))
                for swap in range(2)
            ]
        from_fast = [send(x, at.moves_fast()) for x in far_sums[::-1]][::-1]
        (row_sum,) = products(
            meta, both, jnp.concatenate(near + far, axis=0), (jnp.bfloat16,), n_row, False,
            after=far_sums,
        )
        if last:
            row_sum, base = lax.optimization_barrier((row_sum, base))
        if first:
            scale = kept_of(row_scale, scales_across)
            now = kept_of(row_now, [
                tile.astype(jnp.float32) / factor + rest.astype(jnp.float32)
                for tile, factor, rest in zip(tiles_across, scales_across, across(row_rest))
            ])
        from_row = [row_sum] + [
            send(row_sum, at.moves_chip(d)) for d in range(1, at.chips)
        ]
        sums = [x + y.astype(jnp.float32) for x, y in zip(near_sums, from_fast)]
        total = sums[0]
        for g in range(1, at.group):
            total = total + send(
                sums[g].astype(jnp.bfloat16), at.moves_slow(g)
            ).astype(jnp.float32)
        for x in from_row:
            total = total + jnp.where(is_root, x, jnp.zeros_like(x)).astype(jnp.float32)
        message = total.astype(jnp.bfloat16)
        if last:
            break
        applied = total
        for e in range(1, at.chips):
            got = send(message, at.moves_slow(e * at.group))
            got = jnp.concatenate([chunk_of(got, k ^ e) for k in range(at.chips)], axis=0)
            applied = applied + got.astype(jnp.float32)
        mapped = scale * applied - center_shift * now
        if first:
            updated = mapped / half_width
        else:
            updated = 2.0 / half_width * mapped - before
        before = now
        now = updated
        own = (scale * now).astype(jnp.bfloat16)

    own_scale = scaling.reshape(part, 1, block_len)
    parts = []
    for swap in range(2):
        applied = jnp.zeros(base[swap].shape, jnp.float32)
        for e in range(at.chips):
            begin = e * per_chunk + swap * part
            applied = applied + send(
                message[begin:begin + part], turned(at.moves_home(swap, e))
            ).astype(jnp.float32)
        parts.append(2.0 / half_width * (own_scale * applied) + base[swap])
    result = jnp.stack([jnp.where(core == k, parts[0], parts[1]) for k in range(2)])
    return result.transpose(0, 2, 1, 3).reshape(start_vectors.shape)


def solution(mesh):
    in_specs = (
        P(None, ("row", "col")),
        P(("row", "col")),
        P("row", "col", None, None, None),
        P("row", "col", None, None),
        P("row", "col"),
    )
    out_specs = P(None, ("row", "col"))
    return jax.shard_map(
        per_device, mesh=mesh, in_specs=in_specs, out_specs=out_specs, check_vma=False
    )
```

```python
import functools

import jax
import jax.numpy as jnp
from jax import lax
from jax.experimental import pallas as pl
from jax.experimental.pallas import tpu as pltpu
from jax.sharding import PartitionSpec as P

STEPS = 3

center_shift = 0.5
half_width = 3.0

UNROLL = 64
PACK = 4
VMEM_LIMIT = 24 * 1024 * 1024
AXES = ("row", "col")
PAD = 8


class Layout:
    def __init__(self, rows, cols):
        self.rows, self.cols = rows, cols
        self.chips = cols // 2
        self.fast = 2
        self.slow = rows // 2
        self.group = self.slow // self.chips
        assert self.group * self.chips * self.fast == rows

    def device(self, slow, fast, chip, core):
        return (slow * self.fast + fast) * self.cols + chip * 2 + core

    def home(self, chunk):
        chip, k = chunk // self.rows, chunk % self.rows
        e, f, t = k % self.chips, (k // self.chips) % self.fast, k // (self.chips * self.fast)
        return (chip ^ e) * self.group + t, f, chip

    def moves_home(self, swap):
        pairs = []
        for chunk in range(self.rows * self.chips):
            row, chip = chunk // self.chips, chunk % self.chips
            for core in range(2):
                source = row * self.cols + chip * 2 + core
                pairs.append((source, self.device(*self.home(chunk), core ^ swap)))
        return pairs

    def moves_slow(self, d, side=0):
        return [
            (self.device(s, f, c, q), self.device(s ^ d, f ^ side, c, q))
            for s in range(self.slow) for f in range(self.fast)
            for c in range(self.chips) for q in range(2)
        ]

    def moves_fast(self):
        return self.moves_slow(0, 1)

    def moves_chip(self, d, swap=0):
        return [
            (self.device(s, f, c, q), self.device(s, f, c ^ d, q ^ swap))
            for s in range(self.slow) for f in range(self.fast)
            for c in range(self.chips) for q in range(2)
        ]

    def moves_core(self):
        return [(i, i ^ 1) for i in range(self.rows * self.cols)]


def turned(pairs):
    return [(b, a) for a, b in pairs]


def product_kernel(transpose, cap, n_out, after, meta_in, vecs_in, *refs):
    slab_refs, refs = refs[:2], refs[2 + after:]
    outs, refs = refs[:n_out], refs[n_out:]
    meta_ref, vecs_ref, slabs, acc, slab_sem, in_sem = refs
    base = 0 if transpose else 4 * cap

    def slab_copy(which, g):
        span = pl.ds(g * UNROLL, UNROLL)
        to = pl.ds(which * cap + g * UNROLL, UNROLL)
        sem = slab_sem.at[which * (cap // UNROLL) + g]
        return pltpu.make_async_copy(slab_refs[which].at[span], slabs.at[to], sem)

    def start_slab(which, g, carry):
        slab_copy(which, g).start()
        return carry

    meta_copy = pltpu.make_async_copy(meta_in, meta_ref, in_sem.at[0])
    vecs_copy = pltpu.make_async_copy(vecs_in, vecs_ref, in_sem.at[1])
    meta_copy.start()
    slab_copy(0, 0).start()
    vecs_copy.start()
    slab_copy(1, 0).start()
    acc[...] = jnp.zeros_like(acc)
    meta_copy.wait()
    groups = [
        jnp.maximum((meta_ref[8 * cap + which] + (UNROLL - 1)) // UNROLL, 1)
        for which in range(2)
    ]
    for which in range(2):
        lax.fori_loop(1, groups[which], functools.partial(start_slab, which), 0)
    vecs_copy.wait()
    vec_count, block_len = vecs_ref.shape[1:]
    zero = jnp.zeros((vec_count, block_len), jnp.bfloat16)

    def body(which, g, carry):
        slab_copy(which, g).wait()
        start = which * cap + g * UNROLL
        products = []
        for u in range(0, UNROLL, PACK):
            v = [vecs_ref[meta_ref[base + start + u + k]] for k in range(PACK)]
            m = [slabs[start + u + k] for k in range(PACK)]
            left = jnp.concatenate([
                jnp.concatenate([v[0], zero, v[2], zero], axis=0),
                jnp.concatenate([zero, v[1], zero, v[3]], axis=0),
            ], axis=1)
            if transpose:
                halves = [jnp.concatenate(m[:2], axis=0), jnp.concatenate(m[2:], axis=0)]
                right, dims = jnp.concatenate(halves, axis=1), (((1,), (0,)), ((), ()))
            else:
                halves = [jnp.concatenate(m[:2], axis=1), jnp.concatenate(m[2:], axis=1)]
                right, dims = jnp.concatenate(halves, axis=0), (((1,), (1,)), ((), ()))
            products.append(
                lax.dot_general(left, right, dims, preferred_element_type=jnp.float32)
            )
        for u in range(UNROLL):
            k = u % PACK
            rows = slice(k * vec_count, (k + 1) * vec_count)
            lanes = slice((k // 2) * block_len, (k // 2 + 1) * block_len)
            acc[meta_ref[base + 2 * cap + start + u]] += products[u // PACK][rows, lanes]
        return carry

    for which in range(2):
        lax.fori_loop(0, groups[which], functools.partial(body, which), 0)
    size = outs[0].shape[0]
    for k, out in enumerate(outs):
        out[...] = acc[k * size:(k + 1) * size].astype(out.dtype)


def products(meta, slabs, vecs, out_dtypes, out_blocks, transpose, after=()):
    cap, block_len, _ = slabs[0].shape
    vec_count = vecs.shape[1]
    total_out = out_blocks * len(out_dtypes)
    anywhere = pl.BlockSpec(memory_space=pl.ANY)
    vmem = pl.BlockSpec(memory_space=pltpu.VMEM)
    return pl.pallas_call(
        functools.partial(product_kernel, transpose, cap, len(out_dtypes), len(after)),
        in_specs=[anywhere] * (4 + len(after)),
        out_specs=[vmem] * len(out_dtypes),
        out_shape=[
            jax.ShapeDtypeStruct((out_blocks, vec_count, block_len), dtype)
            for dtype in out_dtypes
        ],
        scratch_shapes=[
            pltpu.SMEM(meta.shape, jnp.int32),
            pltpu.VMEM(vecs.shape, jnp.bfloat16),
            pltpu.VMEM((2 * cap, block_len, block_len), jnp.bfloat16),
            pltpu.VMEM((total_out + 1, vec_count, block_len), jnp.float32),
            pltpu.SemaphoreType.DMA((2 * cap // UNROLL,)),
            pltpu.SemaphoreType.DMA((2,)),
        ],
        compiler_params=pltpu.CompilerParams(vmem_limit_bytes=VMEM_LIMIT),
        cost_estimate=pl.CostEstimate(
            flops=4 * cap * vec_count * block_len * block_len,
            bytes_accessed=2 * vec_count * block_len * (vecs.shape[0] + total_out),
            transcendentals=0,
        ),
        name="transposed" if transpose else "direct",
    )(meta, vecs, *slabs, *after)


def per_device(start_vectors, scaling, block_values, block_places, block_counts):
    at = Layout(lax.axis_size("row"), lax.axis_size("col"))
    cap = block_values.shape[2]
    block_len = block_values.shape[-1]
    half = start_vectors.shape[0] // 2
    part = start_vectors.shape[1] // block_len
    per_chunk = 2 * part
    row_index = lax.axis_index("row").astype(jnp.int32)
    col_index = lax.axis_index("col").astype(jnp.int32)
    slow, fast = row_index // at.fast, row_index % at.fast
    chip, core = col_index // 2, col_index % 2
    root = slow // at.group
    is_root = chip == root
    def send(x, pairs):
        return lax.ppermute(x, AXES, pairs)

    slabs = block_values.reshape(cap, block_len, block_len)
    slots = jnp.concatenate([block_places.reshape(2 * cap), block_counts.reshape(1)])
    other_slabs = send(slabs, at.moves_core())

    halves = start_vectors.reshape(2, half, part, block_len).transpose(0, 2, 1, 3)
    scale_rows = jnp.broadcast_to(
        scaling.reshape(1, part, 1, block_len), (2, part, PAD, block_len)
    )
    halves = jnp.concatenate([halves, scale_rows], axis=2)
    packed = [
        jnp.where(core == swap, halves[0], halves[1]) for swap in range(2)
    ]
    pieces = [
        jnp.concatenate([
            packed[swap] if (d, swap) == (0, 0) else send(packed[swap], at.moves_chip(d, swap))
            for swap in range(2)
        ], axis=0)
        for d in range(at.chips)
    ]
    n_kept = at.chips * per_chunk

    def chunk_of(x, e):
        return x[e * per_chunk:(e + 1) * per_chunk]

    def pick(index, choices):
        x = choices[0]
        for d in range(1, len(choices)):
            x = jnp.where(index == d, choices[d], x)
        return x

    row_state = jnp.concatenate([pick(chip ^ e, pieces) for e in range(at.chips)], axis=0)

    other_slots = send(slots, at.moves_core())
    n_col = at.rows * per_chunk
    n_row = at.chips * per_chunk
    lists = []
    for which, held in enumerate((slots, other_slots)):
        row_block, col_block = held[:cap], held[cap:2 * cap]
        live = jnp.arange(cap, dtype=jnp.int32) < held[2 * cap]

        def inside(block):
            return ((block // part) ^ core) * part + block % part

        e = row_block // per_chunk
        row_at = e * per_chunk + inside(row_block % per_chunk)
        block = (core ^ which) * (n_col // 2) + col_block
        k = block // per_chunk
        e, f, t = k % at.chips, (k // at.chips) % at.fast, k // (at.chips * at.fast)
        d = slow ^ ((chip ^ e) * at.group + t)
        place = (d % at.group) * at.chips + d // at.group
        col_at = ((fast ^ f) * at.slow + place) * per_chunk + inside(block % per_chunk)
        lists.append((
            row_at, jnp.where(live, col_at, n_col), col_at, jnp.where(live, row_at, n_row)
        ))
    meta = jnp.concatenate(
        [jnp.concatenate([mine, theirs]) for mine, theirs in zip(*lists)]
        + [slots[2 * cap:], other_slots[2 * cap:], jnp.zeros(126, jnp.int32)]
    )

    row_state, meta, other_slabs = lax.optimization_barrier((row_state, meta, other_slabs))
    both = (send(other_slabs, at.moves_core()), other_slabs)

    def across(x):
        return [send(x, at.moves_slow(d * at.group)) for d in range(1, at.chips)]

    def kept_of(x, got):
        got = [
            jnp.concatenate([chunk_of(y, k ^ d) for k in range(at.chips)], axis=0)
            for d, y in enumerate(got, 1)
        ]
        return pick(chip ^ root, [x] + got)

    row_now, row_scale = row_state[:, :half], row_state[:, half:half + 1]
    row_tile = (row_scale * row_now).astype(jnp.bfloat16)
    tiles_across = across(row_tile)
    row_tile, row_state = lax.optimization_barrier((row_tile, row_state))
    row_now, row_scale = row_state[:, :half], row_state[:, half:half + 1]
    row_rest = (row_now - row_tile.astype(jnp.float32) / row_scale).astype(jnp.bfloat16)

    before = None
    for iterate in range(STEPS):
        first, last = iterate == 0, iterate == STEPS - 1
        if not first:
            row_tile = pick(
                chip ^ root,
                [own] + [send(own, at.moves_chip(d)) for d in range(1, at.chips)],
            )
        dtypes = (jnp.float32,) * at.group + (jnp.bfloat16,) * at.group
        if first:
            sums = products(meta, (slabs, other_slabs), row_tile, dtypes, n_kept, True)
            sums, tiles_across, row_scale = lax.optimization_barrier(
                (sums, tiles_across, row_scale)
            )
            own = kept_of(row_tile, tiles_across)
            scales_across = across(row_scale)
        near = [own] + [send(own, at.moves_slow(g)) for g in range(1, at.group)]
        far = [send(own, at.moves_slow(g, 1)) for g in range(at.group)]
        if first:
            sums, near = lax.optimization_barrier((sums, near))
        else:
            sums = products(meta, both, row_tile, dtypes, n_kept, True)
        near_sums, far_sums = sums[:at.group], sums[at.group:]
        from_fast = [send(x, at.moves_fast()) for x in far_sums[::-1]][::-1]
        if first:
            row_rest, far = lax.optimization_barrier((row_rest, far))
            scale = kept_of(row_scale, scales_across)
            now = kept_of(row_now, [
                tile.astype(jnp.float32) / factor + rest.astype(jnp.float32)
                for tile, factor, rest in zip(tiles_across, scales_across, across(row_rest))
            ])
        (row_sum,) = products(
            meta, both, jnp.concatenate(near + far, axis=0), (jnp.bfloat16,), n_row, False,
            after=far_sums,
        )
        if first:
            from_fast[-1], row_sum = lax.optimization_barrier((from_fast[-1], row_sum))
        from_row = [row_sum] + [
            send(row_sum, at.moves_chip(d)) for d in range(1, at.chips)
        ]
        sums = [x + y.astype(jnp.float32) for x, y in zip(near_sums, from_fast)]
        total = sums[0]
        for g in range(1, at.group):
            total = total + send(
                sums[g].astype(jnp.bfloat16), at.moves_slow(g)
            ).astype(jnp.float32)
        for x in from_row:
            total = total + jnp.where(is_root, x, jnp.zeros_like(x)).astype(jnp.float32)
        message = total.astype(jnp.bfloat16)
        if last:
            total, now, scale = chunk_of(total, 0), chunk_of(now, 0), chunk_of(scale, 0)
            before = chunk_of(before, 0)
        applied = total
        for e in range(1, at.chips):
            if last:
                got = send(chunk_of(message, e), at.moves_slow(e * at.group))
            else:
                got = send(message, at.moves_slow(e * at.group))
                got = jnp.concatenate([chunk_of(got, k ^ e) for k in range(at.chips)], axis=0)
            applied = applied + got.astype(jnp.float32)
        mapped = scale * applied - center_shift * now
        if first:
            updated = mapped / half_width
        else:
            updated = 2.0 / half_width * mapped - before
        before = now
        now = updated
        if not last:
            own = (scale * now).astype(jnp.bfloat16)
    back = [
        send(now[swap * part:(swap + 1) * part], turned(at.moves_home(swap)))
        for swap in range(2)
    ]
    result = jnp.stack([jnp.where(core == k, back[0], back[1]) for k in range(2)])
    return result.transpose(0, 2, 1, 3).reshape(start_vectors.shape)


def solution(mesh):
    in_specs = (
        P(None, ("row", "col")),
        P(("row", "col")),
        P("row", "col", None, None, None),
        P("row", "col", None, None),
        P("row", "col"),
    )
    out_specs = P(None, ("row", "col"))
    return jax.shard_map(
        per_device, mesh=mesh, in_specs=in_specs, out_specs=out_specs, check_vma=False
    )
```

```python
import functools

import jax
import jax.numpy as jnp
from jax import lax
from jax.experimental import pallas as pl
from jax.experimental.pallas import tpu as pltpu
from jax.sharding import PartitionSpec as P

STEPS = 3

center_shift = 0.5
half_width = 3.0

UNROLL = 64
PACK = 4
VMEM_LIMIT = 16 * 1024 * 1024
AXES = ("row", "col")
PAD = 8


class Layout:
    def __init__(self, rows, cols):
        self.rows, self.cols = rows, cols
        self.chips = cols // 2
        self.fast = 2
        self.slow = rows // 2
        self.group = self.slow // self.chips
        assert self.group * self.chips * self.fast == rows

    def device(self, slow, fast, chip, core):
        return (slow * self.fast + fast) * self.cols + chip * 2 + core

    def home(self, chunk):
        chip, k = chunk // self.rows, chunk % self.rows
        e, f, t = k % self.chips, (k // self.chips) % self.fast, k // (self.chips * self.fast)
        return (chip ^ e) * self.group + t, f, chip

    def moves_home(self, swap):
        pairs = []
        for chunk in range(self.rows * self.chips):
            row, chip = chunk // self.chips, chunk % self.chips
            for core in range(2):
                source = row * self.cols + chip * 2 + core
                pairs.append((source, self.device(*self.home(chunk), core ^ swap)))
        return pairs

    def moves_slow(self, d, side=0):
        return [
            (self.device(s, f, c, q), self.device(s ^ d, f ^ side, c, q))
            for s in range(self.slow) for f in range(self.fast)
            for c in range(self.chips) for q in range(2)
        ]

    def moves_fast(self):
        return self.moves_slow(0, 1)

    def moves_chip(self, d, swap=0):
        return [
            (self.device(s, f, c, q), self.device(s, f, c ^ d, q ^ swap))
            for s in range(self.slow) for f in range(self.fast)
            for c in range(self.chips) for q in range(2)
        ]

    def moves_core(self):
        return [(i, i ^ 1) for i in range(self.rows * self.cols)]


def turned(pairs):
    return [(b, a) for a, b in pairs]


def live_groups(meta_ref, cap, which):
    return jnp.maximum((meta_ref[8 * cap + which] + (UNROLL - 1)) // UNROLL, 1)


def stage_kernel(cap, meta_ref, mine_ref, other_ref, out_ref, sem):
    def copy(which, g):
        ref = (mine_ref, other_ref)[which]
        to = pl.ds(which * cap + g * UNROLL, UNROLL)
        return pltpu.make_async_copy(
            ref.at[pl.ds(g * UNROLL, UNROLL)], out_ref.at[to],
            sem.at[which * (cap // UNROLL) + g],
        )

    def start(which, g, carry):
        copy(which, g).start()
        return carry

    def wait(which, g, carry):
        copy(which, g).wait()
        return carry

    for step in (start, wait):
        for which in range(2):
            lax.fori_loop(
                0, live_groups(meta_ref, cap, which), functools.partial(step, which), 0
            )


def stage(meta, mine, other):
    cap = mine.shape[0]
    anywhere = pl.BlockSpec(memory_space=pl.ANY)
    return pl.pallas_call(
        functools.partial(stage_kernel, cap),
        in_specs=[pl.BlockSpec(memory_space=pltpu.SMEM), anywhere, anywhere],
        out_specs=anywhere,
        out_shape=jax.ShapeDtypeStruct((2 * cap,) + mine.shape[1:], mine.dtype),
        scratch_shapes=[pltpu.SemaphoreType.DMA((2 * cap // UNROLL,))],
        name="stage",
    )(meta, mine, other)


def product_kernel(transpose, cap, n_out, after, meta_in, vecs_in, slabs_in, *refs):
    refs = refs[after:]
    outs, refs = refs[:n_out], refs[n_out:]
    meta_ref, vecs_ref, slabs, acc, slab_sem, in_sem = refs
    base = 0 if transpose else 4 * cap

    def slab_copy(which, g):
        span = pl.ds(which * cap + g * UNROLL, UNROLL)
        sem = slab_sem.at[which * (cap // UNROLL) + g]
        return pltpu.make_async_copy(slabs_in.at[span], slabs.at[span], sem)

    def start_slab(which, g, carry):
        slab_copy(which, g).start()
        return carry

    meta_copy = pltpu.make_async_copy(meta_in, meta_ref, in_sem.at[0])
    vecs_copy = pltpu.make_async_copy(vecs_in, vecs_ref, in_sem.at[1])
    meta_copy.start()
    slab_copy(0, 0).start()
    vecs_copy.start()
    slab_copy(1, 0).start()
    acc[...] = jnp.zeros_like(acc)
    meta_copy.wait()
    groups = [live_groups(meta_ref, cap, which) for which in range(2)]
    for which in range(2):
        lax.fori_loop(1, groups[which], functools.partial(start_slab, which), 0)
    vecs_copy.wait()
    vec_count, block_len = vecs_ref.shape[1:]
    zero = jnp.zeros((vec_count, block_len), jnp.bfloat16)

    def body(which, g, carry):
        slab_copy(which, g).wait()
        start = which * cap + g * UNROLL
        products = []
        for u in range(0, UNROLL, PACK):
            v = [vecs_ref[meta_ref[base + start + u + k]] for k in range(PACK)]
            m = [slabs[start + u + k] for k in range(PACK)]
            left = jnp.concatenate([
                jnp.concatenate([v[0], zero, v[2], zero], axis=0),
                jnp.concatenate([zero, v[1], zero, v[3]], axis=0),
            ], axis=1)
            if transpose:
                halves = [jnp.concatenate(m[:2], axis=0), jnp.concatenate(m[2:], axis=0)]
                right, dims = jnp.concatenate(halves, axis=1), (((1,), (0,)), ((), ()))
            else:
                halves = [jnp.concatenate(m[:2], axis=1), jnp.concatenate(m[2:], axis=1)]
                right, dims = jnp.concatenate(halves, axis=0), (((1,), (1,)), ((), ()))
            products.append(
                lax.dot_general(left, right, dims, preferred_element_type=jnp.float32)
            )
        for u in range(UNROLL):
            k = u % PACK
            rows = slice(k * vec_count, (k + 1) * vec_count)
            lanes = slice((k // 2) * block_len, (k // 2 + 1) * block_len)
            acc[meta_ref[base + 2 * cap + start + u]] += products[u // PACK][rows, lanes]
        return carry

    for which in range(2):
        lax.fori_loop(0, groups[which], functools.partial(body, which), 0)
    size = outs[0].shape[0]
    for k, out in enumerate(outs):
        out[...] = acc[k * size:(k + 1) * size].astype(out.dtype)


def products(meta, slabs, vecs, out_dtypes, out_blocks, transpose, after=()):
    slots, block_len, _ = slabs.shape
    cap = slots // 2
    vec_count = vecs.shape[1]
    total_out = out_blocks * len(out_dtypes)
    anywhere = pl.BlockSpec(memory_space=pl.ANY)
    vmem = pl.BlockSpec(memory_space=pltpu.VMEM)
    return pl.pallas_call(
        functools.partial(product_kernel, transpose, cap, len(out_dtypes), len(after)),
        in_specs=[anywhere] * (3 + len(after)),
        out_specs=[vmem] * len(out_dtypes),
        out_shape=[
            jax.ShapeDtypeStruct((out_blocks, vec_count, block_len), dtype)
            for dtype in out_dtypes
        ],
        scratch_shapes=[
            pltpu.SMEM(meta.shape, jnp.int32),
            pltpu.VMEM(vecs.shape, jnp.bfloat16),
            pltpu.VMEM(slabs.shape, jnp.bfloat16),
            pltpu.VMEM((total_out + 1, vec_count, block_len), jnp.float32),
            pltpu.SemaphoreType.DMA((2 * cap // UNROLL,)),
            pltpu.SemaphoreType.DMA((2,)),
        ],
        compiler_params=pltpu.CompilerParams(vmem_limit_bytes=VMEM_LIMIT),
        cost_estimate=pl.CostEstimate(
            flops=4 * cap * vec_count * block_len * block_len,
            bytes_accessed=2 * vec_count * block_len * (vecs.shape[0] + total_out),
            transcendentals=0,
        ),
        name="transposed" if transpose else "direct",
    )(meta, vecs, slabs, *after)


def per_device(start_vectors, scaling, block_values, block_places, block_counts):
    at = Layout(lax.axis_size("row"), lax.axis_size("col"))
    cap = block_values.shape[2]
    block_len = block_values.shape[-1]
    half = start_vectors.shape[0] // 2
    part = start_vectors.shape[1] // block_len
    per_chunk = 2 * part
    row_index = lax.axis_index("row").astype(jnp.int32)
    col_index = lax.axis_index("col").astype(jnp.int32)
    slow, fast = row_index // at.fast, row_index % at.fast
    chip, core = col_index // 2, col_index % 2
    root = slow // at.group
    is_root = chip == root
    def send(x, pairs):
        return lax.ppermute(x, AXES, pairs)

    slabs = block_values.reshape(cap, block_len, block_len)
    slots = jnp.concatenate([block_places.reshape(2 * cap), block_counts.reshape(1)])
    other_slabs = send(slabs, at.moves_core())

    halves = start_vectors.reshape(2, half, part, block_len).transpose(0, 2, 1, 3)
    scale_rows = jnp.broadcast_to(
        scaling.reshape(1, part, 1, block_len), (2, part, PAD, block_len)
    )
    halves = jnp.concatenate([halves, scale_rows], axis=2)
    packed = [
        jnp.where(core == swap, halves[0], halves[1]) for swap in range(2)
    ]
    pieces = [
        jnp.concatenate([
            packed[swap] if (d, swap) == (0, 0) else send(packed[swap], at.moves_chip(d, swap))
            for swap in range(2)
        ], axis=0)
        for d in range(at.chips)
    ]
    n_kept = at.chips * per_chunk

    def chunk_of(x, e):
        return x[e * per_chunk:(e + 1) * per_chunk]

    def pick(index, choices):
        x = choices[0]
        for d in range(1, len(choices)):
            x = jnp.where(index == d, choices[d], x)
        return x

    row_state = jnp.concatenate([pick(chip ^ e, pieces) for e in range(at.chips)], axis=0)

    other_slots = send(slots, at.moves_core())
    n_col = at.rows * per_chunk
    n_row = at.chips * per_chunk
    lists = []
    for which, held in enumerate((slots, other_slots)):
        row_block, col_block = held[:cap], held[cap:2 * cap]
        live = jnp.arange(cap, dtype=jnp.int32) < held[2 * cap]

        def inside(block):
            return ((block // part) ^ core) * part + block % part

        e = row_block // per_chunk
        row_at = e * per_chunk + inside(row_block % per_chunk)
        block = (core ^ which) * (n_col // 2) + col_block
        k = block // per_chunk
        e, f, t = k % at.chips, (k // at.chips) % at.fast, k // (at.chips * at.fast)
        d = slow ^ ((chip ^ e) * at.group + t)
        place = (d % at.group) * at.chips + d // at.group
        col_at = ((fast ^ f) * at.slow + place) * per_chunk + inside(block % per_chunk)
        lists.append((
            row_at, jnp.where(live, col_at, n_col), col_at, jnp.where(live, row_at, n_row)
        ))
    meta = jnp.concatenate(
        [jnp.concatenate([mine, theirs]) for mine, theirs in zip(*lists)]
        + [slots[2 * cap:], other_slots[2 * cap:], jnp.zeros(126, jnp.int32)]
    )

    row_state, meta, other_slabs = lax.optimization_barrier((row_state, meta, other_slabs))
    both = stage(meta, slabs, other_slabs)

    def across(x):
        return [send(x, at.moves_slow(d * at.group)) for d in range(1, at.chips)]

    def kept_of(x, got):
        got = [
            jnp.concatenate([chunk_of(y, k ^ d) for k in range(at.chips)], axis=0)
            for d, y in enumerate(got, 1)
        ]
        return pick(chip ^ root, [x] + got)

    row_now, row_scale = row_state[:, :half], row_state[:, half:half + 1]
    row_tile = (row_scale * row_now).astype(jnp.bfloat16)
    tiles_across = across(row_tile)
    row_tile, row_state = lax.optimization_barrier((row_tile, row_state))
    row_now, row_scale = row_state[:, :half], row_state[:, half:half + 1]
    row_rest = (row_now - row_tile.astype(jnp.float32) / row_scale).astype(jnp.bfloat16)

    before = None
    for iterate in range(STEPS):
        first, last = iterate == 0, iterate == STEPS - 1
        if not first:
            row_tile = pick(
                chip ^ root,
                [own] + [send(own, at.moves_chip(d)) for d in range(1, at.chips)],
            )
        dtypes = (jnp.float32,) * at.group + (jnp.bfloat16,) * at.group
        if not first:
            near = [own] + [send(own, at.moves_slow(g)) for g in range(1, at.group)]
            far = [send(own, at.moves_slow(g, 1)) for g in range(at.group)]
        sums = products(meta, both, row_tile, dtypes, n_kept, True)
        near_sums, far_sums = sums[:at.group], sums[at.group:]
        from_fast = [send(x, at.moves_fast()) for x in far_sums[::-1]][::-1]
        if first:
            tiles_across, far_sums = lax.optimization_barrier((tiles_across, far_sums))
            own = kept_of(row_tile, tiles_across)
            near = [own] + [send(own, at.moves_slow(g)) for g in range(1, at.group)]
            far = [send(own, at.moves_slow(g, 1)) for g in range(at.group)]
            row_rest, row_scale, near = lax.optimization_barrier((row_rest, row_scale, near))
            scales_across, rests_across = across(row_scale), across(row_rest)
        (row_sum,) = products(
            meta, both, jnp.concatenate(near + far, axis=0), (jnp.bfloat16,), n_row, False,
            after=far_sums,
        )
        if first:
            from_fast[-1], row_sum, scales_across, rests_across = lax.optimization_barrier(
                (from_fast[-1], row_sum, scales_across, rests_across)
            )
            scale = kept_of(row_scale, scales_across)
            now = kept_of(row_now, [
                tile.astype(jnp.float32) / factor + rest.astype(jnp.float32)
                for tile, factor, rest in zip(tiles_across, scales_across, rests_across)
            ])
        from_row = [row_sum] + [
            send(row_sum, at.moves_chip(d)) for d in range(1, at.chips)
        ]
        sums = [x + y.astype(jnp.float32) for x, y in zip(near_sums, from_fast)]
        total = sums[0]
        for g in range(1, at.group):
            total = total + send(
                sums[g].astype(jnp.bfloat16), at.moves_slow(g)
            ).astype(jnp.float32)
        for x in from_row:
            total = total + jnp.where(is_root, x, jnp.zeros_like(x)).astype(jnp.float32)
        message = total.astype(jnp.bfloat16)
        if last:
            total, now, scale = chunk_of(total, 0), chunk_of(now, 0), chunk_of(scale, 0)
            before = chunk_of(before, 0)
        applied = total
        for e in range(1, at.chips):
            if last:
                got = send(chunk_of(message, e), at.moves_slow(e * at.group))
            else:
                got = send(message, at.moves_slow(e * at.group))
                got = jnp.concatenate([chunk_of(got, k ^ e) for k in range(at.chips)], axis=0)
            applied = applied + got.astype(jnp.float32)
        mapped = scale * applied - center_shift * now
        if first:
            updated = mapped / half_width
        else:
            updated = 2.0 / half_width * mapped - before
        before = now
        now = updated
        if not last:
            own = (scale * now).astype(jnp.bfloat16)
    back = [
        send(now[swap * part:(swap + 1) * part], turned(at.moves_home(swap)))
        for swap in range(2)
    ]
    result = jnp.stack([jnp.where(core == k, back[0], back[1]) for k in range(2)])
    return result.transpose(0, 2, 1, 3).reshape(start_vectors.shape)


def solution(mesh):
    in_specs = (
        P(None, ("row", "col")),
        P(("row", "col")),
        P("row", "col", None, None, None),
        P("row", "col", None, None),
        P("row", "col"),
    )
    out_specs = P(None, ("row", "col"))
    return jax.shard_map(
        per_device, mesh=mesh, in_specs=in_specs, out_specs=out_specs, check_vma=False
    )
```

```python
import functools

import jax
import jax.numpy as jnp
from jax import lax
from jax.experimental import pallas as pl
from jax.experimental.pallas import tpu as pltpu
from jax.sharding import PartitionSpec as P

STEPS = 3

center_shift = 0.5
half_width = 3.0

UNROLL = 64
PACK = 4
VMEM_LIMIT = 16 * 1024 * 1024
AXES = ("row", "col")
PAD = 8


class Layout:
    def __init__(self, rows, cols):
        self.rows, self.cols = rows, cols
        self.chips = cols // 2
        self.fast = 2
        self.slow = rows // 2
        self.group = self.slow // self.chips
        assert self.group * self.chips * self.fast == rows

    def device(self, slow, fast, chip, core):
        return (slow * self.fast + fast) * self.cols + chip * 2 + core

    def home(self, chunk):
        chip, k = chunk // self.rows, chunk % self.rows
        e, f, t = k % self.chips, (k // self.chips) % self.fast, k // (self.chips * self.fast)
        return (chip ^ e) * self.group + t, f, chip

    def moves_home(self, swap):
        pairs = []
        for chunk in range(self.rows * self.chips):
            row, chip = chunk // self.chips, chunk % self.chips
            for core in range(2):
                source = row * self.cols + chip * 2 + core
                pairs.append((source, self.device(*self.home(chunk), core ^ swap)))
        return pairs

    def moves_slow(self, d, side=0):
        return [
            (self.device(s, f, c, q), self.device(s ^ d, f ^ side, c, q))
            for s in range(self.slow) for f in range(self.fast)
            for c in range(self.chips) for q in range(2)
        ]

    def moves_fast(self):
        return self.moves_slow(0, 1)

    def moves_chip(self, d, swap=0):
        return [
            (self.device(s, f, c, q), self.device(s, f, c ^ d, q ^ swap))
            for s in range(self.slow) for f in range(self.fast)
            for c in range(self.chips) for q in range(2)
        ]

    def moves_core(self):
        return [(i, i ^ 1) for i in range(self.rows * self.cols)]


def turned(pairs):
    return [(b, a) for a, b in pairs]


def live_groups(meta_ref, cap, which):
    return jnp.maximum((meta_ref[8 * cap + which] + (UNROLL - 1)) // UNROLL, 1)


def product_kernel(transpose, cap, n_out, carry, after, meta_in, vecs_in, *refs):
    slab_refs, refs = refs[:2], refs[2 + after:]
    outs, refs = refs[:n_out], refs[n_out + carry:]
    meta_ref, vecs_ref, slabs, acc, slab_sem, in_sem = refs
    base = 0 if transpose else 4 * cap

    def slab_copy(which, g):
        span = pl.ds(g * UNROLL, UNROLL)
        to = pl.ds(which * cap + g * UNROLL, UNROLL)
        sem = slab_sem.at[which * (cap // UNROLL) + g]
        return pltpu.make_async_copy(slab_refs[which].at[span], slabs.at[to], sem)

    def start_slab(which, g, carry):
        slab_copy(which, g).start()
        return carry

    meta_copy = pltpu.make_async_copy(meta_in, meta_ref, in_sem.at[0])
    vecs_copy = pltpu.make_async_copy(vecs_in, vecs_ref, in_sem.at[1])
    meta_copy.start()
    slab_copy(0, 0).start()
    vecs_copy.start()
    slab_copy(1, 0).start()
    acc[...] = jnp.zeros_like(acc)
    meta_copy.wait()
    groups = [live_groups(meta_ref, cap, which) for which in range(2)]
    for which in range(2):
        lax.fori_loop(1, groups[which], functools.partial(start_slab, which), 0)
    vecs_copy.wait()
    vec_count, block_len = vecs_ref.shape[1:]
    zero = jnp.zeros((vec_count, block_len), jnp.bfloat16)

    def body(which, g, carry):
        slab_copy(which, g).wait()
        start = which * cap + g * UNROLL
        products = []
        for u in range(0, UNROLL, PACK):
            v = [vecs_ref[meta_ref[base + start + u + k]] for k in range(PACK)]
            m = [slabs[start + u + k] for k in range(PACK)]
            left = jnp.concatenate([
                jnp.concatenate([v[0], zero, v[2], zero], axis=0),
                jnp.concatenate([zero, v[1], zero, v[3]], axis=0),
            ], axis=1)
            if transpose:
                halves = [jnp.concatenate(m[:2], axis=0), jnp.concatenate(m[2:], axis=0)]
                right, dims = jnp.concatenate(halves, axis=1), (((1,), (0,)), ((), ()))
            else:
                halves = [jnp.concatenate(m[:2], axis=1), jnp.concatenate(m[2:], axis=1)]
                right, dims = jnp.concatenate(halves, axis=0), (((1,), (1,)), ((), ()))
            products.append(
                lax.dot_general(left, right, dims, preferred_element_type=jnp.float32)
            )
        for u in range(UNROLL):
            k = u % PACK
            rows = slice(k * vec_count, (k + 1) * vec_count)
            lanes = slice((k // 2) * block_len, (k // 2 + 1) * block_len)
            acc[meta_ref[base + 2 * cap + start + u]] += products[u // PACK][rows, lanes]
        return carry

    for which in range(2):
        lax.fori_loop(0, groups[which], functools.partial(body, which), 0)
    size = outs[0].shape[0]
    for k, out in enumerate(outs):
        out[...] = acc[k * size:(k + 1) * size].astype(out.dtype)


def products(meta, slabs, vecs, out_dtypes, out_blocks, transpose, carry=False, after=()):
    cap, block_len, _ = slabs[0].shape
    vec_count = vecs.shape[1]
    n_out = len(out_dtypes)
    total_out = out_blocks * n_out
    anywhere = pl.BlockSpec(memory_space=pl.ANY)
    vmem = pl.BlockSpec(memory_space=pltpu.VMEM)
    out_shape = [
        jax.ShapeDtypeStruct((out_blocks, vec_count, block_len), dtype) for dtype in out_dtypes
    ]
    if carry:
        out_shape.append(jax.ShapeDtypeStruct(slabs[1].shape, slabs[1].dtype))
    return pl.pallas_call(
        functools.partial(product_kernel, transpose, cap, n_out, carry, len(after)),
        in_specs=[anywhere] * (4 + len(after)),
        out_specs=[vmem] * n_out + [anywhere] * carry,
        out_shape=out_shape,
        input_output_aliases={3: n_out} if carry else {},
        scratch_shapes=[
            pltpu.SMEM(meta.shape, jnp.int32),
            pltpu.VMEM(vecs.shape, jnp.bfloat16),
            pltpu.VMEM((2 * cap, block_len, block_len), jnp.bfloat16),
            pltpu.VMEM((total_out + 1, vec_count, block_len), jnp.float32),
            pltpu.SemaphoreType.DMA((2 * cap // UNROLL,)),
            pltpu.SemaphoreType.DMA((2,)),
        ],
        compiler_params=pltpu.CompilerParams(vmem_limit_bytes=VMEM_LIMIT),
        cost_estimate=pl.CostEstimate(
            flops=4 * cap * vec_count * block_len * block_len,
            bytes_accessed=2 * vec_count * block_len * (vecs.shape[0] + total_out),
            transcendentals=0,
        ),
        name="transposed" if transpose else "direct",
    )(meta, vecs, *slabs, *after)


def per_device(start_vectors, scaling, block_values, block_places, block_counts):
    at = Layout(lax.axis_size("row"), lax.axis_size("col"))
    cap = block_values.shape[2]
    block_len = block_values.shape[-1]
    half = start_vectors.shape[0] // 2
    part = start_vectors.shape[1] // block_len
    per_chunk = 2 * part
    row_index = lax.axis_index("row").astype(jnp.int32)
    col_index = lax.axis_index("col").astype(jnp.int32)
    slow, fast = row_index // at.fast, row_index % at.fast
    chip, core = col_index // 2, col_index % 2
    root = slow // at.group
    is_root = chip == root
    def send(x, pairs):
        return lax.ppermute(x, AXES, pairs)

    slabs = block_values.reshape(cap, block_len, block_len)
    slots = jnp.concatenate([block_places.reshape(2 * cap), block_counts.reshape(1)])
    other_slabs = send(slabs, at.moves_core())

    halves = start_vectors.reshape(2, half, part, block_len).transpose(0, 2, 1, 3)
    scale_rows = jnp.broadcast_to(
        scaling.reshape(1, part, 1, block_len), (2, part, PAD, block_len)
    )
    halves = jnp.concatenate([halves, scale_rows], axis=2)
    packed = [
        jnp.where(core == swap, halves[0], halves[1]) for swap in range(2)
    ]
    pieces = [
        jnp.concatenate([
            packed[swap] if (d, swap) == (0, 0) else send(packed[swap], at.moves_chip(d, swap))
            for swap in range(2)
        ], axis=0)
        for d in range(at.chips)
    ]
    n_kept = at.chips * per_chunk

    def chunk_of(x, e):
        return x[e * per_chunk:(e + 1) * per_chunk]

    def pick(index, choices):
        x = choices[0]
        for d in range(1, len(choices)):
            x = jnp.where(index == d, choices[d], x)
        return x

    row_state = jnp.concatenate([pick(chip ^ e, pieces) for e in range(at.chips)], axis=0)

    other_slots = send(slots, at.moves_core())
    n_col = at.rows * per_chunk
    n_row = at.chips * per_chunk
    lists = []
    for which, held in enumerate((slots, other_slots)):
        row_block, col_block = held[:cap], held[cap:2 * cap]
        live = jnp.arange(cap, dtype=jnp.int32) < held[2 * cap]

        def inside(block):
            return ((block // part) ^ core) * part + block % part

        e = row_block // per_chunk
        row_at = e * per_chunk + inside(row_block % per_chunk)
        block = (core ^ which) * (n_col // 2) + col_block
        k = block // per_chunk
        e, f, t = k % at.chips, (k // at.chips) % at.fast, k // (at.chips * at.fast)
        d = slow ^ ((chip ^ e) * at.group + t)
        place = (d % at.group) * at.chips + d // at.group
        col_at = ((fast ^ f) * at.slow + place) * per_chunk + inside(block % per_chunk)
        lists.append((
            row_at, jnp.where(live, col_at, n_col), col_at, jnp.where(live, row_at, n_row)
        ))
    meta = jnp.concatenate(
        [jnp.concatenate([mine, theirs]) for mine, theirs in zip(*lists)]
        + [slots[2 * cap:], other_slots[2 * cap:], jnp.zeros(126, jnp.int32)]
    )

    row_state, meta, other_slabs = lax.optimization_barrier((row_state, meta, other_slabs))
    both = (slabs, other_slabs)

    def across(x):
        return [send(x, at.moves_slow(d * at.group)) for d in range(1, at.chips)]

    def kept_of(x, got):
        got = [
            jnp.concatenate([chunk_of(y, k ^ d) for k in range(at.chips)], axis=0)
            for d, y in enumerate(got, 1)
        ]
        return pick(chip ^ root, [x] + got)

    row_now, row_scale = row_state[:, :half], row_state[:, half:half + 1]
    row_tile = (row_scale * row_now).astype(jnp.bfloat16)
    tiles_across = across(row_tile)
    row_tile, row_state = lax.optimization_barrier((row_tile, row_state))
    row_now, row_scale = row_state[:, :half], row_state[:, half:half + 1]
    row_rest = (row_now - row_tile.astype(jnp.float32) / row_scale).astype(jnp.bfloat16)

    before = None
    for iterate in range(STEPS):
        first, last = iterate == 0, iterate == STEPS - 1
        if not first:
            row_tile = pick(
                chip ^ root,
                [own] + [send(own, at.moves_chip(d)) for d in range(1, at.chips)],
            )
        dtypes = (jnp.float32,) * at.group + (jnp.bfloat16,) * at.group
        if not first:
            near = [own] + [send(own, at.moves_slow(g)) for g in range(1, at.group)]
            far = [send(own, at.moves_slow(g, 1)) for g in range(at.group)]
        sums = list(products(meta, both, row_tile, dtypes, n_kept, True, carry=first))
        if first:
            both = (slabs, sums.pop())
        near_sums, far_sums = list(sums[:at.group]), list(sums[at.group:])
        from_fast = [send(x, at.moves_fast()) for x in far_sums[::-1]][::-1]
        if first:
            tiles_across, far_sums = lax.optimization_barrier((tiles_across, far_sums))
            own = kept_of(row_tile, tiles_across)
            near = [own] + [send(own, at.moves_slow(g)) for g in range(1, at.group)]
            far = [send(own, at.moves_slow(g, 1)) for g in range(at.group)]
            row_rest, row_scale, near = lax.optimization_barrier((row_rest, row_scale, near))
            scales_across, rests_across = across(row_scale), across(row_rest)
        (row_sum,) = products(
            meta, both, jnp.concatenate(near + far, axis=0), (jnp.bfloat16,), n_row, False,
            after=far_sums,
        )
        if first:
            from_fast[-1], row_sum, scales_across, rests_across = lax.optimization_barrier(
                (from_fast[-1], row_sum, scales_across, rests_across)
            )
            scale = kept_of(row_scale, scales_across)
            now = kept_of(row_now, [
                tile.astype(jnp.float32) / factor + rest.astype(jnp.float32)
                for tile, factor, rest in zip(tiles_across, scales_across, rests_across)
            ])
        from_row = [row_sum] + [
            send(row_sum, at.moves_chip(d)) for d in range(1, at.chips)
        ]
        sums = [x + y.astype(jnp.float32) for x, y in zip(near_sums, from_fast)]
        total = sums[0]
        for g in range(1, at.group):
            total = total + send(
                sums[g].astype(jnp.bfloat16), at.moves_slow(g)
            ).astype(jnp.float32)
        for x in from_row:
            total = total + jnp.where(is_root, x, jnp.zeros_like(x)).astype(jnp.float32)
        message = total.astype(jnp.bfloat16)
        if last:
            total, now, scale = chunk_of(total, 0), chunk_of(now, 0), chunk_of(scale, 0)
            before = chunk_of(before, 0)
        applied = total
        for e in range(1, at.chips):
            if last:
                got = send(chunk_of(message, e), at.moves_slow(e * at.group))
            else:
                got = send(message, at.moves_slow(e * at.group))
                got = jnp.concatenate([chunk_of(got, k ^ e) for k in range(at.chips)], axis=0)
            applied = applied + got.astype(jnp.float32)
        mapped = scale * applied - center_shift * now
        if first:
            updated = mapped / half_width
        else:
            updated = 2.0 / half_width * mapped - before
        before = now
        now = updated
        if not last:
            own = (scale * now).astype(jnp.bfloat16)
    back = [
        send(now[swap * part:(swap + 1) * part], turned(at.moves_home(swap)))
        for swap in range(2)
    ]
    result = jnp.stack([jnp.where(core == k, back[0], back[1]) for k in range(2)])
    return result.transpose(0, 2, 1, 3).reshape(start_vectors.shape)


def solution(mesh):
    in_specs = (
        P(None, ("row", "col")),
        P(("row", "col")),
        P("row", "col", None, None, None),
        P("row", "col", None, None),
        P("row", "col"),
    )
    out_specs = P(None, ("row", "col"))
    return jax.shard_map(
        per_device, mesh=mesh, in_specs=in_specs, out_specs=out_specs, check_vma=False
    )
```

```python
import functools

import jax
import jax.numpy as jnp
from jax import lax
from jax.experimental import pallas as pl
from jax.experimental.pallas import tpu as pltpu
from jax.sharding import PartitionSpec as P

STEPS = 3

center_shift = 0.5
half_width = 3.0

UNROLL = 64
PACK = 4
VMEM_LIMIT = 16 * 1024 * 1024
AXES = ("row", "col")
PAD = 8


class Layout:
    def __init__(self, rows, cols):
        self.rows, self.cols = rows, cols
        self.chips = cols // 2
        self.fast = 2
        self.slow = rows // 2
        self.group = self.slow // self.chips
        assert self.group * self.chips * self.fast == rows

    def device(self, slow, fast, chip, core):
        return (slow * self.fast + fast) * self.cols + chip * 2 + core

    def home(self, chunk):
        chip, k = chunk // self.rows, chunk % self.rows
        e, f, t = k % self.chips, (k // self.chips) % self.fast, k // (self.chips * self.fast)
        return (chip ^ e) * self.group + t, f, chip

    def moves_home(self, swap):
        pairs = []
        for chunk in range(self.rows * self.chips):
            row, chip = chunk // self.chips, chunk % self.chips
            for core in range(2):
                source = row * self.cols + chip * 2 + core
                pairs.append((source, self.device(*self.home(chunk), core ^ swap)))
        return pairs

    def moves_slow(self, d, side=0):
        return [
            (self.device(s, f, c, q), self.device(s ^ d, f ^ side, c, q))
            for s in range(self.slow) for f in range(self.fast)
            for c in range(self.chips) for q in range(2)
        ]

    def moves_fast(self):
        return self.moves_slow(0, 1)

    def moves_chip(self, d, swap=0, slow=0):
        return [
            (self.device(s, f, c, q), self.device(s ^ slow, f, c ^ d, q ^ swap))
            for s in range(self.slow) for f in range(self.fast)
            for c in range(self.chips) for q in range(2)
        ]

    def moves_core(self):
        return [(i, i ^ 1) for i in range(self.rows * self.cols)]


def turned(pairs):
    return [(b, a) for a, b in pairs]


def live_groups(meta_ref, cap, which):
    return jnp.maximum((meta_ref[8 * cap + which] + (UNROLL - 1)) // UNROLL, 1)


def product_kernel(transpose, cap, n_out, after, meta_in, vecs_in, *refs):
    slab_refs, refs = refs[:2], refs[2 + after:]
    outs, refs = refs[:n_out], refs[n_out:]
    meta_ref, vecs_ref, slabs, acc, slab_sem, in_sem = refs
    base = 0 if transpose else 4 * cap

    def slab_copy(which, g):
        span = pl.ds(g * UNROLL, UNROLL)
        to = pl.ds(which * cap + g * UNROLL, UNROLL)
        sem = slab_sem.at[which * (cap // UNROLL) + g]
        return pltpu.make_async_copy(slab_refs[which].at[span], slabs.at[to], sem)

    def start_slab(which, g, carry):
        slab_copy(which, g).start()
        return carry

    meta_copy = pltpu.make_async_copy(meta_in, meta_ref, in_sem.at[0])
    vecs_copy = pltpu.make_async_copy(vecs_in, vecs_ref, in_sem.at[1])
    meta_copy.start()
    slab_copy(0, 0).start()
    vecs_copy.start()
    slab_copy(1, 0).start()
    acc[...] = jnp.zeros_like(acc)
    meta_copy.wait()
    groups = [live_groups(meta_ref, cap, which) for which in range(2)]
    for which in range(2):
        lax.fori_loop(1, groups[which], functools.partial(start_slab, which), 0)
    vecs_copy.wait()
    vec_count, block_len = vecs_ref.shape[1:]
    zero = jnp.zeros((vec_count, block_len), jnp.bfloat16)

    def body(which, g, carry):
        slab_copy(which, g).wait()
        start = which * cap + g * UNROLL
        products = []
        for u in range(0, UNROLL, PACK):
            v = [vecs_ref[meta_ref[base + start + u + k]] for k in range(PACK)]
            m = [slabs[start + u + k] for k in range(PACK)]
            left = jnp.concatenate([
                jnp.concatenate([v[0], zero, v[2], zero], axis=0),
                jnp.concatenate([zero, v[1], zero, v[3]], axis=0),
            ], axis=1)
            if transpose:
                halves = [jnp.concatenate(m[:2], axis=0), jnp.concatenate(m[2:], axis=0)]
                right, dims = jnp.concatenate(halves, axis=1), (((1,), (0,)), ((), ()))
            else:
                halves = [jnp.concatenate(m[:2], axis=1), jnp.concatenate(m[2:], axis=1)]
                right, dims = jnp.concatenate(halves, axis=0), (((1,), (1,)), ((), ()))
            products.append(
                lax.dot_general(left, right, dims, preferred_element_type=jnp.float32)
            )
        for u in range(UNROLL):
            k = u % PACK
            rows = slice(k * vec_count, (k + 1) * vec_count)
            lanes = slice((k // 2) * block_len, (k // 2 + 1) * block_len)
            acc[meta_ref[base + 2 * cap + start + u]] += products[u // PACK][rows, lanes]
        return carry

    for which in range(2):
        lax.fori_loop(0, groups[which], functools.partial(body, which), 0)
    size = outs[0].shape[0]
    for k, out in enumerate(outs):
        out[...] = acc[k * size:(k + 1) * size].astype(out.dtype)


def products(meta, slabs, vecs, out_dtypes, out_blocks, transpose, after=()):
    cap, block_len, _ = slabs[0].shape
    vec_count = vecs.shape[1]
    n_out = len(out_dtypes)
    total_out = out_blocks * n_out
    anywhere = pl.BlockSpec(memory_space=pl.ANY)
    vmem = pl.BlockSpec(memory_space=pltpu.VMEM)
    out_shape = [
        jax.ShapeDtypeStruct((out_blocks, vec_count, block_len), dtype) for dtype in out_dtypes
    ]
    return pl.pallas_call(
        functools.partial(product_kernel, transpose, cap, n_out, len(after)),
        in_specs=[anywhere] * (4 + len(after)),
        out_specs=[vmem] * n_out,
        out_shape=out_shape,
        scratch_shapes=[
            pltpu.SMEM(meta.shape, jnp.int32),
            pltpu.VMEM(vecs.shape, jnp.bfloat16),
            pltpu.VMEM((2 * cap, block_len, block_len), jnp.bfloat16),
            pltpu.VMEM((total_out + 1, vec_count, block_len), jnp.float32),
            pltpu.SemaphoreType.DMA((2 * cap // UNROLL,)),
            pltpu.SemaphoreType.DMA((2,)),
        ],
        compiler_params=pltpu.CompilerParams(vmem_limit_bytes=VMEM_LIMIT),
        cost_estimate=pl.CostEstimate(
            flops=4 * cap * vec_count * block_len * block_len,
            bytes_accessed=2 * vec_count * block_len * (vecs.shape[0] + total_out),
            transcendentals=0,
        ),
        name="transposed" if transpose else "direct",
    )(meta, vecs, *slabs, *after)


def per_device(start_vectors, scaling, block_values, block_places, block_counts):
    at = Layout(lax.axis_size("row"), lax.axis_size("col"))
    cap = block_values.shape[2]
    block_len = block_values.shape[-1]
    half = start_vectors.shape[0] // 2
    part = start_vectors.shape[1] // block_len
    per_chunk = 2 * part
    row_index = lax.axis_index("row").astype(jnp.int32)
    col_index = lax.axis_index("col").astype(jnp.int32)
    slow, fast = row_index // at.fast, row_index % at.fast
    chip, core = col_index // 2, col_index % 2
    root = slow // at.group
    is_root = chip == root
    def send(x, pairs):
        return lax.ppermute(x, AXES, pairs)

    slabs = block_values.reshape(cap, block_len, block_len)
    slots = jnp.concatenate([block_places.reshape(2 * cap), block_counts.reshape(1)])
    other_slabs = send(slabs, at.moves_core())

    halves = start_vectors.reshape(2, half, part, block_len).transpose(0, 2, 1, 3)
    scale_rows = jnp.broadcast_to(
        scaling.reshape(1, part, 1, block_len), (2, part, PAD, block_len)
    )
    halves = jnp.concatenate([halves, scale_rows], axis=2)
    packed = [
        jnp.where(core == swap, halves[0], halves[1]) for swap in range(2)
    ]
    chunk = jnp.concatenate([packed[0], send(packed[1], at.moves_core())], axis=0)
    pieces = [chunk] + [send(chunk, at.moves_chip(d)) for d in range(1, at.chips)]
    n_kept = at.chips * per_chunk

    def chunk_of(x, e):
        return x[e * per_chunk:(e + 1) * per_chunk]

    def pick(index, choices):
        x = choices[0]
        for d in range(1, len(choices)):
            x = jnp.where(index == d, choices[d], x)
        return x

    row_state = jnp.concatenate([pick(chip ^ e, pieces) for e in range(at.chips)], axis=0)

    other_slots = send(slots, at.moves_core())
    n_col = at.rows * per_chunk
    n_row = at.chips * per_chunk
    lists = []
    for which, held in enumerate((slots, other_slots)):
        row_block, col_block = held[:cap], held[cap:2 * cap]
        live = jnp.arange(cap, dtype=jnp.int32) < held[2 * cap]

        def inside(block):
            return ((block // part) ^ core) * part + block % part

        e = row_block // per_chunk
        row_at = e * per_chunk + inside(row_block % per_chunk)
        block = (core ^ which) * (n_col // 2) + col_block
        k = block // per_chunk
        e, f, t = k % at.chips, (k // at.chips) % at.fast, k // (at.chips * at.fast)
        d = slow ^ ((chip ^ e) * at.group + t)
        place = (d % at.group) * at.chips + d // at.group
        col_at = ((fast ^ f) * at.slow + place) * per_chunk + inside(block % per_chunk)
        lists.append((
            row_at, jnp.where(live, col_at, n_col), col_at, jnp.where(live, row_at, n_row)
        ))
    meta = jnp.concatenate(
        [jnp.concatenate([mine, theirs]) for mine, theirs in zip(*lists)]
        + [slots[2 * cap:], other_slots[2 * cap:], jnp.zeros(126, jnp.int32)]
    )

    both = (slabs, other_slabs)

    def across(x):
        return [send(x, at.moves_slow(d * at.group)) for d in range(1, at.chips)]

    def kept_of(x, got):
        got = [
            jnp.concatenate([chunk_of(y, k ^ d) for k in range(at.chips)], axis=0)
            for d, y in enumerate(got, 1)
        ]
        return pick(chip ^ root, [x] + got)

    scaled = (chunk[:, half:half + 1] * chunk[:, :half]).astype(jnp.bfloat16)
    tiles_across = []
    for d in range(1, at.chips):
        got = [send(scaled, at.moves_chip(c, 0, d * at.group)) for c in range(at.chips)]
        tiles_across.append(
            jnp.concatenate([pick(chip ^ e, got) for e in range(at.chips)], axis=0)
        )
    row_now, row_scale = row_state[:, :half], row_state[:, half:half + 1]
    row_tile = (row_scale * row_now).astype(jnp.bfloat16)
    own = kept_of(row_tile, tiles_across)
    scales_across = across(row_scale)

    before = None
    for iterate in range(STEPS):
        first, last = iterate == 0, iterate == STEPS - 1
        if not first:
            row_tile = pick(
                chip ^ root,
                [own] + [send(own, at.moves_chip(d)) for d in range(1, at.chips)],
            )
        dtypes = (jnp.float32,) * at.group + (jnp.bfloat16,) * at.group
        near = [own] + [send(own, at.moves_slow(g)) for g in range(1, at.group)]
        far = [send(own, at.moves_slow(g, 1)) for g in range(at.group)]
        sums = products(meta, both, row_tile, dtypes, n_kept, True)
        near_sums, far_sums = list(sums[:at.group]), list(sums[at.group:])
        if first:
            row_tile, row_state, near, scales_across = lax.optimization_barrier(
                (row_tile, row_state, near, scales_across)
            )
            row_now, row_scale = row_state[:, :half], row_state[:, half:half + 1]
            rests_across = across(
                (row_now - row_tile.astype(jnp.float32) / row_scale).astype(jnp.bfloat16)
            )
        from_fast = [send(x, at.moves_fast()) for x in far_sums[::-1]][::-1]
        (row_sum,) = products(
            meta, both, jnp.concatenate(near + far, axis=0), (jnp.bfloat16,), n_row, False,
            after=far_sums,
        )
        if first:
            from_fast[-1], row_sum, rests_across = lax.optimization_barrier(
                (from_fast[-1], row_sum, rests_across)
            )
            scale = kept_of(row_scale, scales_across)
            now = kept_of(row_now, [
                tile.astype(jnp.float32) / factor + rest.astype(jnp.float32)
                for tile, factor, rest in zip(tiles_across, scales_across, rests_across)
            ])
        from_row = [row_sum] + [
            send(row_sum, at.moves_chip(d)) for d in range(1, at.chips)
        ]
        sums = [x + y.astype(jnp.float32) for x, y in zip(near_sums, from_fast)]
        total = sums[0]
        for g in range(1, at.group):
            total = total + send(
                sums[g].astype(jnp.bfloat16), at.moves_slow(g)
            ).astype(jnp.float32)
        for x in from_row:
            total = total + jnp.where(is_root, x, jnp.zeros_like(x)).astype(jnp.float32)
        message = total.astype(jnp.bfloat16)
        if last:
            total, now, scale = chunk_of(total, 0), chunk_of(now, 0), chunk_of(scale, 0)
            before = chunk_of(before, 0)
        applied = total
        for e in range(1, at.chips):
            if last:
                got = send(chunk_of(message, e), at.moves_slow(e * at.group))
            else:
                got = send(message, at.moves_slow(e * at.group))
                got = jnp.concatenate([chunk_of(got, k ^ e) for k in range(at.chips)], axis=0)
            applied = applied + got.astype(jnp.float32)
        mapped = scale * applied - center_shift * now
        if first:
            updated = mapped / half_width
        else:
            updated = 2.0 / half_width * mapped - before
        before = now
        now = updated
        if not last:
            own = (scale * now).astype(jnp.bfloat16)
    back = [
        send(now[swap * part:(swap + 1) * part], turned(at.moves_home(swap)))
        for swap in range(2)
    ]
    result = jnp.stack([jnp.where(core == k, back[0], back[1]) for k in range(2)])
    return result.transpose(0, 2, 1, 3).reshape(start_vectors.shape)


def solution(mesh):
    in_specs = (
        P(None, ("row", "col")),
        P(("row", "col")),
        P("row", "col", None, None, None),
        P("row", "col", None, None),
        P("row", "col"),
    )
    out_specs = P(None, ("row", "col"))
    return jax.shard_map(
        per_device, mesh=mesh, in_specs=in_specs, out_specs=out_specs, check_vma=False
    )
```

```python
import functools

import jax
import jax.numpy as jnp
from jax import lax
from jax.experimental import pallas as pl
from jax.experimental.pallas import tpu as pltpu
from jax.sharding import PartitionSpec as P

STEPS = 3

center_shift = 0.5
half_width = 3.0

UNROLL = 64
PACK = 4
VMEM_LIMIT = 16 * 1024 * 1024
AXES = ("row", "col")
PAD = 8


class Layout:
    def __init__(self, rows, cols):
        self.rows, self.cols = rows, cols
        self.chips = cols // 2
        self.fast = 2
        self.slow = rows // 2
        self.group = self.slow // self.chips
        assert self.group * self.chips * self.fast == rows

    def device(self, slow, fast, chip, core):
        return (slow * self.fast + fast) * self.cols + chip * 2 + core

    def home(self, chunk):
        chip, k = chunk // self.rows, chunk % self.rows
        e, f, t = k % self.chips, (k // self.chips) % self.fast, k // (self.chips * self.fast)
        return (chip ^ e) * self.group + t, f, chip

    def moves_home(self, swap):
        pairs = []
        for chunk in range(self.rows * self.chips):
            row, chip = chunk // self.chips, chunk % self.chips
            for core in range(2):
                source = row * self.cols + chip * 2 + core
                pairs.append((source, self.device(*self.home(chunk), core ^ swap)))
        return pairs

    def moves_slow(self, d, side=0):
        return [
            (self.device(s, f, c, q), self.device(s ^ d, f ^ side, c, q))
            for s in range(self.slow) for f in range(self.fast)
            for c in range(self.chips) for q in range(2)
        ]

    def moves_fast(self):
        return self.moves_slow(0, 1)

    def moves_chip(self, d, swap=0):
        return [
            (self.device(s, f, c, q), self.device(s, f, c ^ d, q ^ swap))
            for s in range(self.slow) for f in range(self.fast)
            for c in range(self.chips) for q in range(2)
        ]

    def moves_core(self):
        return [(i, i ^ 1) for i in range(self.rows * self.cols)]


def turned(pairs):
    return [(b, a) for a, b in pairs]


def live_groups(meta_ref, cap, which):
    return jnp.maximum((meta_ref[8 * cap + which] + (UNROLL - 1)) // UNROLL, 1)


def product_kernel(transpose, cap, n_out, after, meta_in, vecs_in, *refs):
    slab_refs, refs = refs[:2], refs[2 + after:]
    outs, refs = refs[:n_out], refs[n_out:]
    meta_ref, vecs_ref, slabs, acc, slab_sem, in_sem = refs
    base = 0 if transpose else 4 * cap

    def slab_copy(which, g):
        span = pl.ds(g * UNROLL, UNROLL)
        to = pl.ds(which * cap + g * UNROLL, UNROLL)
        sem = slab_sem.at[which * (cap // UNROLL) + g]
        return pltpu.make_async_copy(slab_refs[which].at[span], slabs.at[to], sem)

    def start_slab(which, g, carry):
        slab_copy(which, g).start()
        return carry

    meta_copy = pltpu.make_async_copy(meta_in, meta_ref, in_sem.at[0])
    vecs_copy = pltpu.make_async_copy(vecs_in, vecs_ref, in_sem.at[1])
    meta_copy.start()
    slab_copy(0, 0).start()
    vecs_copy.start()
    slab_copy(1, 0).start()
    acc[...] = jnp.zeros_like(acc)
    meta_copy.wait()
    groups = [live_groups(meta_ref, cap, which) for which in range(2)]
    for which in range(2):
        lax.fori_loop(1, groups[which], functools.partial(start_slab, which), 0)
    vecs_copy.wait()
    vec_count, block_len = vecs_ref.shape[1:]
    zero = jnp.zeros((vec_count, block_len), jnp.bfloat16)

    def body(which, g, carry):
        slab_copy(which, g).wait()
        start = which * cap + g * UNROLL
        products = []
        for u in range(0, UNROLL, PACK):
            v = [vecs_ref[meta_ref[base + start + u + k]] for k in range(PACK)]
            m = [slabs[start + u + k] for k in range(PACK)]
            left = jnp.concatenate([
                jnp.concatenate([v[0], zero, v[2], zero], axis=0),
                jnp.concatenate([zero, v[1], zero, v[3]], axis=0),
            ], axis=1)
            if transpose:
                halves = [jnp.concatenate(m[:2], axis=0), jnp.concatenate(m[2:], axis=0)]
                right, dims = jnp.concatenate(halves, axis=1), (((1,), (0,)), ((), ()))
            else:
                halves = [jnp.concatenate(m[:2], axis=1), jnp.concatenate(m[2:], axis=1)]
                right, dims = jnp.concatenate(halves, axis=0), (((1,), (1,)), ((), ()))
            products.append(
                lax.dot_general(left, right, dims, preferred_element_type=jnp.float32)
            )
        for u in range(UNROLL):
            k = u % PACK
            rows = slice(k * vec_count, (k + 1) * vec_count)
            lanes = slice((k // 2) * block_len, (k // 2 + 1) * block_len)
            acc[meta_ref[base + 2 * cap + start + u]] += products[u // PACK][rows, lanes]
        return carry

    for which in range(2):
        lax.fori_loop(0, groups[which], functools.partial(body, which), 0)
    size = outs[0].shape[0]
    for k, out in enumerate(outs):
        out[...] = acc[k * size:(k + 1) * size].astype(out.dtype)


def products(meta, slabs, vecs, out_dtypes, out_blocks, transpose, after=()):
    cap, block_len, _ = slabs[0].shape
    vec_count = vecs.shape[1]
    n_out = len(out_dtypes)
    total_out = out_blocks * n_out
    anywhere = pl.BlockSpec(memory_space=pl.ANY)
    vmem = pl.BlockSpec(memory_space=pltpu.VMEM)
    out_shape = [
        jax.ShapeDtypeStruct((out_blocks, vec_count, block_len), dtype) for dtype in out_dtypes
    ]
    return pl.pallas_call(
        functools.partial(product_kernel, transpose, cap, n_out, len(after)),
        in_specs=[anywhere] * (4 + len(after)),
        out_specs=[vmem] * n_out,
        out_shape=out_shape,
        scratch_shapes=[
            pltpu.SMEM(meta.shape, jnp.int32),
            pltpu.VMEM(vecs.shape, jnp.bfloat16),
            pltpu.VMEM((2 * cap, block_len, block_len), jnp.bfloat16),
            pltpu.VMEM((total_out + 1, vec_count, block_len), jnp.float32),
            pltpu.SemaphoreType.DMA((2 * cap // UNROLL,)),
            pltpu.SemaphoreType.DMA((2,)),
        ],
        compiler_params=pltpu.CompilerParams(vmem_limit_bytes=VMEM_LIMIT),
        cost_estimate=pl.CostEstimate(
            flops=4 * cap * vec_count * block_len * block_len,
            bytes_accessed=2 * vec_count * block_len * (vecs.shape[0] + total_out),
            transcendentals=0,
        ),
        name="transposed" if transpose else "direct",
    )(meta, vecs, *slabs, *after)


def per_device(start_vectors, scaling, block_values, block_places, block_counts):
    at = Layout(lax.axis_size("row"), lax.axis_size("col"))
    cap = block_values.shape[2]
    block_len = block_values.shape[-1]
    half = start_vectors.shape[0] // 2
    part = start_vectors.shape[1] // block_len
    per_chunk = 2 * part
    row_index = lax.axis_index("row").astype(jnp.int32)
    col_index = lax.axis_index("col").astype(jnp.int32)
    slow, fast = row_index // at.fast, row_index % at.fast
    chip, core = col_index // 2, col_index % 2
    root = slow // at.group
    is_root = chip == root
    def send(x, pairs):
        return lax.ppermute(x, AXES, pairs)

    slabs = block_values.reshape(cap, block_len, block_len)
    slots = jnp.concatenate([block_places.reshape(2 * cap), block_counts.reshape(1)])
    other_slabs = send(slabs, at.moves_core())

    halves = start_vectors.reshape(2, half, part, block_len).transpose(0, 2, 1, 3)
    scale_rows = jnp.broadcast_to(
        scaling.reshape(1, part, 1, block_len), (2, part, PAD, block_len)
    )
    halves = jnp.concatenate([halves, scale_rows], axis=2)
    packed = [
        jnp.where(core == swap, halves[0], halves[1]) for swap in range(2)
    ]
    pieces = [
        jnp.concatenate([
            packed[swap] if (d, swap) == (0, 0) else send(packed[swap], at.moves_chip(d, swap))
            for swap in range(2)
        ], axis=0)
        for d in range(at.chips)
    ]
    n_kept = at.chips * per_chunk

    def chunk_of(x, e):
        return x[e * per_chunk:(e + 1) * per_chunk]

    def pick(index, choices):
        x = choices[0]
        for d in range(1, len(choices)):
            x = jnp.where(index == d, choices[d], x)
        return x

    row_state = jnp.concatenate([pick(chip ^ e, pieces) for e in range(at.chips)], axis=0)

    other_slots = send(slots, at.moves_core())
    n_col = at.rows * per_chunk
    n_row = at.chips * per_chunk
    lists = []
    for which, held in enumerate((slots, other_slots)):
        row_block, col_block = held[:cap], held[cap:2 * cap]
        live = jnp.arange(cap, dtype=jnp.int32) < held[2 * cap]

        def inside(block):
            return ((block // part) ^ core) * part + block % part

        e = row_block // per_chunk
        row_at = e * per_chunk + inside(row_block % per_chunk)
        block = (core ^ which) * (n_col // 2) + col_block
        k = block // per_chunk
        e, f, t = k % at.chips, (k // at.chips) % at.fast, k // (at.chips * at.fast)
        d = slow ^ ((chip ^ e) * at.group + t)
        place = (d % at.group) * at.chips + d // at.group
        col_at = ((fast ^ f) * at.slow + place) * per_chunk + inside(block % per_chunk)
        lists.append((
            row_at, jnp.where(live, col_at, n_col), col_at, jnp.where(live, row_at, n_row)
        ))
    meta = jnp.concatenate(
        [jnp.concatenate([mine, theirs]) for mine, theirs in zip(*lists)]
        + [slots[2 * cap:], other_slots[2 * cap:], jnp.zeros(126, jnp.int32)]
    )

    row_state, meta, other_slabs = lax.optimization_barrier((row_state, meta, other_slabs))
    both = (slabs, other_slabs)

    def across(x):
        return [send(x, at.moves_slow(d * at.group)) for d in range(1, at.chips)]

    def kept_of(x, got):
        got = [
            jnp.concatenate([chunk_of(y, k ^ d) for k in range(at.chips)], axis=0)
            for d, y in enumerate(got, 1)
        ]
        return pick(chip ^ root, [x] + got)

    row_now, row_scale = row_state[:, :half], row_state[:, half:half + 1]
    row_tile = (row_scale * row_now).astype(jnp.bfloat16)
    tiles_across = across(row_tile)
    row_tile, row_state = lax.optimization_barrier((row_tile, row_state))
    row_now, row_scale = row_state[:, :half], row_state[:, half:half + 1]
    row_rest = (row_now - row_tile.astype(jnp.float32) / row_scale).astype(jnp.bfloat16)

    before = None
    for iterate in range(STEPS):
        first, last = iterate == 0, iterate == STEPS - 1
        if not first:
            row_tile = pick(
                chip ^ root,
                [own] + [send(own, at.moves_chip(d)) for d in range(1, at.chips)],
            )
        dtypes = (jnp.float32,) * at.group + (jnp.bfloat16,) * at.group
        if not first:
            near = [own] + [send(own, at.moves_slow(g)) for g in range(1, at.group)]
            far = [send(own, at.moves_slow(g, 1)) for g in range(at.group)]
        sums = products(meta, both, row_tile, dtypes, n_kept, True)
        near_sums, far_sums = list(sums[:at.group]), list(sums[at.group:])
        from_fast = [send(x, at.moves_fast()) for x in far_sums[::-1]][::-1]
        if first:
            tiles_across, far_sums = lax.optimization_barrier((tiles_across, far_sums))
            own = kept_of(row_tile, tiles_across)
            near = [own] + [send(own, at.moves_slow(g)) for g in range(1, at.group)]
            far = [send(own, at.moves_slow(g, 1)) for g in range(at.group)]
            row_rest, near = lax.optimization_barrier((row_rest, near))
            rests_across = across(row_rest)
        (row_sum,) = products(
            meta, both, jnp.concatenate(near + far, axis=0), (jnp.bfloat16,), n_row, False,
            after=far_sums,
        )
        if first:
            from_fast[-1], row_sum, row_scale, rests_across = lax.optimization_barrier(
                (from_fast[-1], row_sum, row_scale, rests_across)
            )
            scales_across = across(row_scale)
            scale = kept_of(row_scale, scales_across)
            now = kept_of(row_now, [
                tile.astype(jnp.float32) / factor + rest.astype(jnp.float32)
                for tile, factor, rest in zip(tiles_across, scales_across, rests_across)
            ])
        from_row = [row_sum] + [
            send(row_sum, at.moves_chip(d)) for d in range(1, at.chips)
        ]
        sums = [x + y.astype(jnp.float32) for x, y in zip(near_sums, from_fast)]
        total = sums[0]
        for g in range(1, at.group):
            total = total + send(
                sums[g].astype(jnp.bfloat16), at.moves_slow(g)
            ).astype(jnp.float32)
        for x in from_row:
            total = total + jnp.where(is_root, x, jnp.zeros_like(x)).astype(jnp.float32)
        message = total.astype(jnp.bfloat16)
        if last:
            total, now, scale = chunk_of(total, 0), chunk_of(now, 0), chunk_of(scale, 0)
            before = chunk_of(before, 0)
        applied = total
        for e in range(1, at.chips):
            if last:
                got = send(chunk_of(message, e), at.moves_slow(e * at.group))
            else:
                got = send(message, at.moves_slow(e * at.group))
                got = jnp.concatenate([chunk_of(got, k ^ e) for k in range(at.chips)], axis=0)
            applied = applied + got.astype(jnp.float32)
        mapped = scale * applied - center_shift * now
        if first:
            updated = mapped / half_width
        else:
            updated = 2.0 / half_width * mapped - before
        before = now
        now = updated
        if not last:
            own = (scale * now).astype(jnp.bfloat16)
    back = [
        send(now[swap * part:(swap + 1) * part], turned(at.moves_home(swap)))
        for swap in range(2)
    ]
    result = jnp.stack([jnp.where(core == k, back[0], back[1]) for k in range(2)])
    return result.transpose(0, 2, 1, 3).reshape(start_vectors.shape)


def solution(mesh):
    in_specs = (
        P(None, ("row", "col")),
        P(("row", "col")),
        P("row", "col", None, None, None),
        P("row", "col", None, None),
        P("row", "col"),
    )
    out_specs = P(None, ("row", "col"))
    return jax.shard_map(
        per_device, mesh=mesh, in_specs=in_specs, out_specs=out_specs, check_vma=False
    )
```

```python
import functools

import jax
import jax.numpy as jnp
from jax import lax
from jax.experimental import pallas as pl
from jax.experimental.pallas import tpu as pltpu
from jax.sharding import PartitionSpec as P

STEPS = 3

center_shift = 0.5
half_width = 3.0

UNROLL = 64
PACK = 4
VMEM_LIMIT = 16 * 1024 * 1024
AXES = ("row", "col")
PAD = 8


class Layout:
    def __init__(self, rows, cols):
        self.rows, self.cols = rows, cols
        self.chips = cols // 2
        self.fast = 2
        self.slow = rows // 2
        self.group = self.slow // self.chips
        assert self.group * self.chips * self.fast == rows

    def device(self, slow, fast, chip, core):
        return (slow * self.fast + fast) * self.cols + chip * 2 + core

    def home(self, chunk):
        chip, k = chunk // self.rows, chunk % self.rows
        e, f, t = k % self.chips, (k // self.chips) % self.fast, k // (self.chips * self.fast)
        return (chip ^ e) * self.group + t, f, chip

    def moves_home(self, swap):
        pairs = []
        for chunk in range(self.rows * self.chips):
            row, chip = chunk // self.chips, chunk % self.chips
            for core in range(2):
                source = row * self.cols + chip * 2 + core
                pairs.append((source, self.device(*self.home(chunk), core ^ swap)))
        return pairs

    def moves_slow(self, d, side=0):
        return [
            (self.device(s, f, c, q), self.device(s ^ d, f ^ side, c, q))
            for s in range(self.slow) for f in range(self.fast)
            for c in range(self.chips) for q in range(2)
        ]

    def moves_fast(self):
        return self.moves_slow(0, 1)

    def moves_chip(self, d, swap=0):
        return [
            (self.device(s, f, c, q), self.device(s, f, c ^ d, q ^ swap))
            for s in range(self.slow) for f in range(self.fast)
            for c in range(self.chips) for q in range(2)
        ]

    def moves_core(self):
        return [(i, i ^ 1) for i in range(self.rows * self.cols)]


def turned(pairs):
    return [(b, a) for a, b in pairs]


def live_groups(meta_ref, cap, which):
    return jnp.maximum((meta_ref[8 * cap + which] + (UNROLL - 1)) // UNROLL, 1)


def product_kernel(transpose, cap, n_out, after, meta_in, vecs_in, *refs):
    slab_refs, refs = refs[:2], refs[2 + after:]
    outs, refs = refs[:n_out], refs[n_out:]
    meta_ref, vecs_ref, slabs, acc, slab_sem, in_sem = refs
    base = 0 if transpose else 4 * cap

    def slab_copy(which, g):
        span = pl.ds(g * UNROLL, UNROLL)
        to = pl.ds(which * cap + g * UNROLL, UNROLL)
        sem = slab_sem.at[which * (cap // UNROLL) + g]
        return pltpu.make_async_copy(slab_refs[which].at[span], slabs.at[to], sem)

    def start_slab(which, g, carry):
        slab_copy(which, g).start()
        return carry

    meta_copy = pltpu.make_async_copy(meta_in, meta_ref, in_sem.at[0])
    vecs_copy = pltpu.make_async_copy(vecs_in, vecs_ref, in_sem.at[1])
    meta_copy.start()
    slab_copy(0, 0).start()
    vecs_copy.start()
    slab_copy(1, 0).start()
    acc[...] = jnp.zeros_like(acc)
    meta_copy.wait()
    groups = [live_groups(meta_ref, cap, which) for which in range(2)]
    for which in range(2):
        lax.fori_loop(1, groups[which], functools.partial(start_slab, which), 0)
    vecs_copy.wait()
    vec_count, block_len = vecs_ref.shape[1:]
    zero = jnp.zeros((vec_count, block_len), jnp.bfloat16)

    def body(which, g, carry):
        slab_copy(which, g).wait()
        start = which * cap + g * UNROLL
        products = []
        for u in range(0, UNROLL, PACK):
            v = [vecs_ref[meta_ref[base + start + u + k]] for k in range(PACK)]
            m = [slabs[start + u + k] for k in range(PACK)]
            left = jnp.concatenate([
                jnp.concatenate([v[0], zero, v[2], zero], axis=0),
                jnp.concatenate([zero, v[1], zero, v[3]], axis=0),
            ], axis=1)
            if transpose:
                halves = [jnp.concatenate(m[:2], axis=0), jnp.concatenate(m[2:], axis=0)]
                right, dims = jnp.concatenate(halves, axis=1), (((1,), (0,)), ((), ()))
            else:
                halves = [jnp.concatenate(m[:2], axis=1), jnp.concatenate(m[2:], axis=1)]
                right, dims = jnp.concatenate(halves, axis=0), (((1,), (1,)), ((), ()))
            products.append(
                lax.dot_general(left, right, dims, preferred_element_type=jnp.float32)
            )
        for u in range(UNROLL):
            k = u % PACK
            rows = slice(k * vec_count, (k + 1) * vec_count)
            lanes = slice((k // 2) * block_len, (k // 2 + 1) * block_len)
            acc[meta_ref[base + 2 * cap + start + u]] += products[u // PACK][rows, lanes]
        return carry

    for which in range(2):
        lax.fori_loop(0, groups[which], functools.partial(body, which), 0)
    size = outs[0].shape[0]
    for k, out in enumerate(outs):
        out[...] = acc[k * size:(k + 1) * size].astype(out.dtype)


def products(meta, slabs, vecs, out_dtypes, out_blocks, transpose, after=()):
    cap, block_len, _ = slabs[0].shape
    vec_count = vecs.shape[1]
    n_out = len(out_dtypes)
    total_out = out_blocks * n_out
    anywhere = pl.BlockSpec(memory_space=pl.ANY)
    vmem = pl.BlockSpec(memory_space=pltpu.VMEM)
    out_shape = [
        jax.ShapeDtypeStruct((out_blocks, vec_count, block_len), dtype) for dtype in out_dtypes
    ]
    return pl.pallas_call(
        functools.partial(product_kernel, transpose, cap, n_out, len(after)),
        in_specs=[anywhere] * (4 + len(after)),
        out_specs=[vmem] * n_out,
        out_shape=out_shape,
        scratch_shapes=[
            pltpu.SMEM(meta.shape, jnp.int32),
            pltpu.VMEM(vecs.shape, jnp.bfloat16),
            pltpu.VMEM((2 * cap, block_len, block_len), jnp.bfloat16),
            pltpu.VMEM((total_out + 1, vec_count, block_len), jnp.float32),
            pltpu.SemaphoreType.DMA((2 * cap // UNROLL,)),
            pltpu.SemaphoreType.DMA((2,)),
        ],
        compiler_params=pltpu.CompilerParams(vmem_limit_bytes=VMEM_LIMIT),
        cost_estimate=pl.CostEstimate(
            flops=4 * cap * vec_count * block_len * block_len,
            bytes_accessed=2 * vec_count * block_len * (vecs.shape[0] + total_out),
            transcendentals=0,
        ),
        name="transposed" if transpose else "direct",
    )(meta, vecs, *slabs, *after)


def per_device(start_vectors, scaling, block_values, block_places, block_counts):
    at = Layout(lax.axis_size("row"), lax.axis_size("col"))
    cap = block_values.shape[2]
    block_len = block_values.shape[-1]
    half = start_vectors.shape[0] // 2
    part = start_vectors.shape[1] // block_len
    per_chunk = 2 * part
    row_index = lax.axis_index("row").astype(jnp.int32)
    col_index = lax.axis_index("col").astype(jnp.int32)
    slow, fast = row_index // at.fast, row_index % at.fast
    chip, core = col_index // 2, col_index % 2
    root = slow // at.group
    is_root = chip == root
    def send(x, pairs):
        return lax.ppermute(x, AXES, pairs)

    slabs = block_values.reshape(cap, block_len, block_len)
    slots = jnp.concatenate([block_places.reshape(2 * cap), block_counts.reshape(1)])
    other_slabs = send(slabs, at.moves_core())

    halves = start_vectors.reshape(2, half, part, block_len).transpose(0, 2, 1, 3)
    scale_rows = jnp.broadcast_to(
        scaling.reshape(1, part, 1, block_len), (2, part, PAD, block_len)
    )
    halves = jnp.concatenate([halves, scale_rows], axis=2)
    packed = [
        jnp.where(core == swap, halves[0], halves[1]) for swap in range(2)
    ]
    pieces = [
        jnp.concatenate([
            packed[swap] if (d, swap) == (0, 0) else send(packed[swap], at.moves_chip(d, swap))
            for swap in range(2)
        ], axis=0)
        for d in range(at.chips)
    ]
    n_kept = at.chips * per_chunk

    def chunk_of(x, e):
        return x[e * per_chunk:(e + 1) * per_chunk]

    def pick(index, choices):
        x = choices[0]
        for d in range(1, len(choices)):
            x = jnp.where(index == d, choices[d], x)
        return x

    row_state = jnp.concatenate([pick(chip ^ e, pieces) for e in range(at.chips)], axis=0)

    other_slots = send(slots, at.moves_core())
    n_col = at.rows * per_chunk
    n_row = at.chips * per_chunk
    lists = []
    for which, held in enumerate((slots, other_slots)):
        row_block, col_block = held[:cap], held[cap:2 * cap]
        live = jnp.arange(cap, dtype=jnp.int32) < held[2 * cap]

        def inside(block):
            return ((block // part) ^ core) * part + block % part

        e = row_block // per_chunk
        row_at = e * per_chunk + inside(row_block % per_chunk)
        block = (core ^ which) * (n_col // 2) + col_block
        k = block // per_chunk
        e, f, t = k % at.chips, (k // at.chips) % at.fast, k // (at.chips * at.fast)
        d = slow ^ ((chip ^ e) * at.group + t)
        place = (d % at.group) * at.chips + d // at.group
        col_at = ((fast ^ f) * at.slow + place) * per_chunk + inside(block % per_chunk)
        lists.append((
            row_at, jnp.where(live, col_at, n_col), col_at, jnp.where(live, row_at, n_row)
        ))
    meta = jnp.concatenate(
        [jnp.concatenate([mine, theirs]) for mine, theirs in zip(*lists)]
        + [slots[2 * cap:], other_slots[2 * cap:], jnp.zeros(126, jnp.int32)]
    )

    row_state, meta, other_slabs = lax.optimization_barrier((row_state, meta, other_slabs))
    both = (slabs, other_slabs)

    def across(x):
        return [send(x, at.moves_slow(d * at.group)) for d in range(1, at.chips)]

    def kept_of(x, got):
        got = [
            jnp.concatenate([chunk_of(y, k ^ d) for k in range(at.chips)], axis=0)
            for d, y in enumerate(got, 1)
        ]
        return pick(chip ^ root, [x] + got)

    row_now, row_scale = row_state[:, :half], row_state[:, half:half + 1]
    row_tile = (row_scale * row_now).astype(jnp.bfloat16)
    tiles_across = across(row_tile)
    row_tile, row_state = lax.optimization_barrier((row_tile, row_state))
    row_now, row_scale = row_state[:, :half], row_state[:, half:half + 1]
    high = lax.optimization_barrier(row_scale.astype(jnp.bfloat16))
    low = lax.optimization_barrier(
        (row_scale - high.astype(jnp.float32)).astype(jnp.bfloat16)
    )

    def joined(high, low):
        return high.astype(jnp.float32) + low.astype(jnp.float32)

    row_rest = (
        row_now - row_tile.astype(jnp.float32) / joined(high, low)
    ).astype(jnp.bfloat16)
    row_rest = jnp.concatenate(
        [row_rest] + [jnp.broadcast_to(x, (n_kept, PAD, block_len)) for x in (high, low)],
        axis=1,
    )

    before = None
    for iterate in range(STEPS):
        first, last = iterate == 0, iterate == STEPS - 1
        if not first:
            row_tile = pick(
                chip ^ root,
                [own] + [send(own, at.moves_chip(d)) for d in range(1, at.chips)],
            )
        dtypes = (jnp.float32,) * at.group + (jnp.bfloat16,) * at.group
        if not first:
            near = [own] + [send(own, at.moves_slow(g)) for g in range(1, at.group)]
            far = [send(own, at.moves_slow(g, 1)) for g in range(at.group)]
        sums = products(meta, both, row_tile, dtypes, n_kept, True)
        near_sums, far_sums = list(sums[:at.group]), list(sums[at.group:])
        from_fast = [send(x, at.moves_fast()) for x in far_sums[::-1]][::-1]
        if first:
            tiles_across, far_sums = lax.optimization_barrier((tiles_across, far_sums))
            own = kept_of(row_tile, tiles_across)
            near = [own] + [send(own, at.moves_slow(g)) for g in range(1, at.group)]
            far = [send(own, at.moves_slow(g, 1)) for g in range(at.group)]
            row_rest, near = lax.optimization_barrier((row_rest, near))
            rests_across = across(row_rest)
        (row_sum,) = products(
            meta, both, jnp.concatenate(near + far, axis=0), (jnp.bfloat16,), n_row, False,
            after=far_sums,
        )
        if first:
            from_fast[-1], row_sum, rests_across = lax.optimization_barrier(
                (from_fast[-1], row_sum, rests_across)
            )
            scales = [
                joined(x[:, half:half + 1], x[:, half + PAD:half + PAD + 1])
                for x in rests_across
            ]
            scale = kept_of(row_scale, scales)
            now = kept_of(row_now, [
                tile.astype(jnp.float32) / factor + rest[:, :half].astype(jnp.float32)
                for tile, factor, rest in zip(tiles_across, scales, rests_across)
            ])
        from_row = [row_sum] + [
            send(row_sum, at.moves_chip(d)) for d in range(1, at.chips)
        ]
        sums = [x + y.astype(jnp.float32) for x, y in zip(near_sums, from_fast)]
        total = sums[0]
        for g in range(1, at.group):
            total = total + send(
                sums[g].astype(jnp.bfloat16), at.moves_slow(g)
            ).astype(jnp.float32)
        for x in from_row:
            total = total + jnp.where(is_root, x, jnp.zeros_like(x)).astype(jnp.float32)
        message = total.astype(jnp.bfloat16)
        if last:
            total, now, scale = chunk_of(total, 0), chunk_of(now, 0), chunk_of(scale, 0)
            before = chunk_of(before, 0)
        applied = total
        for e in range(1, at.chips):
            if last:
                got = send(chunk_of(message, e), at.moves_slow(e * at.group))
            else:
                got = send(message, at.moves_slow(e * at.group))
                got = jnp.concatenate([chunk_of(got, k ^ e) for k in range(at.chips)], axis=0)
            applied = applied + got.astype(jnp.float32)
        mapped = scale * applied - center_shift * now
        if first:
            updated = mapped / half_width
        else:
            updated = 2.0 / half_width * mapped - before
        before = now
        now = updated
        if not last:
            own = (scale * now).astype(jnp.bfloat16)
    back = [
        send(now[swap * part:(swap + 1) * part], turned(at.moves_home(swap)))
        for swap in range(2)
    ]
    result = jnp.stack([jnp.where(core == k, back[0], back[1]) for k in range(2)])
    return result.transpose(0, 2, 1, 3).reshape(start_vectors.shape)


def solution(mesh):
    in_specs = (
        P(None, ("row", "col")),
        P(("row", "col")),
        P("row", "col", None, None, None),
        P("row", "col", None, None),
        P("row", "col"),
    )
    out_specs = P(None, ("row", "col"))
    return jax.shard_map(
        per_device, mesh=mesh, in_specs=in_specs, out_specs=out_specs, check_vma=False
    )
```

```python
import functools

import jax
import jax.numpy as jnp
from jax import lax
from jax.experimental import pallas as pl
from jax.experimental.pallas import tpu as pltpu
from jax.sharding import PartitionSpec as P

STEPS = 3

center_shift = 0.5
half_width = 3.0

UNROLL = 32
PACK = 4
VMEM_LIMIT = 13 * 1024 * 1024
AXES = ("row", "col")
PAD = 8


class Layout:
    def __init__(self, rows, cols):
        self.rows, self.cols = rows, cols
        self.chips = cols // 2
        self.fast = 2
        self.slow = rows // 2
        self.group = self.slow // self.chips
        assert self.group * self.chips * self.fast == rows

    def device(self, slow, fast, chip, core):
        return (slow * self.fast + fast) * self.cols + chip * 2 + core

    def home(self, chunk):
        chip, k = chunk // self.rows, chunk % self.rows
        e, f, t = k % self.chips, (k // self.chips) % self.fast, k // (self.chips * self.fast)
        return (chip ^ e) * self.group + t, f, chip

    def moves_home(self, swap):
        pairs = []
        for chunk in range(self.rows * self.chips):
            row, chip = chunk // self.chips, chunk % self.chips
            for core in range(2):
                source = row * self.cols + chip * 2 + core
                pairs.append((source, self.device(*self.home(chunk), core ^ swap)))
        return pairs

    def moves_slow(self, d, side=0):
        return [
            (self.device(s, f, c, q), self.device(s ^ d, f ^ side, c, q))
            for s in range(self.slow) for f in range(self.fast)
            for c in range(self.chips) for q in range(2)
        ]

    def moves_fast(self):
        return self.moves_slow(0, 1)

    def moves_chip(self, d, swap=0):
        return [
            (self.device(s, f, c, q), self.device(s, f, c ^ d, q ^ swap))
            for s in range(self.slow) for f in range(self.fast)
            for c in range(self.chips) for q in range(2)
        ]

    def moves_core(self):
        return [(i, i ^ 1) for i in range(self.rows * self.cols)]


def turned(pairs):
    return [(b, a) for a, b in pairs]


def live_groups(meta_ref, cap, which):
    return jnp.maximum((meta_ref[8 * cap + which] + (UNROLL - 1)) // UNROLL, 1)


def product_kernel(transpose, cap, n_out, after, meta_in, vecs_in, *refs):
    slab_refs, refs = refs[:2], refs[2 + after:]
    outs, refs = refs[:n_out], refs[n_out:]
    meta_ref, vecs_ref, slabs, acc, slab_sem, in_sem = refs
    base = 0 if transpose else 4 * cap

    def slab_copy(which, g):
        span = pl.ds(g * UNROLL, UNROLL)
        to = pl.ds(which * cap + g * UNROLL, UNROLL)
        sem = slab_sem.at[which * (cap // UNROLL) + g]
        return pltpu.make_async_copy(slab_refs[which].at[span], slabs.at[to], sem)

    def start_slab(which, g, carry):
        slab_copy(which, g).start()
        return carry

    meta_copy = pltpu.make_async_copy(meta_in, meta_ref, in_sem.at[0])
    vecs_copy = pltpu.make_async_copy(vecs_in, vecs_ref, in_sem.at[1])
    meta_copy.start()
    slab_copy(0, 0).start()
    vecs_copy.start()
    slab_copy(1, 0).start()
    acc[...] = jnp.zeros_like(acc)
    meta_copy.wait()
    groups = [live_groups(meta_ref, cap, which) for which in range(2)]
    for which in range(2):
        lax.fori_loop(1, groups[which], functools.partial(start_slab, which), 0)
    vecs_copy.wait()
    vec_count, block_len = vecs_ref.shape[1:]
    zero = jnp.zeros((vec_count, block_len), jnp.bfloat16)

    def body(which, g, carry):
        slab_copy(which, g).wait()
        start = which * cap + g * UNROLL
        products = []
        for u in range(0, UNROLL, PACK):
            v = [vecs_ref[meta_ref[base + start + u + k]] for k in range(PACK)]
            m = [slabs[start + u + k] for k in range(PACK)]
            left = jnp.concatenate([
                jnp.concatenate([v[0], zero, v[2], zero], axis=0),
                jnp.concatenate([zero, v[1], zero, v[3]], axis=0),
            ], axis=1)
            if transpose:
                halves = [jnp.concatenate(m[:2], axis=0), jnp.concatenate(m[2:], axis=0)]
                right, dims = jnp.concatenate(halves, axis=1), (((1,), (0,)), ((), ()))
            else:
                halves = [jnp.concatenate(m[:2], axis=1), jnp.concatenate(m[2:], axis=1)]
                right, dims = jnp.concatenate(halves, axis=0), (((1,), (1,)), ((), ()))
            products.append(
                lax.dot_general(left, right, dims, preferred_element_type=jnp.float32)
            )
        for u in range(UNROLL):
            k = u % PACK
            rows = slice(k * vec_count, (k + 1) * vec_count)
            lanes = slice((k // 2) * block_len, (k // 2 + 1) * block_len)
            acc[meta_ref[base + 2 * cap + start + u]] += products[u // PACK][rows, lanes]
        return carry

    for which in range(2):
        lax.fori_loop(0, groups[which], functools.partial(body, which), 0)
    size = outs[0].shape[0]
    for k, out in enumerate(outs):
        out[...] = acc[k * size:(k + 1) * size].astype(out.dtype)


def products(meta, slabs, vecs, out_dtypes, out_blocks, transpose, after=()):
    cap, block_len, _ = slabs[0].shape
    vec_count = vecs.shape[1]
    n_out = len(out_dtypes)
    total_out = out_blocks * n_out
    anywhere = pl.BlockSpec(memory_space=pl.ANY)
    vmem = pl.BlockSpec(memory_space=pltpu.VMEM)
    out_shape = [
        jax.ShapeDtypeStruct((out_blocks, vec_count, block_len), dtype) for dtype in out_dtypes
    ]
    return pl.pallas_call(
        functools.partial(product_kernel, transpose, cap, n_out, len(after)),
        in_specs=[anywhere] * (4 + len(after)),
        out_specs=[vmem] * n_out,
        out_shape=out_shape,
        scratch_shapes=[
            pltpu.SMEM(meta.shape, jnp.int32),
            pltpu.VMEM(vecs.shape, jnp.bfloat16),
            pltpu.VMEM((2 * cap, block_len, block_len), jnp.bfloat16),
            pltpu.VMEM((total_out + 1, vec_count, block_len), jnp.float32),
            pltpu.SemaphoreType.DMA((2 * cap // UNROLL,)),
            pltpu.SemaphoreType.DMA((2,)),
        ],
        compiler_params=pltpu.CompilerParams(vmem_limit_bytes=VMEM_LIMIT),
        cost_estimate=pl.CostEstimate(
            flops=4 * cap * vec_count * block_len * block_len,
            bytes_accessed=2 * vec_count * block_len * (vecs.shape[0] + total_out),
            transcendentals=0,
        ),
        name="transposed" if transpose else "direct",
    )(meta, vecs, *slabs, *after)


def per_device(start_vectors, scaling, block_values, block_places, block_counts):
    at = Layout(lax.axis_size("row"), lax.axis_size("col"))
    cap = block_values.shape[2]
    block_len = block_values.shape[-1]
    half = start_vectors.shape[0] // 2
    part = start_vectors.shape[1] // block_len
    per_chunk = 2 * part
    row_index = lax.axis_index("row").astype(jnp.int32)
    col_index = lax.axis_index("col").astype(jnp.int32)
    slow, fast = row_index // at.fast, row_index % at.fast
    chip, core = col_index // 2, col_index % 2
    root = slow // at.group
    is_root = chip == root
    def send(x, pairs):
        return lax.ppermute(x, AXES, pairs)

    slabs = block_values.reshape(cap, block_len, block_len)
    slots = jnp.concatenate([block_places.reshape(2 * cap), block_counts.reshape(1)])
    other_slabs = send(slabs, at.moves_core())

    halves = start_vectors.reshape(2, half, part, block_len).transpose(0, 2, 1, 3)
    scale_rows = jnp.broadcast_to(
        scaling.reshape(1, part, 1, block_len), (2, part, PAD, block_len)
    )
    halves = jnp.concatenate([halves, scale_rows], axis=2)
    packed = [
        jnp.where(core == swap, halves[0], halves[1]) for swap in range(2)
    ]
    pieces = [
        jnp.concatenate([
            packed[swap] if (d, swap) == (0, 0) else send(packed[swap], at.moves_chip(d, swap))
            for swap in range(2)
        ], axis=0)
        for d in range(at.chips)
    ]
    n_kept = at.chips * per_chunk

    def chunk_of(x, e):
        return x[e * per_chunk:(e + 1) * per_chunk]

    def pick(index, choices):
        x = choices[0]
        for d in range(1, len(choices)):
            x = jnp.where(index == d, choices[d], x)
        return x

    row_state = jnp.concatenate([pick(chip ^ e, pieces) for e in range(at.chips)], axis=0)

    other_slots = send(slots, at.moves_core())
    n_col = at.rows * per_chunk
    n_row = at.chips * per_chunk
    lists = []
    for which, held in enumerate((slots, other_slots)):
        row_block, col_block = held[:cap], held[cap:2 * cap]
        live = jnp.arange(cap, dtype=jnp.int32) < held[2 * cap]

        def inside(block):
            return ((block // part) ^ core) * part + block % part

        e = row_block // per_chunk
        row_at = e * per_chunk + inside(row_block % per_chunk)
        block = (core ^ which) * (n_col // 2) + col_block
        k = block // per_chunk
        e, f, t = k % at.chips, (k // at.chips) % at.fast, k // (at.chips * at.fast)
        d = slow ^ ((chip ^ e) * at.group + t)
        place = (d % at.group) * at.chips + d // at.group
        col_at = ((fast ^ f) * at.slow + place) * per_chunk + inside(block % per_chunk)
        lists.append((
            row_at, jnp.where(live, col_at, n_col), col_at, jnp.where(live, row_at, n_row)
        ))
    meta = jnp.concatenate(
        [jnp.concatenate([mine, theirs]) for mine, theirs in zip(*lists)]
        + [slots[2 * cap:], other_slots[2 * cap:], jnp.zeros(126, jnp.int32)]
    )

    row_state, meta, other_slabs = lax.optimization_barrier((row_state, meta, other_slabs))
    both = (slabs, other_slabs)

    def across(x):
        return [send(x, at.moves_slow(d * at.group)) for d in range(1, at.chips)]

    def kept_of(x, got):
        got = [
            jnp.concatenate([chunk_of(y, k ^ d) for k in range(at.chips)], axis=0)
            for d, y in enumerate(got, 1)
        ]
        return pick(chip ^ root, [x] + got)

    row_now, row_scale = row_state[:, :half], row_state[:, half:half + 1]
    row_tile = (row_scale * row_now).astype(jnp.bfloat16)
    tiles_across = across(row_tile)
    row_tile, row_state = lax.optimization_barrier((row_tile, row_state))
    row_now, row_scale = row_state[:, :half], row_state[:, half:half + 1]
    high = lax.optimization_barrier(row_scale.astype(jnp.bfloat16))
    low = lax.optimization_barrier(
        (row_scale - high.astype(jnp.float32)).astype(jnp.bfloat16)
    )

    def joined(high, low):
        return high.astype(jnp.float32) + low.astype(jnp.float32)

    row_rest = (
        row_now - row_tile.astype(jnp.float32) / joined(high, low)
    ).astype(jnp.bfloat16)
    row_rest = jnp.concatenate(
        [row_rest] + [jnp.broadcast_to(x, (n_kept, PAD, block_len)) for x in (high, low)],
        axis=1,
    )

    before = None
    for iterate in range(STEPS):
        first, last = iterate == 0, iterate == STEPS - 1
        if not first:
            row_tile = pick(
                chip ^ root,
                [own] + [send(own, at.moves_chip(d)) for d in range(1, at.chips)],
            )
        dtypes = (jnp.float32,) * at.group + (jnp.bfloat16,) * at.group
        if not first:
            near = [own] + [send(own, at.moves_slow(g)) for g in range(1, at.group)]
            far = [send(own, at.moves_slow(g, 1)) for g in range(at.group)]
        sums = products(meta, both, row_tile, dtypes, n_kept, True)
        near_sums, far_sums = list(sums[:at.group]), list(sums[at.group:])
        from_fast = [send(x, at.moves_fast()) for x in far_sums[::-1]][::-1]
        if first:
            tiles_across, far_sums = lax.optimization_barrier((tiles_across, far_sums))
            own = kept_of(row_tile, tiles_across)
            near = [own] + [send(own, at.moves_slow(g)) for g in range(1, at.group)]
            far = [send(own, at.moves_slow(g, 1)) for g in range(at.group)]
            row_rest, near = lax.optimization_barrier((row_rest, near))
            rests_across = across(row_rest)
        (row_sum,) = products(
            meta, both, jnp.concatenate(near + far, axis=0), (jnp.bfloat16,), n_row, False,
            after=far_sums,
        )
        if first:
            from_fast[-1], row_sum, rests_across = lax.optimization_barrier(
                (from_fast[-1], row_sum, rests_across)
            )
            scales = [
                joined(x[:, half:half + 1], x[:, half + PAD:half + PAD + 1])
                for x in rests_across
            ]
            scale = kept_of(row_scale, scales)
            now = kept_of(row_now, [
                tile.astype(jnp.float32) / factor + rest[:, :half].astype(jnp.float32)
                for tile, factor, rest in zip(tiles_across, scales, rests_across)
            ])
        from_row = [row_sum] + [
            send(row_sum, at.moves_chip(d)) for d in range(1, at.chips)
        ]
        sums = [x + y.astype(jnp.float32) for x, y in zip(near_sums, from_fast)]
        total = sums[0]
        for g in range(1, at.group):
            total = total + send(
                sums[g].astype(jnp.bfloat16), at.moves_slow(g)
            ).astype(jnp.float32)
        for x in from_row:
            total = total + jnp.where(is_root, x, jnp.zeros_like(x)).astype(jnp.float32)
        message = total.astype(jnp.bfloat16)
        if last:
            total, now, scale = chunk_of(total, 0), chunk_of(now, 0), chunk_of(scale, 0)
            before = chunk_of(before, 0)
        applied = total
        for e in range(1, at.chips):
            if last:
                got = send(chunk_of(message, e), at.moves_slow(e * at.group))
            else:
                got = send(message, at.moves_slow(e * at.group))
                got = jnp.concatenate([chunk_of(got, k ^ e) for k in range(at.chips)], axis=0)
            applied = applied + got.astype(jnp.float32)
        mapped = scale * applied - center_shift * now
        if first:
            updated = mapped / half_width
        else:
            updated = 2.0 / half_width * mapped - before
        before = now
        now = updated
        if not last:
            own = (scale * now).astype(jnp.bfloat16)
    back = [
        send(now[swap * part:(swap + 1) * part], turned(at.moves_home(swap)))
        for swap in range(2)
    ]
    result = jnp.stack([jnp.where(core == k, back[0], back[1]) for k in range(2)])
    return result.transpose(0, 2, 1, 3).reshape(start_vectors.shape)


def solution(mesh):
    in_specs = (
        P(None, ("row", "col")),
        P(("row", "col")),
        P("row", "col", None, None, None),
        P("row", "col", None, None),
        P("row", "col"),
    )
    out_specs = P(None, ("row", "col"))
    return jax.shard_map(
        per_device, mesh=mesh, in_specs=in_specs, out_specs=out_specs, check_vma=False
    )
```

```python
import functools

import jax
import jax.numpy as jnp
from jax import lax
from jax.experimental import pallas as pl
from jax.experimental.pallas import tpu as pltpu
from jax.sharding import PartitionSpec as P

STEPS = 3

center_shift = 0.5
half_width = 3.0

CHUNK = 32
PACK = 4
VMEM_LIMIT = 13 * 1024 * 1024
AXES = ("row", "col")
PAD = 8


class Layout:
    def __init__(self, rows, cols):
        self.rows, self.cols = rows, cols
        self.chips = cols // 2
        self.fast = 2
        self.slow = rows // 2
        self.group = self.slow // self.chips
        assert self.group * self.chips * self.fast == rows

    def device(self, slow, fast, chip, core):
        return (slow * self.fast + fast) * self.cols + chip * 2 + core

    def home(self, chunk):
        chip, k = chunk // self.rows, chunk % self.rows
        e, f, t = k % self.chips, (k // self.chips) % self.fast, k // (self.chips * self.fast)
        return (chip ^ e) * self.group + t, f, chip

    def moves_home(self, swap):
        pairs = []
        for chunk in range(self.rows * self.chips):
            row, chip = chunk // self.chips, chunk % self.chips
            for core in range(2):
                source = row * self.cols + chip * 2 + core
                pairs.append((source, self.device(*self.home(chunk), core ^ swap)))
        return pairs

    def moves_slow(self, d, side=0):
        return [
            (self.device(s, f, c, q), self.device(s ^ d, f ^ side, c, q))
            for s in range(self.slow) for f in range(self.fast)
            for c in range(self.chips) for q in range(2)
        ]

    def moves_fast(self):
        return self.moves_slow(0, 1)

    def moves_chip(self, d, swap=0):
        return [
            (self.device(s, f, c, q), self.device(s, f, c ^ d, q ^ swap))
            for s in range(self.slow) for f in range(self.fast)
            for c in range(self.chips) for q in range(2)
        ]

    def moves_core(self):
        return [(i, i ^ 1) for i in range(self.rows * self.cols)]


def turned(pairs):
    return [(b, a) for a, b in pairs]


def live_groups(meta_ref, cap, which):
    return jnp.maximum((meta_ref[8 * cap + which] + (CHUNK - 1)) // CHUNK, 1)


def product_kernel(transpose, cap, n_out, after, meta_in, vecs_in, *refs):
    slab_refs, refs = refs[:2], refs[2 + after:]
    outs, refs = refs[:n_out], refs[n_out:]
    meta_ref, vecs_ref, slabs, acc, slab_sem, in_sem = refs
    base = 0 if transpose else 4 * cap

    def slab_copy(which, g):
        span = pl.ds(g * CHUNK, CHUNK)
        to = pl.ds(which * cap + g * CHUNK, CHUNK)
        sem = slab_sem.at[which * (cap // CHUNK) + g]
        return pltpu.make_async_copy(slab_refs[which].at[span], slabs.at[to], sem)

    def start_slab(which, g, carry):
        slab_copy(which, g).start()
        return carry

    meta_copy = pltpu.make_async_copy(meta_in, meta_ref, in_sem.at[0])
    vecs_copy = pltpu.make_async_copy(vecs_in, vecs_ref, in_sem.at[1])
    meta_copy.start()
    slab_copy(0, 0).start()
    vecs_copy.start()
    slab_copy(1, 0).start()
    acc[...] = jnp.zeros_like(acc)
    meta_copy.wait()
    groups = [live_groups(meta_ref, cap, which) for which in range(2)]
    for which in range(2):
        lax.fori_loop(1, groups[which], functools.partial(start_slab, which), 0)
    vecs_copy.wait()
    vec_count, block_len = vecs_ref.shape[1:]
    zero = jnp.zeros((vec_count, block_len), jnp.bfloat16)

    def work(which, chunk, chunks):
        for k in range(chunks):
            slab_copy(which, chunk + k).wait()
        start = which * cap + chunk * CHUNK
        products = []
        for u in range(0, chunks * CHUNK, PACK):
            v = [vecs_ref[meta_ref[base + start + u + k]] for k in range(PACK)]
            m = [slabs[start + u + k] for k in range(PACK)]
            left = jnp.concatenate([
                jnp.concatenate([v[0], zero, v[2], zero], axis=0),
                jnp.concatenate([zero, v[1], zero, v[3]], axis=0),
            ], axis=1)
            if transpose:
                halves = [jnp.concatenate(m[:2], axis=0), jnp.concatenate(m[2:], axis=0)]
                right, dims = jnp.concatenate(halves, axis=1), (((1,), (0,)), ((), ()))
            else:
                halves = [jnp.concatenate(m[:2], axis=1), jnp.concatenate(m[2:], axis=1)]
                right, dims = jnp.concatenate(halves, axis=0), (((1,), (1,)), ((), ()))
            products.append(
                lax.dot_general(left, right, dims, preferred_element_type=jnp.float32)
            )
        for u in range(chunks * CHUNK):
            k = u % PACK
            rows = slice(k * vec_count, (k + 1) * vec_count)
            lanes = slice((k // 2) * block_len, (k // 2 + 1) * block_len)
            acc[meta_ref[base + 2 * cap + start + u]] += products[u // PACK][rows, lanes]

    def two(which, g, carry):
        work(which, 2 * g, 2)
        return carry

    for which in range(2):
        lax.fori_loop(0, groups[which] // 2, functools.partial(two, which), 0)

        @pl.when(groups[which] % 2 == 1)
        def _():
            work(which, groups[which] - 1, 1)

    size = outs[0].shape[0]
    for k, out in enumerate(outs):
        out[...] = acc[k * size:(k + 1) * size].astype(out.dtype)


def products(meta, slabs, vecs, out_dtypes, out_blocks, transpose, after=()):
    cap, block_len, _ = slabs[0].shape
    vec_count = vecs.shape[1]
    n_out = len(out_dtypes)
    total_out = out_blocks * n_out
    anywhere = pl.BlockSpec(memory_space=pl.ANY)
    vmem = pl.BlockSpec(memory_space=pltpu.VMEM)
    out_shape = [
        jax.ShapeDtypeStruct((out_blocks, vec_count, block_len), dtype) for dtype in out_dtypes
    ]
    return pl.pallas_call(
        functools.partial(product_kernel, transpose, cap, n_out, len(after)),
        in_specs=[anywhere] * (4 + len(after)),
        out_specs=[vmem] * n_out,
        out_shape=out_shape,
        scratch_shapes=[
            pltpu.SMEM(meta.shape, jnp.int32),
            pltpu.VMEM(vecs.shape, jnp.bfloat16),
            pltpu.VMEM((2 * cap, block_len, block_len), jnp.bfloat16),
            pltpu.VMEM((total_out + 1, vec_count, block_len), jnp.float32),
            pltpu.SemaphoreType.DMA((2 * cap // CHUNK,)),
            pltpu.SemaphoreType.DMA((2,)),
        ],
        compiler_params=pltpu.CompilerParams(vmem_limit_bytes=VMEM_LIMIT),
        cost_estimate=pl.CostEstimate(
            flops=4 * cap * vec_count * block_len * block_len,
            bytes_accessed=2 * vec_count * block_len * (vecs.shape[0] + total_out),
            transcendentals=0,
        ),
        name="transposed" if transpose else "direct",
    )(meta, vecs, *slabs, *after)


def per_device(start_vectors, scaling, block_values, block_places, block_counts):
    at = Layout(lax.axis_size("row"), lax.axis_size("col"))
    cap = block_values.shape[2]
    block_len = block_values.shape[-1]
    half = start_vectors.shape[0] // 2
    part = start_vectors.shape[1] // block_len
    per_chunk = 2 * part
    row_index = lax.axis_index("row").astype(jnp.int32)
    col_index = lax.axis_index("col").astype(jnp.int32)
    slow, fast = row_index // at.fast, row_index % at.fast
    chip, core = col_index // 2, col_index % 2
    root = slow // at.group
    is_root = chip == root
    def send(x, pairs):
        return lax.ppermute(x, AXES, pairs)

    slabs = block_values.reshape(cap, block_len, block_len)
    slots = jnp.concatenate([block_places.reshape(2 * cap), block_counts.reshape(1)])
    other_slabs = send(slabs, at.moves_core())

    halves = start_vectors.reshape(2, half, part, block_len).transpose(0, 2, 1, 3)
    scale_rows = jnp.broadcast_to(
        scaling.reshape(1, part, 1, block_len), (2, part, PAD, block_len)
    )
    halves = jnp.concatenate([halves, scale_rows], axis=2)
    packed = [
        jnp.where(core == swap, halves[0], halves[1]) for swap in range(2)
    ]
    pieces = [
        jnp.concatenate([
            packed[swap] if (d, swap) == (0, 0) else send(packed[swap], at.moves_chip(d, swap))
            for swap in range(2)
        ], axis=0)
        for d in range(at.chips)
    ]
    n_kept = at.chips * per_chunk

    def chunk_of(x, e):
        return x[e * per_chunk:(e + 1) * per_chunk]

    def pick(index, choices):
        x = choices[0]
        for d in range(1, len(choices)):
            x = jnp.where(index == d, choices[d], x)
        return x

    row_state = jnp.concatenate([pick(chip ^ e, pieces) for e in range(at.chips)], axis=0)

    other_slots = send(slots, at.moves_core())
    both = (slabs, other_slabs)

    def across(x):
        return [send(x, at.moves_slow(d * at.group)) for d in range(1, at.chips)]

    def kept_of(x, got):
        got = [
            jnp.concatenate([chunk_of(y, k ^ d) for k in range(at.chips)], axis=0)
            for d, y in enumerate(got, 1)
        ]
        return pick(chip ^ root, [x] + got)

    row_now, row_scale = row_state[:, :half], row_state[:, half:half + 1]
    row_tile = (row_scale * row_now).astype(jnp.bfloat16)
    row_tile, slots, other_slots = lax.optimization_barrier((row_tile, slots, other_slots))
    tiles_across = across(row_tile)

    n_col = at.rows * per_chunk
    n_row = at.chips * per_chunk
    lists = []
    for which, held in enumerate((slots, other_slots)):
        row_block, col_block = held[:cap], held[cap:2 * cap]
        live = jnp.arange(cap, dtype=jnp.int32) < held[2 * cap]

        def inside(block):
            return ((block // part) ^ core) * part + block % part

        e = row_block // per_chunk
        row_at = e * per_chunk + inside(row_block % per_chunk)
        block = (core ^ which) * (n_col // 2) + col_block
        k = block // per_chunk
        e, f, t = k % at.chips, (k // at.chips) % at.fast, k // (at.chips * at.fast)
        d = slow ^ ((chip ^ e) * at.group + t)
        place = (d % at.group) * at.chips + d // at.group
        col_at = ((fast ^ f) * at.slow + place) * per_chunk + inside(block % per_chunk)
        lists.append((
            row_at, jnp.where(live, col_at, n_col), col_at, jnp.where(live, row_at, n_row)
        ))
    meta = jnp.concatenate(
        [jnp.concatenate([mine, theirs]) for mine, theirs in zip(*lists)]
        + [slots[2 * cap:], other_slots[2 * cap:], jnp.zeros(126, jnp.int32)]
    )

    row_tile, row_state = lax.optimization_barrier((row_tile, row_state))
    row_now, row_scale = row_state[:, :half], row_state[:, half:half + 1]
    high = lax.optimization_barrier(row_scale.astype(jnp.bfloat16))
    low = lax.optimization_barrier(
        (row_scale - high.astype(jnp.float32)).astype(jnp.bfloat16)
    )

    def joined(high, low):
        return high.astype(jnp.float32) + low.astype(jnp.float32)

    row_rest = (
        row_now - row_tile.astype(jnp.float32) / joined(high, low)
    ).astype(jnp.bfloat16)
    row_rest = jnp.concatenate(
        [row_rest] + [jnp.broadcast_to(x, (n_kept, PAD, block_len)) for x in (high, low)],
        axis=1,
    )

    before = None
    for iterate in range(STEPS):
        first, last = iterate == 0, iterate == STEPS - 1
        if not first:
            row_tile = pick(
                chip ^ root,
                [own] + [send(own, at.moves_chip(d)) for d in range(1, at.chips)],
            )
        dtypes = (jnp.float32,) * at.group + (jnp.bfloat16,) * at.group
        if not first:
            near = [own] + [send(own, at.moves_slow(g)) for g in range(1, at.group)]
            far = [send(own, at.moves_slow(g, 1)) for g in range(at.group)]
        sums = products(meta, both, row_tile, dtypes, n_kept, True)
        near_sums, far_sums = list(sums[:at.group]), list(sums[at.group:])
        from_fast = [send(x, at.moves_fast()) for x in far_sums[::-1]][::-1]
        if first:
            tiles_across, far_sums = lax.optimization_barrier((tiles_across, far_sums))
            own = kept_of(row_tile, tiles_across)
            near = [own] + [send(own, at.moves_slow(g)) for g in range(1, at.group)]
            far = [send(own, at.moves_slow(g, 1)) for g in range(at.group)]
            row_rest, near = lax.optimization_barrier((row_rest, near))
            rests_across = across(row_rest)
        (row_sum,) = products(
            meta, both, jnp.concatenate(near + far, axis=0), (jnp.bfloat16,), n_row, False,
            after=far_sums,
        )
        if first:
            from_fast[-1], row_sum, rests_across = lax.optimization_barrier(
                (from_fast[-1], row_sum, rests_across)
            )
            scales = [
                joined(x[:, half:half + 1], x[:, half + PAD:half + PAD + 1])
                for x in rests_across
            ]
            scale = kept_of(row_scale, scales)
            now = kept_of(row_now, [
                tile.astype(jnp.float32) / factor + rest[:, :half].astype(jnp.float32)
                for tile, factor, rest in zip(tiles_across, scales, rests_across)
            ])
        from_row = [row_sum] + [
            send(row_sum, at.moves_chip(d)) for d in range(1, at.chips)
        ]
        sums = [x + y.astype(jnp.float32) for x, y in zip(near_sums, from_fast)]
        total = sums[0]
        for g in range(1, at.group):
            total = total + send(
                sums[g].astype(jnp.bfloat16), at.moves_slow(g)
            ).astype(jnp.float32)
        for x in from_row:
            total = total + jnp.where(is_root, x, jnp.zeros_like(x)).astype(jnp.float32)
        message = total.astype(jnp.bfloat16)
        if last:
            total, now, scale = chunk_of(total, 0), chunk_of(now, 0), chunk_of(scale, 0)
            before = chunk_of(before, 0)
        applied = total
        for e in range(1, at.chips):
            if last:
                got = send(chunk_of(message, e), at.moves_slow(e * at.group))
            else:
                got = send(message, at.moves_slow(e * at.group))
                got = jnp.concatenate([chunk_of(got, k ^ e) for k in range(at.chips)], axis=0)
            applied = applied + got.astype(jnp.float32)
        mapped = scale * applied - center_shift * now
        if first:
            updated = mapped / half_width
        else:
            updated = 2.0 / half_width * mapped - before
        before = now
        now = updated
        if not last:
            own = (scale * now).astype(jnp.bfloat16)
    back = [
        send(now[swap * part:(swap + 1) * part], turned(at.moves_home(swap)))
        for swap in range(2)
    ]
    result = jnp.stack([jnp.where(core == k, back[0], back[1]) for k in range(2)])
    return result.transpose(0, 2, 1, 3).reshape(start_vectors.shape)


def solution(mesh):
    in_specs = (
        P(None, ("row", "col")),
        P(("row", "col")),
        P("row", "col", None, None, None),
        P("row", "col", None, None),
        P("row", "col"),
    )
    out_specs = P(None, ("row", "col"))
    return jax.shard_map(
        per_device, mesh=mesh, in_specs=in_specs, out_specs=out_specs, check_vma=False
    )
```

```python
import functools

import jax
import jax.numpy as jnp
from jax import lax
from jax.experimental import pallas as pl
from jax.experimental.pallas import tpu as pltpu
from jax.sharding import PartitionSpec as P

STEPS = 3

center_shift = 0.5
half_width = 3.0

CHUNK = 32
PACK = 4
VMEM_LIMIT = 13 * 1024 * 1024
AXES = ("row", "col")
PAD = 8


class Layout:
    def __init__(self, rows, cols):
        self.rows, self.cols = rows, cols
        self.chips = cols // 2
        self.fast = 2
        self.slow = rows // 2
        self.group = self.slow // self.chips
        assert self.group * self.chips * self.fast == rows

    def device(self, slow, fast, chip, core):
        return (slow * self.fast + fast) * self.cols + chip * 2 + core

    def home(self, chunk):
        chip, k = chunk // self.rows, chunk % self.rows
        e, f, t = k % self.chips, (k // self.chips) % self.fast, k // (self.chips * self.fast)
        return (chip ^ e) * self.group + t, f, chip

    def moves_home(self, swap):
        pairs = []
        for chunk in range(self.rows * self.chips):
            row, chip = chunk // self.chips, chunk % self.chips
            for core in range(2):
                source = row * self.cols + chip * 2 + core
                pairs.append((source, self.device(*self.home(chunk), core ^ swap)))
        return pairs

    def moves_slow(self, d, side=0):
        return [
            (self.device(s, f, c, q), self.device(s ^ d, f ^ side, c, q))
            for s in range(self.slow) for f in range(self.fast)
            for c in range(self.chips) for q in range(2)
        ]

    def moves_fast(self):
        return self.moves_slow(0, 1)

    def moves_chip(self, d, swap=0):
        return [
            (self.device(s, f, c, q), self.device(s, f, c ^ d, q ^ swap))
            for s in range(self.slow) for f in range(self.fast)
            for c in range(self.chips) for q in range(2)
        ]

    def moves_core(self):
        return [(i, i ^ 1) for i in range(self.rows * self.cols)]


def turned(pairs):
    return [(b, a) for a, b in pairs]


def live_groups(meta_ref, cap, which):
    return jnp.maximum((meta_ref[8 * cap + which] + (CHUNK - 1)) // CHUNK, 1)


def product_kernel(transpose, cap, n_out, after, meta_in, vecs_in, *refs):
    slab_refs, refs = refs[:2], refs[2 + after:]
    outs, refs = refs[:n_out], refs[n_out:]
    meta_ref, vecs_ref, slabs, acc, slab_sem, in_sem = refs
    base = 0 if transpose else 4 * cap

    def slab_copy(which, g):
        span = pl.ds(g * CHUNK, CHUNK)
        to = pl.ds(which * cap + g * CHUNK, CHUNK)
        sem = slab_sem.at[which * (cap // CHUNK) + g]
        return pltpu.make_async_copy(slab_refs[which].at[span], slabs.at[to], sem)

    def start_slab(which, g, carry):
        slab_copy(which, g).start()
        return carry

    meta_copy = pltpu.make_async_copy(meta_in, meta_ref, in_sem.at[0])
    vecs_copy = pltpu.make_async_copy(vecs_in, vecs_ref, in_sem.at[1])
    meta_copy.start()
    slab_copy(0, 0).start()
    vecs_copy.start()
    slab_copy(1, 0).start()
    acc[...] = jnp.zeros_like(acc)
    meta_copy.wait()
    groups = [live_groups(meta_ref, cap, which) for which in range(2)]
    for which in range(2):
        lax.fori_loop(1, groups[which], functools.partial(start_slab, which), 0)
    vecs_copy.wait()
    vec_count, block_len = vecs_ref.shape[1:]
    zero = jnp.zeros((vec_count, block_len), jnp.bfloat16)

    def work(which, chunk, chunks):
        for k in range(chunks):
            slab_copy(which, chunk + k).wait()
        start = which * cap + chunk * CHUNK
        products = []
        for u in range(0, chunks * CHUNK, PACK):
            v = [vecs_ref[meta_ref[base + start + u + k]] for k in range(PACK)]
            m = [slabs[start + u + k] for k in range(PACK)]
            left = jnp.concatenate([
                jnp.concatenate([v[0], zero, v[2], zero], axis=0),
                jnp.concatenate([zero, v[1], zero, v[3]], axis=0),
            ], axis=1)
            if transpose:
                halves = [jnp.concatenate(m[:2], axis=0), jnp.concatenate(m[2:], axis=0)]
                right, dims = jnp.concatenate(halves, axis=1), (((1,), (0,)), ((), ()))
            else:
                halves = [jnp.concatenate(m[:2], axis=1), jnp.concatenate(m[2:], axis=1)]
                right, dims = jnp.concatenate(halves, axis=0), (((1,), (1,)), ((), ()))
            products.append(
                lax.dot_general(left, right, dims, preferred_element_type=jnp.float32)
            )
        for u in range(chunks * CHUNK):
            k = u % PACK
            rows = slice(k * vec_count, (k + 1) * vec_count)
            lanes = slice((k // 2) * block_len, (k // 2 + 1) * block_len)
            acc[meta_ref[base + 2 * cap + start + u]] += products[u // PACK][rows, lanes]

    def two(which, g, carry):
        work(which, 2 * g, 2)
        return carry

    for which in range(2):
        lax.fori_loop(0, groups[which] // 2, functools.partial(two, which), 0)

        @pl.when(groups[which] % 2 == 1)
        def _():
            work(which, groups[which] - 1, 1)

    size = outs[0].shape[0]
    for k, out in enumerate(outs):
        out[...] = acc[k * size:(k + 1) * size].astype(out.dtype)


def products(meta, slabs, vecs, out_dtypes, out_blocks, transpose, after=()):
    cap, block_len, _ = slabs[0].shape
    vec_count = vecs.shape[1]
    n_out = len(out_dtypes)
    total_out = out_blocks * n_out
    anywhere = pl.BlockSpec(memory_space=pl.ANY)
    vmem = pl.BlockSpec(memory_space=pltpu.VMEM)
    out_shape = [
        jax.ShapeDtypeStruct((out_blocks, vec_count, block_len), dtype) for dtype in out_dtypes
    ]
    return pl.pallas_call(
        functools.partial(product_kernel, transpose, cap, n_out, len(after)),
        in_specs=[anywhere] * (4 + len(after)),
        out_specs=[vmem] * n_out,
        out_shape=out_shape,
        scratch_shapes=[
            pltpu.SMEM(meta.shape, jnp.int32),
            pltpu.VMEM(vecs.shape, jnp.bfloat16),
            pltpu.VMEM((2 * cap, block_len, block_len), jnp.bfloat16),
            pltpu.VMEM((total_out + 1, vec_count, block_len), jnp.float32),
            pltpu.SemaphoreType.DMA((2 * cap // CHUNK,)),
            pltpu.SemaphoreType.DMA((2,)),
        ],
        compiler_params=pltpu.CompilerParams(vmem_limit_bytes=VMEM_LIMIT),
        cost_estimate=pl.CostEstimate(
            flops=4 * cap * vec_count * block_len * block_len,
            bytes_accessed=2 * vec_count * block_len * (vecs.shape[0] + total_out),
            transcendentals=0,
        ),
        name="transposed" if transpose else "direct",
    )(meta, vecs, *slabs, *after)


def per_device(start_vectors, scaling, block_values, block_places, block_counts):
    at = Layout(lax.axis_size("row"), lax.axis_size("col"))
    cap = block_values.shape[2]
    block_len = block_values.shape[-1]
    half = start_vectors.shape[0] // 2
    part = start_vectors.shape[1] // block_len
    per_chunk = 2 * part
    row_index = lax.axis_index("row").astype(jnp.int32)
    col_index = lax.axis_index("col").astype(jnp.int32)
    slow, fast = row_index // at.fast, row_index % at.fast
    chip, core = col_index // 2, col_index % 2
    root = slow // at.group
    is_root = chip == root
    def send(x, pairs):
        return lax.ppermute(x, AXES, pairs)

    slabs = block_values.reshape(cap, block_len, block_len)
    slots = jnp.concatenate([block_places.reshape(2 * cap), block_counts.reshape(1)])
    other_slabs = send(slabs, at.moves_core())

    halves = start_vectors.reshape(2, half, part, block_len).transpose(0, 2, 1, 3)
    scale_rows = jnp.broadcast_to(
        scaling.reshape(1, part, 1, block_len), (2, part, PAD, block_len)
    )
    halves = jnp.concatenate([halves, scale_rows], axis=2)
    packed = [
        jnp.where(core == swap, halves[0], halves[1]) for swap in range(2)
    ]
    pieces = [
        jnp.concatenate([
            packed[swap] if (d, swap) == (0, 0) else send(packed[swap], at.moves_chip(d, swap))
            for swap in range(2)
        ], axis=0)
        for d in range(at.chips)
    ]
    n_kept = at.chips * per_chunk

    def chunk_of(x, e):
        return x[e * per_chunk:(e + 1) * per_chunk]

    def pick(index, choices):
        x = choices[0]
        for d in range(1, len(choices)):
            x = jnp.where(index == d, choices[d], x)
        return x

    row_state = jnp.concatenate([pick(chip ^ e, pieces) for e in range(at.chips)], axis=0)

    other_slots = send(slots, at.moves_core())
    n_col = at.rows * per_chunk
    n_row = at.chips * per_chunk
    lists = []
    for which, held in enumerate((slots, other_slots)):
        row_block, col_block = held[:cap], held[cap:2 * cap]
        live = jnp.arange(cap, dtype=jnp.int32) < held[2 * cap]

        def inside(block):
            return ((block // part) ^ core) * part + block % part

        e = row_block // per_chunk
        row_at = e * per_chunk + inside(row_block % per_chunk)
        block = (core ^ which) * (n_col // 2) + col_block
        k = block // per_chunk
        e, f, t = k % at.chips, (k // at.chips) % at.fast, k // (at.chips * at.fast)
        d = slow ^ ((chip ^ e) * at.group + t)
        place = (d % at.group) * at.chips + d // at.group
        col_at = ((fast ^ f) * at.slow + place) * per_chunk + inside(block % per_chunk)
        lists.append((
            row_at, jnp.where(live, col_at, n_col), col_at, jnp.where(live, row_at, n_row)
        ))
    meta = jnp.concatenate(
        [jnp.concatenate([mine, theirs]) for mine, theirs in zip(*lists)]
        + [slots[2 * cap:], other_slots[2 * cap:], jnp.zeros(126, jnp.int32)]
    )

    row_state, meta, other_slabs = lax.optimization_barrier((row_state, meta, other_slabs))
    both = (slabs, other_slabs)

    def across(x):
        return [send(x, at.moves_slow(d * at.group)) for d in range(1, at.chips)]

    def kept_of(x, got):
        got = [
            jnp.concatenate([chunk_of(y, k ^ d) for k in range(at.chips)], axis=0)
            for d, y in enumerate(got, 1)
        ]
        return pick(chip ^ root, [x] + got)

    row_now, row_scale = row_state[:, :half], row_state[:, half:half + 1]
    row_tile = (row_scale * row_now).astype(jnp.bfloat16)
    tiles_across = across(row_tile)
    row_tile, row_state = lax.optimization_barrier((row_tile, row_state))
    row_now, row_scale = row_state[:, :half], row_state[:, half:half + 1]
    high = lax.optimization_barrier(row_scale.astype(jnp.bfloat16))
    low = lax.optimization_barrier(
        (row_scale - high.astype(jnp.float32)).astype(jnp.bfloat16)
    )

    def joined(high, low):
        return high.astype(jnp.float32) + low.astype(jnp.float32)

    row_rest = (
        row_now - row_tile.astype(jnp.float32) / joined(high, low)
    ).astype(jnp.bfloat16)
    row_rest = jnp.concatenate(
        [row_rest] + [jnp.broadcast_to(x, (n_kept, PAD, block_len)) for x in (high, low)],
        axis=1,
    )

    before = None
    for iterate in range(STEPS):
        first, last = iterate == 0, iterate == STEPS - 1
        if not first:
            row_tile = pick(
                chip ^ root,
                [own] + [send(own, at.moves_chip(d)) for d in range(1, at.chips)],
            )
        dtypes = (jnp.float32,) * at.group + (jnp.bfloat16,) * at.group
        if not first:
            near = [own] + [send(own, at.moves_slow(g)) for g in range(1, at.group)]
            far = [send(own, at.moves_slow(g, 1)) for g in range(at.group)]
        sums = products(meta, both, row_tile, dtypes, n_kept, True)
        near_sums, far_sums = list(sums[:at.group]), list(sums[at.group:])
        from_fast = [send(x, at.moves_fast()) for x in far_sums[::-1]][::-1]
        if first:
            tiles_across, far_sums = lax.optimization_barrier((tiles_across, far_sums))
            own = kept_of(row_tile, tiles_across)
            near = [own] + [send(own, at.moves_slow(g)) for g in range(1, at.group)]
            far = [send(own, at.moves_slow(g, 1)) for g in range(at.group)]
            row_rest, near, from_fast[-1] = lax.optimization_barrier(
                (row_rest, near, from_fast[-1])
            )
            rests_across = across(row_rest)
        (row_sum,) = products(
            meta, both, jnp.concatenate(near + far, axis=0), (jnp.bfloat16,), n_row, False,
            after=far_sums,
        )
        if first:
            from_fast[-1], row_sum, rests_across = lax.optimization_barrier(
                (from_fast[-1], row_sum, rests_across)
            )
            scales = [
                joined(x[:, half:half + 1], x[:, half + PAD:half + PAD + 1])
                for x in rests_across
            ]
            scale = kept_of(row_scale, scales)
            now = kept_of(row_now, [
                tile.astype(jnp.float32) / factor + rest[:, :half].astype(jnp.float32)
                for tile, factor, rest in zip(tiles_across, scales, rests_across)
            ])
        from_row = [row_sum] + [
            send(row_sum, at.moves_chip(d)) for d in range(1, at.chips)
        ]
        sums = [x + y.astype(jnp.float32) for x, y in zip(near_sums, from_fast)]
        total = sums[0]
        for g in range(1, at.group):
            total = total + send(
                sums[g].astype(jnp.bfloat16), at.moves_slow(g)
            ).astype(jnp.float32)
        for x in from_row:
            total = total + jnp.where(is_root, x, jnp.zeros_like(x)).astype(jnp.float32)
        message = total.astype(jnp.bfloat16)
        if last:
            total, now, scale = chunk_of(total, 0), chunk_of(now, 0), chunk_of(scale, 0)
            before = chunk_of(before, 0)
        applied = total
        for e in range(1, at.chips):
            if last:
                got = send(chunk_of(message, e), at.moves_slow(e * at.group))
            else:
                got = send(message, at.moves_slow(e * at.group))
                got = jnp.concatenate([chunk_of(got, k ^ e) for k in range(at.chips)], axis=0)
            applied = applied + got.astype(jnp.float32)
        mapped = scale * applied - center_shift * now
        if first:
            updated = mapped / half_width
        else:
            updated = 2.0 / half_width * mapped - before
        before = now
        now = updated
        if not last:
            own = (scale * now).astype(jnp.bfloat16)
    back = [
        send(now[swap * part:(swap + 1) * part], turned(at.moves_home(swap)))
        for swap in range(2)
    ]
    result = jnp.stack([jnp.where(core == k, back[0], back[1]) for k in range(2)])
    return result.transpose(0, 2, 1, 3).reshape(start_vectors.shape)


def solution(mesh):
    in_specs = (
        P(None, ("row", "col")),
        P(("row", "col")),
        P("row", "col", None, None, None),
        P("row", "col", None, None),
        P("row", "col"),
    )
    out_specs = P(None, ("row", "col"))
    return jax.shard_map(
        per_device, mesh=mesh, in_specs=in_specs, out_specs=out_specs, check_vma=False
    )
```

```python
import functools

import jax
import jax.numpy as jnp
from jax import lax
from jax.experimental import pallas as pl
from jax.experimental.pallas import tpu as pltpu
from jax.sharding import PartitionSpec as P

STEPS = 3

center_shift = 0.5
half_width = 3.0

UNROLL = 64
PACK = 4
VMEM_LIMIT = 16 * 1024 * 1024
AXES = ("row", "col")
PAD = 8


class Layout:
    def __init__(self, rows, cols):
        self.rows, self.cols = rows, cols
        self.chips = cols // 2
        self.fast = 2
        self.slow = rows // 2
        self.group = self.slow // self.chips
        assert self.group * self.chips * self.fast == rows

    def device(self, slow, fast, chip, core):
        return (slow * self.fast + fast) * self.cols + chip * 2 + core

    def home(self, chunk):
        chip, k = chunk // self.rows, chunk % self.rows
        e, f, t = k % self.chips, (k // self.chips) % self.fast, k // (self.chips * self.fast)
        return (chip ^ e) * self.group + t, f, chip

    def moves_home(self, swap):
        pairs = []
        for chunk in range(self.rows * self.chips):
            row, chip = chunk // self.chips, chunk % self.chips
            for core in range(2):
                source = row * self.cols + chip * 2 + core
                pairs.append((source, self.device(*self.home(chunk), core ^ swap)))
        return pairs

    def moves_slow(self, d, side=0):
        return [
            (self.device(s, f, c, q), self.device(s ^ d, f ^ side, c, q))
            for s in range(self.slow) for f in range(self.fast)
            for c in range(self.chips) for q in range(2)
        ]

    def moves_fast(self):
        return self.moves_slow(0, 1)

    def moves_chip(self, d, swap=0):
        return [
            (self.device(s, f, c, q), self.device(s, f, c ^ d, q ^ swap))
            for s in range(self.slow) for f in range(self.fast)
            for c in range(self.chips) for q in range(2)
        ]

    def moves_core(self):
        return [(i, i ^ 1) for i in range(self.rows * self.cols)]


def turned(pairs):
    return [(b, a) for a, b in pairs]


def live_groups(meta_ref, cap, which):
    return jnp.maximum((meta_ref[8 * cap + which] + (UNROLL - 1)) // UNROLL, 1)


def product_kernel(transpose, cap, n_out, after, meta_in, vecs_in, *refs):
    slab_refs, refs = refs[:2], refs[2 + after:]
    outs, refs = refs[:n_out], refs[n_out:]
    meta_ref, vecs_ref, slabs, acc, slab_sem, in_sem = refs
    base = 0 if transpose else 4 * cap

    def slab_copy(which, g):
        span = pl.ds(g * UNROLL, UNROLL)
        to = pl.ds(which * cap + g * UNROLL, UNROLL)
        sem = slab_sem.at[which * (cap // UNROLL) + g]
        return pltpu.make_async_copy(slab_refs[which].at[span], slabs.at[to], sem)

    def start_slab(which, g, carry):
        slab_copy(which, g).start()
        return carry

    meta_copy = pltpu.make_async_copy(meta_in, meta_ref, in_sem.at[0])
    vecs_copy = pltpu.make_async_copy(vecs_in, vecs_ref, in_sem.at[1])
    meta_copy.start()
    slab_copy(0, 0).start()
    vecs_copy.start()
    slab_copy(1, 0).start()
    acc[...] = jnp.zeros_like(acc)
    meta_copy.wait()
    groups = [live_groups(meta_ref, cap, which) for which in range(2)]
    for which in range(2):
        lax.fori_loop(1, groups[which], functools.partial(start_slab, which), 0)
    vecs_copy.wait()
    vec_count, block_len = vecs_ref.shape[1:]
    zero = jnp.zeros((vec_count, block_len), jnp.bfloat16)

    def body(which, g, carry):
        slab_copy(which, g).wait()
        start = which * cap + g * UNROLL
        products = []
        for u in range(0, UNROLL, PACK):
            v = [vecs_ref[meta_ref[base + start + u + k]] for k in range(PACK)]
            m = [slabs[start + u + k] for k in range(PACK)]
            left = jnp.concatenate([
                jnp.concatenate([v[0], zero, v[2], zero], axis=0),
                jnp.concatenate([zero, v[1], zero, v[3]], axis=0),
            ], axis=1)
            if transpose:
                halves = [jnp.concatenate(m[:2], axis=0), jnp.concatenate(m[2:], axis=0)]
                right, dims = jnp.concatenate(halves, axis=1), (((1,), (0,)), ((), ()))
            else:
                halves = [jnp.concatenate(m[:2], axis=1), jnp.concatenate(m[2:], axis=1)]
                right, dims = jnp.concatenate(halves, axis=0), (((1,), (1,)), ((), ()))
            products.append(
                lax.dot_general(left, right, dims, preferred_element_type=jnp.float32)
            )
        for u in range(UNROLL):
            k = u % PACK
            rows = slice(k * vec_count, (k + 1) * vec_count)
            lanes = slice((k // 2) * block_len, (k // 2 + 1) * block_len)
            acc[meta_ref[base + 2 * cap + start + u]] += products[u // PACK][rows, lanes]
        return carry

    for which in range(2):
        lax.fori_loop(0, groups[which], functools.partial(body, which), 0)
    size = outs[0].shape[0]
    for k, out in enumerate(outs):
        out[...] = acc[k * size:(k + 1) * size].astype(out.dtype)


def products(meta, slabs, vecs, out_dtypes, out_blocks, transpose, after=()):
    cap, block_len, _ = slabs[0].shape
    vec_count = vecs.shape[1]
    n_out = len(out_dtypes)
    total_out = out_blocks * n_out
    anywhere = pl.BlockSpec(memory_space=pl.ANY)
    vmem = pl.BlockSpec(memory_space=pltpu.VMEM)
    out_shape = [
        jax.ShapeDtypeStruct((out_blocks, vec_count, block_len), dtype) for dtype in out_dtypes
    ]
    return pl.pallas_call(
        functools.partial(product_kernel, transpose, cap, n_out, len(after)),
        in_specs=[anywhere] * (4 + len(after)),
        out_specs=[vmem] * n_out,
        out_shape=out_shape,
        scratch_shapes=[
            pltpu.SMEM(meta.shape, jnp.int32),
            pltpu.VMEM(vecs.shape, jnp.bfloat16),
            pltpu.VMEM((2 * cap, block_len, block_len), jnp.bfloat16),
            pltpu.VMEM((total_out + 1, vec_count, block_len), jnp.float32),
            pltpu.SemaphoreType.DMA((2 * cap // UNROLL,)),
            pltpu.SemaphoreType.DMA((2,)),
        ],
        compiler_params=pltpu.CompilerParams(vmem_limit_bytes=VMEM_LIMIT),
        cost_estimate=pl.CostEstimate(
            flops=4 * cap * vec_count * block_len * block_len,
            bytes_accessed=2 * vec_count * block_len * (vecs.shape[0] + total_out),
            transcendentals=0,
        ),
        name="transposed" if transpose else "direct",
    )(meta, vecs, *slabs, *after)


def per_device(start_vectors, scaling, block_values, block_places, block_counts):
    at = Layout(lax.axis_size("row"), lax.axis_size("col"))
    cap = block_values.shape[2]
    block_len = block_values.shape[-1]
    half = start_vectors.shape[0] // 2
    part = start_vectors.shape[1] // block_len
    per_chunk = 2 * part
    row_index = lax.axis_index("row").astype(jnp.int32)
    col_index = lax.axis_index("col").astype(jnp.int32)
    slow, fast = row_index // at.fast, row_index % at.fast
    chip, core = col_index // 2, col_index % 2
    root = slow // at.group
    is_root = chip == root
    def send(x, pairs):
        return lax.ppermute(x, AXES, pairs)

    slabs = block_values.reshape(cap, block_len, block_len)
    slots = jnp.concatenate([block_places.reshape(2 * cap), block_counts.reshape(1)])
    other_slabs = send(slabs, at.moves_core())

    halves = start_vectors.reshape(2, half, part, block_len).transpose(0, 2, 1, 3)
    scale_rows = jnp.broadcast_to(
        scaling.reshape(1, part, 1, block_len), (2, part, PAD, block_len)
    )
    halves = jnp.concatenate([halves, scale_rows], axis=2)
    packed = [
        jnp.where(core == swap, halves[0], halves[1]) for swap in range(2)
    ]
    pieces = [
        jnp.concatenate([
            packed[swap] if (d, swap) == (0, 0) else send(packed[swap], at.moves_chip(d, swap))
            for swap in range(2)
        ], axis=0)
        for d in range(at.chips)
    ]
    n_kept = at.chips * per_chunk

    def chunk_of(x, e):
        return x[e * per_chunk:(e + 1) * per_chunk]

    def pick(index, choices):
        x = choices[0]
        for d in range(1, len(choices)):
            x = jnp.where(index == d, choices[d], x)
        return x

    row_state = jnp.concatenate([pick(chip ^ e, pieces) for e in range(at.chips)], axis=0)

    other_slots = send(slots, at.moves_core())
    n_col = at.rows * per_chunk
    n_row = at.chips * per_chunk
    lists = []
    for which, held in enumerate((slots, other_slots)):
        row_block, col_block = held[:cap], held[cap:2 * cap]
        live = jnp.arange(cap, dtype=jnp.int32) < held[2 * cap]

        def inside(block):
            return ((block // part) ^ core) * part + block % part

        e = row_block // per_chunk
        row_at = e * per_chunk + inside(row_block % per_chunk)
        block = (core ^ which) * (n_col // 2) + col_block
        k = block // per_chunk
        e, f, t = k % at.chips, (k // at.chips) % at.fast, k // (at.chips * at.fast)
        d = slow ^ ((chip ^ e) * at.group + t)
        place = (d % at.group) * at.chips + d // at.group
        col_at = ((fast ^ f) * at.slow + place) * per_chunk + inside(block % per_chunk)
        lists.append((
            row_at, jnp.where(live, col_at, n_col), col_at, jnp.where(live, row_at, n_row)
        ))
    meta = jnp.concatenate(
        [jnp.concatenate([mine, theirs]) for mine, theirs in zip(*lists)]
        + [slots[2 * cap:], other_slots[2 * cap:], jnp.zeros(126, jnp.int32)]
    )

    row_state, meta, other_slabs = lax.optimization_barrier((row_state, meta, other_slabs))
    both = (slabs, other_slabs)

    def across(x):
        return [send(x, at.moves_slow(d * at.group)) for d in range(1, at.chips)]

    def kept_of(x, got):
        got = [
            jnp.concatenate([chunk_of(y, k ^ d) for k in range(at.chips)], axis=0)
            for d, y in enumerate(got, 1)
        ]
        return pick(chip ^ root, [x] + got)

    row_now, row_scale = row_state[:, :half], row_state[:, half:half + 1]
    row_tile = (row_scale * row_now).astype(jnp.bfloat16)
    tiles_across = across(row_tile)
    row_tile, row_state = lax.optimization_barrier((row_tile, row_state))
    row_now, row_scale = row_state[:, :half], row_state[:, half:half + 1]
    high = lax.optimization_barrier(row_scale.astype(jnp.bfloat16))
    low = lax.optimization_barrier(
        (row_scale - high.astype(jnp.float32)).astype(jnp.bfloat16)
    )

    def joined(high, low):
        return high.astype(jnp.float32) + low.astype(jnp.float32)

    row_rest = (
        row_now - row_tile.astype(jnp.float32) / joined(high, low)
    ).astype(jnp.bfloat16)
    row_rest = jnp.concatenate(
        [row_rest] + [jnp.broadcast_to(x, (n_kept, PAD, block_len)) for x in (high, low)],
        axis=1,
    )
    row_tile, row_rest = lax.optimization_barrier((row_tile, row_rest))

    before = None
    for iterate in range(STEPS):
        first, last = iterate == 0, iterate == STEPS - 1
        if not first:
            row_tile = pick(
                chip ^ root,
                [own] + [send(own, at.moves_chip(d)) for d in range(1, at.chips)],
            )
        dtypes = (jnp.float32,) * at.group + (jnp.bfloat16,) * at.group
        if not first:
            near = [own] + [send(own, at.moves_slow(g)) for g in range(1, at.group)]
            far = [send(own, at.moves_slow(g, 1)) for g in range(at.group)]
        sums = products(meta, both, row_tile, dtypes, n_kept, True)
        near_sums, far_sums = list(sums[:at.group]), list(sums[at.group:])
        from_fast = [send(x, at.moves_fast()) for x in far_sums[::-1]][::-1]
        if first:
            tiles_across, far_sums = lax.optimization_barrier((tiles_across, far_sums))
            own = kept_of(row_tile, tiles_across)
            near = [own] + [send(own, at.moves_slow(g)) for g in range(1, at.group)]
            far = [send(own, at.moves_slow(g, 1)) for g in range(at.group)]
            row_rest, near = lax.optimization_barrier((row_rest, near))
            rests_across = across(row_rest)
        (row_sum,) = products(
            meta, both, jnp.concatenate(near + far, axis=0), (jnp.bfloat16,), n_row, False,
            after=far_sums,
        )
        if first:
            from_fast[-1], row_sum, rests_across = lax.optimization_barrier(
                (from_fast[-1], row_sum, rests_across)
            )
            scales = [
                joined(x[:, half:half + 1], x[:, half + PAD:half + PAD + 1])
                for x in rests_across
            ]
            scale = kept_of(row_scale, scales)
            now = kept_of(row_now, [
                tile.astype(jnp.float32) / factor + rest[:, :half].astype(jnp.float32)
                for tile, factor, rest in zip(tiles_across, scales, rests_across)
            ])
        from_row = [row_sum] + [
            send(row_sum, at.moves_chip(d)) for d in range(1, at.chips)
        ]
        sums = [x + y.astype(jnp.float32) for x, y in zip(near_sums, from_fast)]
        total = sums[0]
        for g in range(1, at.group):
            total = total + send(
                sums[g].astype(jnp.bfloat16), at.moves_slow(g)
            ).astype(jnp.float32)
        for x in from_row:
            total = total + jnp.where(is_root, x, jnp.zeros_like(x)).astype(jnp.float32)
        message = total.astype(jnp.bfloat16)
        if last:
            total, now, scale = chunk_of(total, 0), chunk_of(now, 0), chunk_of(scale, 0)
            before = chunk_of(before, 0)
        applied = total
        for e in range(1, at.chips):
            if last:
                got = send(chunk_of(message, e), at.moves_slow(e * at.group))
            else:
                got = send(message, at.moves_slow(e * at.group))
                got = jnp.concatenate([chunk_of(got, k ^ e) for k in range(at.chips)], axis=0)
            applied = applied + got.astype(jnp.float32)
        mapped = scale * applied - center_shift * now
        if first:
            updated = mapped / half_width
        else:
            updated = 2.0 / half_width * mapped - before
        before = now
        now = updated
        if not last:
            own = (scale * now).astype(jnp.bfloat16)
    back = [
        send(now[swap * part:(swap + 1) * part], turned(at.moves_home(swap)))
        for swap in range(2)
    ]
    result = jnp.stack([jnp.where(core == k, back[0], back[1]) for k in range(2)])
    return result.transpose(0, 2, 1, 3).reshape(start_vectors.shape)


def solution(mesh):
    in_specs = (
        P(None, ("row", "col")),
        P(("row", "col")),
        P("row", "col", None, None, None),
        P("row", "col", None, None),
        P("row", "col"),
    )
    out_specs = P(None, ("row", "col"))
    return jax.shard_map(
        per_device, mesh=mesh, in_specs=in_specs, out_specs=out_specs, check_vma=False
    )
```

```python
import functools

import jax
import jax.numpy as jnp
from jax import lax
from jax.experimental import pallas as pl
from jax.experimental.pallas import tpu as pltpu
from jax.sharding import PartitionSpec as P

STEPS = 3

center_shift = 0.5
half_width = 3.0

UNROLL = 64
PACK = 4
VMEM_LIMIT = 16 * 1024 * 1024
AXES = ("row", "col")
PAD = 8


class Layout:
    def __init__(self, rows, cols):
        self.rows, self.cols = rows, cols
        self.chips = cols // 2
        self.fast = 2
        self.slow = rows // 2
        self.group = self.slow // self.chips
        assert self.group * self.chips * self.fast == rows

    def device(self, slow, fast, chip, core):
        return (slow * self.fast + fast) * self.cols + chip * 2 + core

    def home(self, chunk):
        chip, k = chunk // self.rows, chunk % self.rows
        e, f, t = k % self.chips, (k // self.chips) % self.fast, k // (self.chips * self.fast)
        return (chip ^ e) * self.group + t, f, chip

    def moves_home(self, swap):
        pairs = []
        for chunk in range(self.rows * self.chips):
            row, chip = chunk // self.chips, chunk % self.chips
            for core in range(2):
                source = row * self.cols + chip * 2 + core
                pairs.append((source, self.device(*self.home(chunk), core ^ swap)))
        return pairs

    def moves_slow(self, d, side=0):
        return [
            (self.device(s, f, c, q), self.device(s ^ d, f ^ side, c, q))
            for s in range(self.slow) for f in range(self.fast)
            for c in range(self.chips) for q in range(2)
        ]

    def moves_fast(self):
        return self.moves_slow(0, 1)

    def moves_chip(self, d, swap=0):
        return [
            (self.device(s, f, c, q), self.device(s, f, c ^ d, q ^ swap))
            for s in range(self.slow) for f in range(self.fast)
            for c in range(self.chips) for q in range(2)
        ]

    def moves_core(self):
        return [(i, i ^ 1) for i in range(self.rows * self.cols)]


def turned(pairs):
    return [(b, a) for a, b in pairs]


def live_groups(meta_ref, cap, which):
    return jnp.maximum((meta_ref[8 * cap + which] + (UNROLL - 1)) // UNROLL, 1)


def product_kernel(transpose, cap, n_out, carry, after, meta_in, vecs_in, *refs):
    slab_refs, refs = refs[:2], refs[2 + after:]
    outs, refs = refs[:n_out], refs[n_out + carry:]
    meta_ref, vecs_ref, slabs, acc, slab_sem, in_sem = refs
    base = 0 if transpose else 4 * cap

    def slab_copy(which, g):
        span = pl.ds(g * UNROLL, UNROLL)
        to = pl.ds(which * cap + g * UNROLL, UNROLL)
        sem = slab_sem.at[which * (cap // UNROLL) + g]
        return pltpu.make_async_copy(slab_refs[which].at[span], slabs.at[to], sem)

    def start_slab(which, g, carry):
        slab_copy(which, g).start()
        return carry

    meta_copy = pltpu.make_async_copy(meta_in, meta_ref, in_sem.at[0])
    vecs_copy = pltpu.make_async_copy(vecs_in, vecs_ref, in_sem.at[1])
    meta_copy.start()
    slab_copy(0, 0).start()
    vecs_copy.start()
    slab_copy(1, 0).start()
    acc[...] = jnp.zeros_like(acc)
    meta_copy.wait()
    groups = [live_groups(meta_ref, cap, which) for which in range(2)]
    for which in range(2):
        lax.fori_loop(1, groups[which], functools.partial(start_slab, which), 0)
    vecs_copy.wait()
    vec_count, block_len = vecs_ref.shape[1:]
    zero = jnp.zeros((vec_count, block_len), jnp.bfloat16)

    def body(which, g, carry):
        slab_copy(which, g).wait()
        start = which * cap + g * UNROLL
        products = []
        for u in range(0, UNROLL, PACK):
            v = [vecs_ref[meta_ref[base + start + u + k]] for k in range(PACK)]
            m = [slabs[start + u + k] for k in range(PACK)]
            left = jnp.concatenate([
                jnp.concatenate([v[0], zero, v[2], zero], axis=0),
                jnp.concatenate([zero, v[1], zero, v[3]], axis=0),
            ], axis=1)
            if transpose:
                halves = [jnp.concatenate(m[:2], axis=0), jnp.concatenate(m[2:], axis=0)]
                right, dims = jnp.concatenate(halves, axis=1), (((1,), (0,)), ((), ()))
            else:
                halves = [jnp.concatenate(m[:2], axis=1), jnp.concatenate(m[2:], axis=1)]
                right, dims = jnp.concatenate(halves, axis=0), (((1,), (1,)), ((), ()))
            products.append(
                lax.dot_general(left, right, dims, preferred_element_type=jnp.float32)
            )
        for u in range(UNROLL):
            k = u % PACK
            rows = slice(k * vec_count, (k + 1) * vec_count)
            lanes = slice((k // 2) * block_len, (k // 2 + 1) * block_len)
            acc[meta_ref[base + 2 * cap + start + u]] += products[u // PACK][rows, lanes]
        return carry

    for which in range(2):
        lax.fori_loop(0, groups[which], functools.partial(body, which), 0)
    size = outs[0].shape[0]
    for k, out in enumerate(outs):
        out[...] = acc[k * size:(k + 1) * size].astype(out.dtype)


def products(meta, slabs, vecs, out_dtypes, out_blocks, transpose, carry=False, after=()):
    cap, block_len, _ = slabs[0].shape
    vec_count = vecs.shape[1]
    n_out = len(out_dtypes)
    total_out = out_blocks * n_out
    anywhere = pl.BlockSpec(memory_space=pl.ANY)
    vmem = pl.BlockSpec(memory_space=pltpu.VMEM)
    out_shape = [
        jax.ShapeDtypeStruct((out_blocks, vec_count, block_len), dtype) for dtype in out_dtypes
    ]
    if carry:
        out_shape.append(jax.ShapeDtypeStruct(slabs[0].shape, slabs[0].dtype))
    return pl.pallas_call(
        functools.partial(product_kernel, transpose, cap, n_out, carry, len(after)),
        in_specs=[anywhere] * (4 + len(after)),
        out_specs=[vmem] * n_out + [anywhere] * carry,
        out_shape=out_shape,
        input_output_aliases={2: n_out} if carry else {},
        scratch_shapes=[
            pltpu.SMEM(meta.shape, jnp.int32),
            pltpu.VMEM(vecs.shape, jnp.bfloat16),
            pltpu.VMEM((2 * cap, block_len, block_len), jnp.bfloat16),
            pltpu.VMEM((total_out + 1, vec_count, block_len), jnp.float32),
            pltpu.SemaphoreType.DMA((2 * cap // UNROLL,)),
            pltpu.SemaphoreType.DMA((2,)),
        ],
        compiler_params=pltpu.CompilerParams(vmem_limit_bytes=VMEM_LIMIT),
        cost_estimate=pl.CostEstimate(
            flops=4 * cap * vec_count * block_len * block_len,
            bytes_accessed=2 * vec_count * block_len * (vecs.shape[0] + total_out),
            transcendentals=0,
        ),
        name="transposed" if transpose else "direct",
    )(meta, vecs, *slabs, *after)


def per_device(start_vectors, scaling, block_values, block_places, block_counts):
    at = Layout(lax.axis_size("row"), lax.axis_size("col"))
    cap = block_values.shape[2]
    block_len = block_values.shape[-1]
    half = start_vectors.shape[0] // 2
    part = start_vectors.shape[1] // block_len
    per_chunk = 2 * part
    row_index = lax.axis_index("row").astype(jnp.int32)
    col_index = lax.axis_index("col").astype(jnp.int32)
    slow, fast = row_index // at.fast, row_index % at.fast
    chip, core = col_index // 2, col_index % 2
    root = slow // at.group
    is_root = chip == root
    def send(x, pairs):
        return lax.ppermute(x, AXES, pairs)

    slabs = block_values.reshape(cap, block_len, block_len)
    slots = jnp.concatenate([block_places.reshape(2 * cap), block_counts.reshape(1)])
    other_slabs = send(slabs, at.moves_core())

    halves = start_vectors.reshape(2, half, part, block_len).transpose(0, 2, 1, 3)
    scale_rows = jnp.broadcast_to(
        scaling.reshape(1, part, 1, block_len), (2, part, PAD, block_len)
    )
    halves = jnp.concatenate([halves, scale_rows], axis=2)
    packed = [
        jnp.where(core == swap, halves[0], halves[1]) for swap in range(2)
    ]
    pieces = [
        jnp.concatenate([
            packed[swap] if (d, swap) == (0, 0) else send(packed[swap], at.moves_chip(d, swap))
            for swap in range(2)
        ], axis=0)
        for d in range(at.chips)
    ]
    n_kept = at.chips * per_chunk

    def chunk_of(x, e):
        return x[e * per_chunk:(e + 1) * per_chunk]

    def pick(index, choices):
        x = choices[0]
        for d in range(1, len(choices)):
            x = jnp.where(index == d, choices[d], x)
        return x

    row_state = jnp.concatenate([pick(chip ^ e, pieces) for e in range(at.chips)], axis=0)

    other_slots = send(slots, at.moves_core())
    n_col = at.rows * per_chunk
    n_row = at.chips * per_chunk
    lists = []
    for which, held in enumerate((slots, other_slots)):
        row_block, col_block = held[:cap], held[cap:2 * cap]
        live = jnp.arange(cap, dtype=jnp.int32) < held[2 * cap]

        def inside(block):
            return ((block // part) ^ core) * part + block % part

        e = row_block // per_chunk
        row_at = e * per_chunk + inside(row_block % per_chunk)
        block = (core ^ which) * (n_col // 2) + col_block
        k = block // per_chunk
        e, f, t = k % at.chips, (k // at.chips) % at.fast, k // (at.chips * at.fast)
        d = slow ^ ((chip ^ e) * at.group + t)
        place = (d % at.group) * at.chips + d // at.group
        col_at = ((fast ^ f) * at.slow + place) * per_chunk + inside(block % per_chunk)
        lists.append((
            row_at, jnp.where(live, col_at, n_col), col_at, jnp.where(live, row_at, n_row)
        ))
    meta = jnp.concatenate(
        [jnp.concatenate([mine, theirs]) for mine, theirs in zip(*lists)]
        + [slots[2 * cap:], other_slots[2 * cap:], jnp.zeros(126, jnp.int32)]
    )

    row_state, meta, other_slabs = lax.optimization_barrier((row_state, meta, other_slabs))
    both = (slabs, other_slabs)

    def across(x):
        return [send(x, at.moves_slow(d * at.group)) for d in range(1, at.chips)]

    def kept_of(x, got):
        got = [
            jnp.concatenate([chunk_of(y, k ^ d) for k in range(at.chips)], axis=0)
            for d, y in enumerate(got, 1)
        ]
        return pick(chip ^ root, [x] + got)

    row_now, row_scale = row_state[:, :half], row_state[:, half:half + 1]
    row_tile = (row_scale * row_now).astype(jnp.bfloat16)
    tiles_across = across(row_tile)
    row_tile, row_state = lax.optimization_barrier((row_tile, row_state))
    row_now, row_scale = row_state[:, :half], row_state[:, half:half + 1]
    high = lax.optimization_barrier(row_scale.astype(jnp.bfloat16))
    low = lax.optimization_barrier(
        (row_scale - high.astype(jnp.float32)).astype(jnp.bfloat16)
    )

    def joined(high, low):
        return high.astype(jnp.float32) + low.astype(jnp.float32)

    row_rest = (
        row_now - row_tile.astype(jnp.float32) / joined(high, low)
    ).astype(jnp.bfloat16)
    row_rest = jnp.concatenate(
        [row_rest] + [jnp.broadcast_to(x, (n_kept, PAD, block_len)) for x in (high, low)],
        axis=1,
    )

    before = None
    for iterate in range(STEPS):
        first, last = iterate == 0, iterate == STEPS - 1
        if not first:
            row_tile = pick(
                chip ^ root,
                [own] + [send(own, at.moves_chip(d)) for d in range(1, at.chips)],
            )
        dtypes = (jnp.float32,) * at.group + (jnp.bfloat16,) * at.group
        if not first:
            near = [own] + [send(own, at.moves_slow(g)) for g in range(1, at.group)]
            far = [send(own, at.moves_slow(g, 1)) for g in range(at.group)]
        if first:
            row_tile, *both = lax.optimization_barrier((row_tile, *both))
        sums = list(products(meta, both, row_tile, dtypes, n_kept, True, carry=first))
        if first:
            both = (sums.pop(), other_slabs)
        near_sums, far_sums = list(sums[:at.group]), list(sums[at.group:])
        from_fast = [send(x, at.moves_fast()) for x in far_sums[::-1]][::-1]
        if first:
            tiles_across, far_sums = lax.optimization_barrier((tiles_across, far_sums))
            own = kept_of(row_tile, tiles_across)
            near = [own] + [send(own, at.moves_slow(g)) for g in range(1, at.group)]
            far = [send(own, at.moves_slow(g, 1)) for g in range(at.group)]
            row_rest, near = lax.optimization_barrier((row_rest, near))
            rests_across = across(row_rest)
        (row_sum,) = products(
            meta, both, jnp.concatenate(near + far, axis=0), (jnp.bfloat16,), n_row, False,
            after=far_sums,
        )
        if first:
            from_fast[-1], row_sum, rests_across = lax.optimization_barrier(
                (from_fast[-1], row_sum, rests_across)
            )
            scales = [
                joined(x[:, half:half + 1], x[:, half + PAD:half + PAD + 1])
                for x in rests_across
            ]
            scale = kept_of(row_scale, scales)
            now = kept_of(row_now, [
                tile.astype(jnp.float32) / factor + rest[:, :half].astype(jnp.float32)
                for tile, factor, rest in zip(tiles_across, scales, rests_across)
            ])
        from_row = [row_sum] + [
            send(row_sum, at.moves_chip(d)) for d in range(1, at.chips)
        ]
        sums = [x + y.astype(jnp.float32) for x, y in zip(near_sums, from_fast)]
        total = sums[0]
        for g in range(1, at.group):
            total = total + send(
                sums[g].astype(jnp.bfloat16), at.moves_slow(g)
            ).astype(jnp.float32)
        for x in from_row:
            total = total + jnp.where(is_root, x, jnp.zeros_like(x)).astype(jnp.float32)
        message = total.astype(jnp.bfloat16)
        if last:
            total, now, scale = chunk_of(total, 0), chunk_of(now, 0), chunk_of(scale, 0)
            before = chunk_of(before, 0)
        applied = total
        for e in range(1, at.chips):
            if last:
                got = send(chunk_of(message, e), at.moves_slow(e * at.group))
            else:
                got = send(message, at.moves_slow(e * at.group))
                got = jnp.concatenate([chunk_of(got, k ^ e) for k in range(at.chips)], axis=0)
            applied = applied + got.astype(jnp.float32)
        mapped = scale * applied - center_shift * now
        if first:
            updated = mapped / half_width
        else:
            updated = 2.0 / half_width * mapped - before
        before = now
        now = updated
        if not last:
            own = (scale * now).astype(jnp.bfloat16)
    back = [
        send(now[swap * part:(swap + 1) * part], turned(at.moves_home(swap)))
        for swap in range(2)
    ]
    result = jnp.stack([jnp.where(core == k, back[0], back[1]) for k in range(2)])
    return result.transpose(0, 2, 1, 3).reshape(start_vectors.shape)


def solution(mesh):
    in_specs = (
        P(None, ("row", "col")),
        P(("row", "col")),
        P("row", "col", None, None, None),
        P("row", "col", None, None),
        P("row", "col"),
    )
    out_specs = P(None, ("row", "col"))
    return jax.shard_map(
        per_device, mesh=mesh, in_specs=in_specs, out_specs=out_specs, check_vma=False
    )
```

```python
import functools

import jax
import jax.numpy as jnp
from jax import lax
from jax.experimental import pallas as pl
from jax.experimental.pallas import tpu as pltpu
from jax.sharding import PartitionSpec as P

STEPS = 3

center_shift = 0.5
half_width = 3.0

UNROLL = 64
PACK = 4
VMEM_LIMIT = 24 * 1024 * 1024
AXES = ("row", "col")
PAD = 8


class Layout:
    def __init__(self, rows, cols):
        self.rows, self.cols = rows, cols
        self.chips = cols // 2
        self.fast = 2
        self.slow = rows // 2
        self.group = self.slow // self.chips
        assert self.group * self.chips * self.fast == rows

    def device(self, slow, fast, chip, core):
        return (slow * self.fast + fast) * self.cols + chip * 2 + core

    def home(self, chunk):
        chip, k = chunk // self.rows, chunk % self.rows
        e, f, t = k % self.chips, (k // self.chips) % self.fast, k // (self.chips * self.fast)
        return (chip ^ e) * self.group + t, f, chip

    def moves_home(self, swap):
        pairs = []
        for chunk in range(self.rows * self.chips):
            row, chip = chunk // self.chips, chunk % self.chips
            for core in range(2):
                source = row * self.cols + chip * 2 + core
                pairs.append((source, self.device(*self.home(chunk), core ^ swap)))
        return pairs

    def moves_slow(self, d, side=0):
        return [
            (self.device(s, f, c, q), self.device(s ^ d, f ^ side, c, q))
            for s in range(self.slow) for f in range(self.fast)
            for c in range(self.chips) for q in range(2)
        ]

    def moves_fast(self):
        return self.moves_slow(0, 1)

    def moves_chip(self, d, swap=0):
        return [
            (self.device(s, f, c, q), self.device(s, f, c ^ d, q ^ swap))
            for s in range(self.slow) for f in range(self.fast)
            for c in range(self.chips) for q in range(2)
        ]

    def moves_core(self):
        return [(i, i ^ 1) for i in range(self.rows * self.cols)]


def turned(pairs):
    return [(b, a) for a, b in pairs]


def live_groups(meta_ref, cap, which):
    return jnp.maximum((meta_ref[8 * cap + which] + (UNROLL - 1)) // UNROLL, 1)


def product_kernel(transpose, cap, n_out, after, meta_in, vecs_in, *refs):
    slab_refs, refs = refs[:2], refs[2 + after:]
    outs, refs = refs[:n_out], refs[n_out:]
    meta_ref, vecs_ref, slabs, acc, slab_sem, in_sem = refs
    base = 0 if transpose else 4 * cap

    def slab_copy(which, g):
        span = pl.ds(g * UNROLL, UNROLL)
        to = pl.ds(which * cap + g * UNROLL, UNROLL)
        sem = slab_sem.at[which * (cap // UNROLL) + g]
        return pltpu.make_async_copy(slab_refs[which].at[span], slabs.at[to], sem)

    def start_slab(which, g, carry):
        slab_copy(which, g).start()
        return carry

    meta_copy = pltpu.make_async_copy(meta_in, meta_ref, in_sem.at[0])
    vecs_copy = pltpu.make_async_copy(vecs_in, vecs_ref, in_sem.at[1])
    meta_copy.start()
    slab_copy(0, 0).start()
    vecs_copy.start()
    slab_copy(1, 0).start()
    acc[...] = jnp.zeros_like(acc)
    meta_copy.wait()
    groups = [live_groups(meta_ref, cap, which) for which in range(2)]
    for which in range(2):
        lax.fori_loop(1, groups[which], functools.partial(start_slab, which), 0)
    vecs_copy.wait()
    vec_count, block_len = vecs_ref.shape[1:]
    zero = jnp.zeros((vec_count, block_len), jnp.bfloat16)

    def body(which, g, carry):
        slab_copy(which, g).wait()
        start = which * cap + g * UNROLL
        products = []
        for u in range(0, UNROLL, PACK):
            v = [vecs_ref[meta_ref[base + start + u + k]] for k in range(PACK)]
            m = [slabs[start + u + k] for k in range(PACK)]
            left = jnp.concatenate([
                jnp.concatenate([v[0], zero, v[2], zero], axis=0),
                jnp.concatenate([zero, v[1], zero, v[3]], axis=0),
            ], axis=1)
            if transpose:
                halves = [jnp.concatenate(m[:2], axis=0), jnp.concatenate(m[2:], axis=0)]
                right, dims = jnp.concatenate(halves, axis=1), (((1,), (0,)), ((), ()))
            else:
                halves = [jnp.concatenate(m[:2], axis=1), jnp.concatenate(m[2:], axis=1)]
                right, dims = jnp.concatenate(halves, axis=0), (((1,), (1,)), ((), ()))
            products.append(
                lax.dot_general(left, right, dims, preferred_element_type=jnp.float32)
            )
        for u in range(UNROLL):
            k = u % PACK
            rows = slice(k * vec_count, (k + 1) * vec_count)
            lanes = slice((k // 2) * block_len, (k // 2 + 1) * block_len)
            acc[meta_ref[base + 2 * cap + start + u]] += products[u // PACK][rows, lanes]
        return carry

    for which in range(2):
        lax.fori_loop(0, groups[which], functools.partial(body, which), 0)
    size = outs[0].shape[0]
    for k, out in enumerate(outs):
        out[...] = acc[k * size:(k + 1) * size].astype(out.dtype)


def products(meta, slabs, vecs, out_dtypes, out_blocks, transpose, after=()):
    cap, block_len, _ = slabs[0].shape
    vec_count = vecs.shape[1]
    n_out = len(out_dtypes)
    total_out = out_blocks * n_out
    anywhere = pl.BlockSpec(memory_space=pl.ANY)
    vmem = pl.BlockSpec(memory_space=pltpu.VMEM)
    out_shape = [
        jax.ShapeDtypeStruct((out_blocks, vec_count, block_len), dtype) for dtype in out_dtypes
    ]
    return pl.pallas_call(
        functools.partial(product_kernel, transpose, cap, n_out, len(after)),
        in_specs=[anywhere] * (4 + len(after)),
        out_specs=[vmem] * n_out,
        out_shape=out_shape,
        scratch_shapes=[
            pltpu.SMEM(meta.shape, jnp.int32),
            pltpu.VMEM(vecs.shape, jnp.bfloat16),
            pltpu.VMEM((2 * cap, block_len, block_len), jnp.bfloat16),
            pltpu.VMEM((total_out + 1, vec_count, block_len), jnp.float32),
            pltpu.SemaphoreType.DMA((2 * cap // UNROLL,)),
            pltpu.SemaphoreType.DMA((2,)),
        ],
        compiler_params=pltpu.CompilerParams(vmem_limit_bytes=VMEM_LIMIT),
        cost_estimate=pl.CostEstimate(
            flops=4 * cap * vec_count * block_len * block_len,
            bytes_accessed=2 * vec_count * block_len * (vecs.shape[0] + total_out),
            transcendentals=0,
        ),
        name="transposed" if transpose else "direct",
    )(meta, vecs, *slabs, *after)


def per_device(start_vectors, scaling, block_values, block_places, block_counts):
    at = Layout(lax.axis_size("row"), lax.axis_size("col"))
    cap = block_values.shape[2]
    block_len = block_values.shape[-1]
    half = start_vectors.shape[0] // 2
    part = start_vectors.shape[1] // block_len
    per_chunk = 2 * part
    row_index = lax.axis_index("row").astype(jnp.int32)
    col_index = lax.axis_index("col").astype(jnp.int32)
    slow, fast = row_index // at.fast, row_index % at.fast
    chip, core = col_index // 2, col_index % 2
    root = slow // at.group
    is_root = chip == root
    def send(x, pairs):
        return lax.ppermute(x, AXES, pairs)

    slabs = block_values.reshape(cap, block_len, block_len)
    slots = jnp.concatenate([block_places.reshape(2 * cap), block_counts.reshape(1)])
    other_slabs = send(slabs, at.moves_core())

    halves = start_vectors.reshape(2, half, part, block_len).transpose(0, 2, 1, 3)
    scale_rows = jnp.broadcast_to(
        scaling.reshape(1, part, 1, block_len), (2, part, PAD, block_len)
    )
    halves = jnp.concatenate([halves, scale_rows], axis=2)
    packed = [
        jnp.where(core == swap, halves[0], halves[1]) for swap in range(2)
    ]
    pieces = [
        jnp.concatenate([
            packed[swap] if (d, swap) == (0, 0) else send(packed[swap], at.moves_chip(d, swap))
            for swap in range(2)
        ], axis=0)
        for d in range(at.chips)
    ]
    n_kept = at.chips * per_chunk

    def chunk_of(x, e):
        return x[e * per_chunk:(e + 1) * per_chunk]

    def pick(index, choices):
        x = choices[0]
        for d in range(1, len(choices)):
            x = jnp.where(index == d, choices[d], x)
        return x

    row_state = jnp.concatenate([pick(chip ^ e, pieces) for e in range(at.chips)], axis=0)

    other_slots = send(slots, at.moves_core())
    n_col = at.rows * per_chunk
    n_row = at.chips * per_chunk
    lists = []
    for which, held in enumerate((slots, other_slots)):
        row_block, col_block = held[:cap], held[cap:2 * cap]
        live = jnp.arange(cap, dtype=jnp.int32) < held[2 * cap]

        def inside(block):
            return ((block // part) ^ core) * part + block % part

        e = row_block // per_chunk
        row_at = e * per_chunk + inside(row_block % per_chunk)
        block = (core ^ which) * (n_col // 2) + col_block
        k = block // per_chunk
        e, f, t = k % at.chips, (k // at.chips) % at.fast, k // (at.chips * at.fast)
        d = slow ^ ((chip ^ e) * at.group + t)
        place = (d % at.group) * at.chips + d // at.group
        col_at = ((fast ^ f) * at.slow + place) * per_chunk + inside(block % per_chunk)
        lists.append((
            row_at, jnp.where(live, col_at, n_col), col_at, jnp.where(live, row_at, n_row)
        ))
    meta = jnp.concatenate(
        [jnp.concatenate([mine, theirs]) for mine, theirs in zip(*lists)]
        + [slots[2 * cap:], other_slots[2 * cap:], jnp.zeros(126, jnp.int32)]
    )

    row_state, meta, other_slabs = lax.optimization_barrier((row_state, meta, other_slabs))
    both = (slabs, other_slabs)

    def across(x):
        return [send(x, at.moves_slow(d * at.group)) for d in range(1, at.chips)]

    def kept_of(x, got):
        got = [
            jnp.concatenate([chunk_of(y, k ^ d) for k in range(at.chips)], axis=0)
            for d, y in enumerate(got, 1)
        ]
        return pick(chip ^ root, [x] + got)

    row_now, row_scale = row_state[:, :half], row_state[:, half:half + 1]
    row_tile = (row_scale * row_now).astype(jnp.bfloat16)
    tiles_across = across(row_tile)
    row_tile, row_state = lax.optimization_barrier((row_tile, row_state))
    row_now, row_scale = row_state[:, :half], row_state[:, half:half + 1]
    high = lax.optimization_barrier(row_scale.astype(jnp.bfloat16))
    low = lax.optimization_barrier(
        (row_scale - high.astype(jnp.float32)).astype(jnp.bfloat16)
    )

    def joined(high, low):
        return high.astype(jnp.float32) + low.astype(jnp.float32)

    row_rest = (
        row_now - row_tile.astype(jnp.float32) / joined(high, low)
    ).astype(jnp.bfloat16)
    row_rest = jnp.concatenate(
        [row_rest] + [jnp.broadcast_to(x, (n_kept, PAD, block_len)) for x in (high, low)],
        axis=1,
    )

    before = None
    for iterate in range(STEPS):
        first, last = iterate == 0, iterate == STEPS - 1
        if not first:
            row_tile = pick(
                chip ^ root,
                [own] + [send(own, at.moves_chip(d)) for d in range(1, at.chips)],
            )
        dtypes = (jnp.float32,) * at.group + (jnp.bfloat16,) * at.group
        if not first:
            near = [own] + [send(own, at.moves_slow(g)) for g in range(1, at.group)]
            far = [send(own, at.moves_slow(g, 1)) for g in range(at.group)]
        sums = products(meta, both, row_tile, dtypes, n_kept, True)
        near_sums, far_sums = list(sums[:at.group]), list(sums[at.group:])
        from_fast = [send(x, at.moves_fast()) for x in far_sums[::-1]][::-1]
        if first:
            tiles_across, far_sums = lax.optimization_barrier((tiles_across, far_sums))
            own = kept_of(row_tile, tiles_across)
            near = [own] + [send(own, at.moves_slow(g)) for g in range(1, at.group)]
            far = [send(own, at.moves_slow(g, 1)) for g in range(at.group)]
            row_rest, near = lax.optimization_barrier((row_rest, near))
            rests_across = across(row_rest)
        (row_sum,) = products(
            meta, both, jnp.concatenate(near + far, axis=0), (jnp.bfloat16,), n_row, False,
            after=far_sums,
        )
        if first:
            from_fast[-1], row_sum, rests_across = lax.optimization_barrier(
                (from_fast[-1], row_sum, rests_across)
            )
            scales = [
                joined(x[:, half:half + 1], x[:, half + PAD:half + PAD + 1])
                for x in rests_across
            ]
            scale = kept_of(row_scale, scales)
            now = kept_of(row_now, [
                tile.astype(jnp.float32) / factor + rest[:, :half].astype(jnp.float32)
                for tile, factor, rest in zip(tiles_across, scales, rests_across)
            ])
        from_row = [row_sum] + [
            send(row_sum, at.moves_chip(d)) for d in range(1, at.chips)
        ]
        sums = [x + y.astype(jnp.float32) for x, y in zip(near_sums, from_fast)]
        total = sums[0]
        for g in range(1, at.group):
            total = total + send(
                sums[g].astype(jnp.bfloat16), at.moves_slow(g)
            ).astype(jnp.float32)
        for x in from_row:
            total = total + jnp.where(is_root, x, jnp.zeros_like(x)).astype(jnp.float32)
        message = total.astype(jnp.bfloat16)
        if last:
            total, now, scale = chunk_of(total, 0), chunk_of(now, 0), chunk_of(scale, 0)
            before = chunk_of(before, 0)
        applied = total
        for e in range(1, at.chips):
            if last:
                got = send(chunk_of(message, e), at.moves_slow(e * at.group))
            else:
                got = send(message, at.moves_slow(e * at.group))
                got = jnp.concatenate([chunk_of(got, k ^ e) for k in range(at.chips)], axis=0)
            applied = applied + got.astype(jnp.float32)
        mapped = scale * applied - center_shift * now
        if first:
            updated = mapped / half_width
        else:
            updated = 2.0 / half_width * mapped - before
        before = now
        now = updated
        if not last:
            own = (scale * now).astype(jnp.bfloat16)
    back = [
        send(now[swap * part:(swap + 1) * part], turned(at.moves_home(swap)))
        for swap in range(2)
    ]
    result = jnp.stack([jnp.where(core == k, back[0], back[1]) for k in range(2)])
    return result.transpose(0, 2, 1, 3).reshape(start_vectors.shape)


def solution(mesh):
    in_specs = (
        P(None, ("row", "col")),
        P(("row", "col")),
        P("row", "col", None, None, None),
        P("row", "col", None, None),
        P("row", "col"),
    )
    out_specs = P(None, ("row", "col"))
    return jax.shard_map(
        per_device, mesh=mesh, in_specs=in_specs, out_specs=out_specs, check_vma=False
    )
```

```python
import functools

import jax
import jax.numpy as jnp
from jax import lax
from jax.experimental import pallas as pl
from jax.experimental.pallas import tpu as pltpu
from jax.sharding import PartitionSpec as P

STEPS = 3

center_shift = 0.5
half_width = 3.0

UNROLL_TRANSPOSED = 32
UNROLL_DIRECT = 64
PACK = 4
VMEM_LIMIT = 16 * 1024 * 1024
AXES = ("row", "col")
PAD = 8


class Layout:
    def __init__(self, rows, cols):
        self.rows, self.cols = rows, cols
        self.chips = cols // 2
        self.fast = 2
        self.slow = rows // 2
        self.group = self.slow // self.chips
        assert self.group * self.chips * self.fast == rows

    def device(self, slow, fast, chip, core):
        return (slow * self.fast + fast) * self.cols + chip * 2 + core

    def home(self, chunk):
        chip, k = chunk // self.rows, chunk % self.rows
        e, f, t = k % self.chips, (k // self.chips) % self.fast, k // (self.chips * self.fast)
        return (chip ^ e) * self.group + t, f, chip

    def moves_home(self, swap):
        pairs = []
        for chunk in range(self.rows * self.chips):
            row, chip = chunk // self.chips, chunk % self.chips
            for core in range(2):
                source = row * self.cols + chip * 2 + core
                pairs.append((source, self.device(*self.home(chunk), core ^ swap)))
        return pairs

    def moves_slow(self, d, side=0):
        return [
            (self.device(s, f, c, q), self.device(s ^ d, f ^ side, c, q))
            for s in range(self.slow) for f in range(self.fast)
            for c in range(self.chips) for q in range(2)
        ]

    def moves_fast(self):
        return self.moves_slow(0, 1)

    def moves_chip(self, d, swap=0):
        return [
            (self.device(s, f, c, q), self.device(s, f, c ^ d, q ^ swap))
            for s in range(self.slow) for f in range(self.fast)
            for c in range(self.chips) for q in range(2)
        ]

    def moves_core(self):
        return [(i, i ^ 1) for i in range(self.rows * self.cols)]


def turned(pairs):
    return [(b, a) for a, b in pairs]


def live_groups(meta_ref, cap, which, unroll):
    return jnp.maximum((meta_ref[8 * cap + which] + (unroll - 1)) // unroll, 1)


def product_kernel(transpose, cap, n_out, after, meta_in, vecs_in, *refs):
    slab_refs, refs = refs[:2], refs[2 + after:]
    outs, refs = refs[:n_out], refs[n_out:]
    meta_ref, vecs_ref, slabs, acc, slab_sem, in_sem = refs
    base = 0 if transpose else 4 * cap
    unroll = UNROLL_TRANSPOSED if transpose else UNROLL_DIRECT

    def slab_copy(which, g):
        span = pl.ds(g * unroll, unroll)
        to = pl.ds(which * cap + g * unroll, unroll)
        sem = slab_sem.at[which * (cap // unroll) + g]
        return pltpu.make_async_copy(slab_refs[which].at[span], slabs.at[to], sem)

    def start_slab(which, g, carry):
        slab_copy(which, g).start()
        return carry

    meta_copy = pltpu.make_async_copy(meta_in, meta_ref, in_sem.at[0])
    vecs_copy = pltpu.make_async_copy(vecs_in, vecs_ref, in_sem.at[1])
    meta_copy.start()
    slab_copy(0, 0).start()
    vecs_copy.start()
    slab_copy(1, 0).start()
    acc[...] = jnp.zeros_like(acc)
    meta_copy.wait()
    groups = [live_groups(meta_ref, cap, which, unroll) for which in range(2)]
    for which in range(2):
        lax.fori_loop(1, groups[which], functools.partial(start_slab, which), 0)
    vecs_copy.wait()
    vec_count, block_len = vecs_ref.shape[1:]
    zero = jnp.zeros((vec_count, block_len), jnp.bfloat16)

    def body(which, g, carry):
        slab_copy(which, g).wait()
        start = which * cap + g * unroll
        products = []
        for u in range(0, unroll, PACK):
            v = [vecs_ref[meta_ref[base + start + u + k]] for k in range(PACK)]
            m = [slabs[start + u + k] for k in range(PACK)]
            left = jnp.concatenate([
                jnp.concatenate([v[0], zero, v[2], zero], axis=0),
                jnp.concatenate([zero, v[1], zero, v[3]], axis=0),
            ], axis=1)
            if transpose:
                halves = [jnp.concatenate(m[:2], axis=0), jnp.concatenate(m[2:], axis=0)]
                right, dims = jnp.concatenate(halves, axis=1), (((1,), (0,)), ((), ()))
            else:
                halves = [jnp.concatenate(m[:2], axis=1), jnp.concatenate(m[2:], axis=1)]
                right, dims = jnp.concatenate(halves, axis=0), (((1,), (1,)), ((), ()))
            products.append(
                lax.dot_general(left, right, dims, preferred_element_type=jnp.float32)
            )
        for u in range(unroll):
            k = u % PACK
            rows = slice(k * vec_count, (k + 1) * vec_count)
            lanes = slice((k // 2) * block_len, (k // 2 + 1) * block_len)
            acc[meta_ref[base + 2 * cap + start + u]] += products[u // PACK][rows, lanes]
        return carry

    for which in range(2):
        lax.fori_loop(0, groups[which], functools.partial(body, which), 0)
    size = outs[0].shape[0]
    for k, out in enumerate(outs):
        out[...] = acc[k * size:(k + 1) * size].astype(out.dtype)


def products(meta, slabs, vecs, out_dtypes, out_blocks, transpose, after=()):
    cap, block_len, _ = slabs[0].shape
    vec_count = vecs.shape[1]
    n_out = len(out_dtypes)
    total_out = out_blocks * n_out
    anywhere = pl.BlockSpec(memory_space=pl.ANY)
    vmem = pl.BlockSpec(memory_space=pltpu.VMEM)
    out_shape = [
        jax.ShapeDtypeStruct((out_blocks, vec_count, block_len), dtype) for dtype in out_dtypes
    ]
    return pl.pallas_call(
        functools.partial(product_kernel, transpose, cap, n_out, len(after)),
        in_specs=[anywhere] * (4 + len(after)),
        out_specs=[vmem] * n_out,
        out_shape=out_shape,
        scratch_shapes=[
            pltpu.SMEM(meta.shape, jnp.int32),
            pltpu.VMEM(vecs.shape, jnp.bfloat16),
            pltpu.VMEM((2 * cap, block_len, block_len), jnp.bfloat16),
            pltpu.VMEM((total_out + 1, vec_count, block_len), jnp.float32),
            pltpu.SemaphoreType.DMA((2 * cap // min(UNROLL_TRANSPOSED, UNROLL_DIRECT),)),
            pltpu.SemaphoreType.DMA((2,)),
        ],
        compiler_params=pltpu.CompilerParams(vmem_limit_bytes=VMEM_LIMIT),
        cost_estimate=pl.CostEstimate(
            flops=4 * cap * vec_count * block_len * block_len,
            bytes_accessed=2 * vec_count * block_len * (vecs.shape[0] + total_out),
            transcendentals=0,
        ),
        name="transposed" if transpose else "direct",
    )(meta, vecs, *slabs, *after)


def per_device(start_vectors, scaling, block_values, block_places, block_counts):
    at = Layout(lax.axis_size("row"), lax.axis_size("col"))
    cap = block_values.shape[2]
    block_len = block_values.shape[-1]
    half = start_vectors.shape[0] // 2
    part = start_vectors.shape[1] // block_len
    per_chunk = 2 * part
    row_index = lax.axis_index("row").astype(jnp.int32)
    col_index = lax.axis_index("col").astype(jnp.int32)
    slow, fast = row_index // at.fast, row_index % at.fast
    chip, core = col_index // 2, col_index % 2
    root = slow // at.group
    is_root = chip == root
    def send(x, pairs):
        return lax.ppermute(x, AXES, pairs)

    slabs = block_values.reshape(cap, block_len, block_len)
    slots = jnp.concatenate([block_places.reshape(2 * cap), block_counts.reshape(1)])
    other_slabs = send(slabs, at.moves_core())

    halves = start_vectors.reshape(2, half, part, block_len).transpose(0, 2, 1, 3)
    scale_rows = jnp.broadcast_to(
        scaling.reshape(1, part, 1, block_len), (2, part, PAD, block_len)
    )
    halves = jnp.concatenate([halves, scale_rows], axis=2)
    packed = [
        jnp.where(core == swap, halves[0], halves[1]) for swap in range(2)
    ]
    pieces = [
        jnp.concatenate([
            packed[swap] if (d, swap) == (0, 0) else send(packed[swap], at.moves_chip(d, swap))
            for swap in range(2)
        ], axis=0)
        for d in range(at.chips)
    ]
    n_kept = at.chips * per_chunk

    def chunk_of(x, e):
        return x[e * per_chunk:(e + 1) * per_chunk]

    def pick(index, choices):
        x = choices[0]
        for d in range(1, len(choices)):
            x = jnp.where(index == d, choices[d], x)
        return x

    row_state = jnp.concatenate([pick(chip ^ e, pieces) for e in range(at.chips)], axis=0)

    other_slots = send(slots, at.moves_core())
    n_col = at.rows * per_chunk
    n_row = at.chips * per_chunk
    lists = []
    for which, held in enumerate((slots, other_slots)):
        row_block, col_block = held[:cap], held[cap:2 * cap]
        live = jnp.arange(cap, dtype=jnp.int32) < held[2 * cap]

        def inside(block):
            return ((block // part) ^ core) * part + block % part

        e = row_block // per_chunk
        row_at = e * per_chunk + inside(row_block % per_chunk)
        block = (core ^ which) * (n_col // 2) + col_block
        k = block // per_chunk
        e, f, t = k % at.chips, (k // at.chips) % at.fast, k // (at.chips * at.fast)
        d = slow ^ ((chip ^ e) * at.group + t)
        place = (d % at.group) * at.chips + d // at.group
        col_at = ((fast ^ f) * at.slow + place) * per_chunk + inside(block % per_chunk)
        lists.append((
            row_at, jnp.where(live, col_at, n_col), col_at, jnp.where(live, row_at, n_row)
        ))
    meta = jnp.concatenate(
        [jnp.concatenate([mine, theirs]) for mine, theirs in zip(*lists)]
        + [slots[2 * cap:], other_slots[2 * cap:], jnp.zeros(126, jnp.int32)]
    )

    row_state, meta, other_slabs = lax.optimization_barrier((row_state, meta, other_slabs))
    both = (slabs, other_slabs)

    def across(x):
        return [send(x, at.moves_slow(d * at.group)) for d in range(1, at.chips)]

    def kept_of(x, got):
        got = [
            jnp.concatenate([chunk_of(y, k ^ d) for k in range(at.chips)], axis=0)
            for d, y in enumerate(got, 1)
        ]
        return pick(chip ^ root, [x] + got)

    row_now, row_scale = row_state[:, :half], row_state[:, half:half + 1]
    row_tile = (row_scale * row_now).astype(jnp.bfloat16)
    tiles_across = across(row_tile)
    row_tile, row_state = lax.optimization_barrier((row_tile, row_state))
    row_now, row_scale = row_state[:, :half], row_state[:, half:half + 1]
    high = lax.optimization_barrier(row_scale.astype(jnp.bfloat16))
    low = lax.optimization_barrier(
        (row_scale - high.astype(jnp.float32)).astype(jnp.bfloat16)
    )

    def joined(high, low):
        return high.astype(jnp.float32) + low.astype(jnp.float32)

    row_rest = (
        row_now - row_tile.astype(jnp.float32) / joined(high, low)
    ).astype(jnp.bfloat16)
    row_rest = jnp.concatenate(
        [row_rest] + [jnp.broadcast_to(x, (n_kept, PAD, block_len)) for x in (high, low)],
        axis=1,
    )

    before = None
    for iterate in range(STEPS):
        first, last = iterate == 0, iterate == STEPS - 1
        if not first:
            row_tile = pick(
                chip ^ root,
                [own] + [send(own, at.moves_chip(d)) for d in range(1, at.chips)],
            )
        dtypes = (jnp.float32,) * at.group + (jnp.bfloat16,) * at.group
        if not first:
            near = [own] + [send(own, at.moves_slow(g)) for g in range(1, at.group)]
            far = [send(own, at.moves_slow(g, 1)) for g in range(at.group)]
        sums = products(meta, both, row_tile, dtypes, n_kept, True)
        near_sums, far_sums = list(sums[:at.group]), list(sums[at.group:])
        from_fast = [send(x, at.moves_fast()) for x in far_sums[::-1]][::-1]
        if first:
            tiles_across, far_sums = lax.optimization_barrier((tiles_across, far_sums))
            own = kept_of(row_tile, tiles_across)
            near = [own] + [send(own, at.moves_slow(g)) for g in range(1, at.group)]
            far = [send(own, at.moves_slow(g, 1)) for g in range(at.group)]
            row_rest, near = lax.optimization_barrier((row_rest, near))
            rests_across = across(row_rest)
        (row_sum,) = products(
            meta, both, jnp.concatenate(near + far, axis=0), (jnp.bfloat16,), n_row, False,
            after=far_sums,
        )
        if first:
            from_fast[-1], row_sum, rests_across = lax.optimization_barrier(
                (from_fast[-1], row_sum, rests_across)
            )
            scales = [
                joined(x[:, half:half + 1], x[:, half + PAD:half + PAD + 1])
                for x in rests_across
            ]
            scale = kept_of(row_scale, scales)
            now = kept_of(row_now, [
                tile.astype(jnp.float32) / factor + rest[:, :half].astype(jnp.float32)
                for tile, factor, rest in zip(tiles_across, scales, rests_across)
            ])
        from_row = [row_sum] + [
            send(row_sum, at.moves_chip(d)) for d in range(1, at.chips)
        ]
        sums = [x + y.astype(jnp.float32) for x, y in zip(near_sums, from_fast)]
        total = sums[0]
        for g in range(1, at.group):
            total = total + send(
                sums[g].astype(jnp.bfloat16), at.moves_slow(g)
            ).astype(jnp.float32)
        for x in from_row:
            total = total + jnp.where(is_root, x, jnp.zeros_like(x)).astype(jnp.float32)
        message = total.astype(jnp.bfloat16)
        if last:
            total, now, scale = chunk_of(total, 0), chunk_of(now, 0), chunk_of(scale, 0)
            before = chunk_of(before, 0)
        applied = total
        for e in range(1, at.chips):
            if last:
                got = send(chunk_of(message, e), at.moves_slow(e * at.group))
            else:
                got = send(message, at.moves_slow(e * at.group))
                got = jnp.concatenate([chunk_of(got, k ^ e) for k in range(at.chips)], axis=0)
            applied = applied + got.astype(jnp.float32)
        mapped = scale * applied - center_shift * now
        if first:
            updated = mapped / half_width
        else:
            updated = 2.0 / half_width * mapped - before
        before = now
        now = updated
        if not last:
            own = (scale * now).astype(jnp.bfloat16)
    back = [
        send(now[swap * part:(swap + 1) * part], turned(at.moves_home(swap)))
        for swap in range(2)
    ]
    result = jnp.stack([jnp.where(core == k, back[0], back[1]) for k in range(2)])
    return result.transpose(0, 2, 1, 3).reshape(start_vectors.shape)


def solution(mesh):
    in_specs = (
        P(None, ("row", "col")),
        P(("row", "col")),
        P("row", "col", None, None, None),
        P("row", "col", None, None),
        P("row", "col"),
    )
    out_specs = P(None, ("row", "col"))
    return jax.shard_map(
        per_device, mesh=mesh, in_specs=in_specs, out_specs=out_specs, check_vma=False
    )
```
